256 devices in a mesh: px: 32 (over y, z), py: 8 (over x, core).
Axes of the slice: x: 4, y: 4, z: 8, core: 2. Of those that a mesh axis runs over, the one named last changes fastest.
Arguments:
- solution: float32 [1, 8388608], P(None, ('px', 'py')), may hold values from -6 to 6
- residual: float32 [1, 8388608], P(None, ('px', 'py')), may hold values from -400 to 400
- direction: float32 [1, 8388608], P(None, ('px', 'py')), may hold values from -400 to 400
- offsets: float32 [3, 8388608], P(None, ('px', 'py')), may hold values from 0 to 1
- noise: float32 [8388608], P(('px', 'py')), may hold values from 0.3 to 3
- bin_cells: int32 [3, 65536], P(None, ('px', 'py')), may hold values from 1 to 253, as said below
- lengths: float32 [3], replicated, may hold values from 8 to 14
Outputs:
- new_solution: float32 [1, 8388608], P(None, ('px', 'py'))
- new_residual: float32 [1, 8388608], P(None, ('px', 'py'))
- new_direction: float32 [1, 8388608], P(None, ('px', 'py'))
The draws below stay inside these ranges and needn't reach their ends.
Inputs may be any that keep to these rules, and one draw needn't show every extreme that they name: `bin_cells`: bin b is held by the device at position b // 256 of px+py (px major); its cell lies in that device's block of grid rows and columns, and its whole 4 x 4 x 4 stencil lies inside the grid.
All inputs are finite; a program needn't handle non-finite values.
Results may differ from the reference program's by a relative error of at most 0.000086.
Values sent between devices are 32-bit elements; how exact they have to be, the bound alone decides.
No kernel may reach another device: no remote copies, remote signals or barrier semaphores. Data moves between devices by JAX's collectives and lax.ppermute only.
A program may use at most 128 MiB of HBM per device.

```python
import math
import jax
import jax.numpy as jnp
from jax import lax

GRID_X = 128
GRID_Y = 256
GRID_Z = 256
BIN = 128
PROBES = 1
BINS_DEV = 256
BINS = 65536
POINTS = 8388608
N_PX = 32
N_PY = 8


def draw_residual(key, part):
    key = jax.random.fold_in(key, 3)
    value_key, column_key = jax.random.split(key)
    placing = jnp.arange(POINTS).astype(jnp.float32) / (POINTS - 1)
    row_scale = jnp.power(10.0, placing)
    column_scale = jnp.power(10.0, jax.random.uniform(column_key, (PROBES, 1), jnp.float32))
    values = jnp.clip(jax.random.normal(value_key, (PROBES, POINTS), jnp.float32), -4.0, 4.0)
    return values * row_scale[None, :] * column_scale


def draw_direction(key, part):
    key = jax.random.fold_in(key, 5)
    value_key, column_key = jax.random.split(key)
    placing = jnp.arange(POINTS).astype(jnp.float32) / (POINTS - 1)
    row_scale = jnp.power(10.0, placing)
    column_scale = jnp.power(10.0, jax.random.uniform(column_key, (PROBES, 1), jnp.float32))
    values = jnp.clip(jax.random.normal(value_key, (PROBES, POINTS), jnp.float32), -4.0, 4.0)
    return values * row_scale[None, :] * column_scale


def draw_bin_cells(key, part):
    key = jax.random.fold_in(key, 7)
    subkeys = jax.random.split(key, 6)
    bin_owner = jnp.arange(BINS, dtype=jnp.int32) // BINS_DEV
    bin_slot = jnp.arange(BINS, dtype=jnp.int32) % BINS_DEV
    row_width = GRID_X // N_PX
    column_width = GRID_Y // N_PY
    row_start = bin_owner // N_PY * row_width
    column_start = bin_owner % N_PY * column_width
    row_cells = row_start + jax.random.randint(subkeys[0], (BINS,), 0, row_width)
    row_cells = jnp.where(bin_slot == 0, row_start + row_width - 1, row_cells)
    row_cells = jnp.clip(row_cells, 1, GRID_X - 3)
    column_cells = column_start + jax.random.randint(subkeys[1], (BINS,), 0, column_width)
    column_cells = jnp.where(bin_slot == 1, column_start + column_width - 1, column_cells)
    column_cells = jnp.clip(column_cells, 1, GRID_Y - 3)
    spread_depth = jax.random.randint(subkeys[2], (BINS,), 1, GRID_Z - 2)
    face_step = jax.random.randint(subkeys[3], (BINS,), 0, 3)
    face_side = jax.random.randint(subkeys[4], (BINS,), 0, 2)
    face_depth = jnp.where(face_side == 0, 1 + face_step, GRID_Z - 3 - face_step)
    at_face = jax.random.randint(subkeys[5], (BINS,), 0, 2) == 0
    depth_cells = jnp.where(at_face, face_depth, spread_depth)
    depth_cells = jnp.where(bin_slot == 2, GRID_Z - 3, depth_cells)
    depth_cells = jnp.where(bin_slot == 3, 1, depth_cells)
    return jnp.stack([row_cells, column_cells, depth_cells]).astype(jnp.int32)


def levels(own_key, dims, shards, smallest, high):
    gain = 1.0
    for dim, blocks in shards:
        steps = jax.random.uniform(jax.random.fold_in(jax.random.fold_in(own_key, 6), dim), (blocks,), jnp.float32, smallest / len(shards), high / len(shards))
        gain = gain * jnp.repeat(jnp.exp(steps), dims[dim] // blocks).reshape((-1,) + (1,) * (len(dims) - 1 - dim))
    return gain


def gaussian(rng, dims, deviation, limit, cuts=(), kind=jnp.bfloat16):
    level = levels(rng, dims, cuts, -0.22, 0.18) if cuts else 1.0
    entries = jax.random.normal(rng, dims, jnp.float32) * deviation * level
    return jnp.minimum(jnp.maximum(entries, -limit), limit).astype(kind)


def setup_inputs(seed: int = 0) -> dict:
    seeds = jax.random.split(jax.random.key(seed), 8)
    return {
        "solution": gaussian(seeds[0], (PROBES, POINTS), 1.0, 6.0, ((1, 256),), jnp.float32),
        "residual": draw_residual(jax.random.fold_in(seeds[7], 71), 0),
        "direction": draw_direction(jax.random.fold_in(seeds[7], 71), 0),
        "offsets": jnp.clip(1.0 * jax.random.uniform(seeds[3], (3, POINTS), jnp.float32) ** levels(seeds[3], (3, POINTS), ((1, 256),), -0.2, 0.2), 0.0, 1.0),
        "noise": jnp.clip(jnp.exp(math.log(3.0) - 2.3025851 * jax.random.uniform(seeds[4], (POINTS,), jnp.float32) ** levels(seeds[4], (POINTS,), ((0, 256),), -0.2, 0.2)), 0.3, 3.0),
        "bin_cells": draw_bin_cells(jax.random.fold_in(seeds[7], 71), 0),
        "lengths": jnp.clip(jnp.exp(jax.random.uniform(seeds[6], (3,), jnp.float32, math.log(8.0), math.log(14.0))), 8.0, 14.0),
    }


exact_precision = lax.Precision.HIGHEST


def cubic_weights(fraction):
    first_weight = ((-0.5 * fraction + 1.0) * fraction - 0.5) * fraction
    second_weight = (1.5 * fraction - 2.5) * fraction * fraction + 1.0
    third_weight = ((-1.5 * fraction + 2.0) * fraction + 0.5) * fraction
    fourth_weight = (0.5 * fraction - 0.5) * fraction * fraction
    return jnp.stack([first_weight, second_weight, third_weight, fourth_weight], axis=-1)


def stencil_weights(offsets_binned):
    along_rows = cubic_weights(offsets_binned[0])
    along_columns = cubic_weights(offsets_binned[1])
    along_depth = cubic_weights(offsets_binned[2])
    product = along_rows[:, :, :, None, None] * along_columns[:, :, None, :, None] * along_depth[:, :, None, None, :]
    return product.reshape(product.shape[0], product.shape[1], 64)


def stencil_steps():
    corner = jnp.arange(64, dtype=jnp.int32)
    return corner // 16, (corner // 4) % 4, corner % 4


def spectrum_block(lengths, first_freq, second_freq, third_freq, first_size, second_size, third_size):
    shaped_first = lengths[0] * jnp.sin(first_freq * (math.pi / first_size))
    shaped_second = lengths[1] * jnp.sin(second_freq * (math.pi / second_size))
    shaped_third = lengths[2] * jnp.sin(third_freq * (math.pi / third_size))
    denominator = 1.0 + (shaped_first * shaped_first)[:, None, None] + (shaped_second * shaped_second)[None, :, None] + (shaped_third * shaped_third)[None, None, :]
    return 2.0 * lengths[0] * lengths[1] * lengths[2] / (denominator * denominator)


def reference(solution, residual, direction, offsets, noise, bin_cells, lengths):
    weights = stencil_weights(offsets.reshape(3, BINS, BIN))
    step_rows, step_columns, step_depth = stencil_steps()
    row_cells = bin_cells[0][:, None] - 1 + step_rows
    column_cells = bin_cells[1][:, None] - 1 + step_columns
    depth_cells = bin_cells[2][:, None] - 1 + step_depth
    flat_index = (row_cells * GRID_Y + column_cells) * GRID_Z + depth_cells
    binned = direction.reshape(PROBES, BINS, BIN)
    patches = jnp.einsum("rnt,ntc->rnc", binned, weights, precision=exact_precision)
    gridded = jnp.zeros((PROBES, GRID_X * GRID_Y * GRID_Z), jnp.float32).at[:, flat_index].add(patches)
    depth_length = 2 * GRID_Z - 1
    first_freq = jnp.arange(2 * GRID_X).astype(jnp.float32)
    second_freq = jnp.arange(2 * GRID_Y).astype(jnp.float32)
    third_freq = jnp.arange(depth_length).astype(jnp.float32)
    spectrum = spectrum_block(lengths, first_freq, second_freq, third_freq, 2 * GRID_X, 2 * GRID_Y, depth_length)

    def covary(grid_values):
        transformed = jnp.fft.fftn(grid_values, s=(2 * GRID_X, 2 * GRID_Y, depth_length))
        returned = jnp.fft.ifftn(transformed * spectrum)
        return jnp.real(returned)[:GRID_X, :GRID_Y, :GRID_Z]

    covaried = lax.map(covary, gridded.reshape(PROBES, GRID_X, GRID_Y, GRID_Z))
    gathered = covaried.reshape(PROBES, GRID_X * GRID_Y * GRID_Z)[:, flat_index]
    interpolated = jnp.einsum("rnc,ntc->rnt", gathered, weights, precision=exact_precision).reshape(PROBES, POINTS)
    operator_image = interpolated + noise[None, :] * direction
    old_norm = jnp.sum(residual * residual, axis=1)
    curvature = jnp.sum(direction * operator_image, axis=1)
    step_size = old_norm / curvature
    new_solution = solution + step_size[:, None] * direction
    new_residual = residual - step_size[:, None] * operator_image
    new_norm = jnp.sum(new_residual * new_residual, axis=1)
    new_direction = new_residual + (new_norm / old_norm)[:, None] * direction
    return new_solution, new_residual, new_direction
```

```python
import math

import jax
import jax.numpy as jnp
import ml_dtypes
import numpy as np
from jax import lax
from jax.experimental import pallas as pl
from jax.experimental.pallas import tpu as pltpu
from jax.sharding import PartitionSpec as P

GRID_X, GRID_Y, GRID_Z = 128, 256, 256
BIN = 128
N_PX, N_PY = 32, 8
DEVICES = N_PX * N_PY
ROWS, COLUMNS = GRID_X // N_PX, GRID_Y // N_PY
SPAN_X, SPAN_Y = ROWS + 3, COLUMNS + 3
CELLS = 256
M_X, M_Y, M_Z = 2 * GRID_X, 2 * GRID_Y, 2 * GRID_Z - 1
BINS = 256
GROUP = 32
GROUPS = BINS // GROUP
PAIRS = GROUP * 16
BLOCK_X, BLOCK_Y = M_X // ROWS, M_Y // COLUMNS
CHUNKS = 3
PER_CHUNK = (BLOCK_X // 2 + 1) // CHUNKS
CHUNK = PER_CHUNK * BLOCK_Y

f32, bf16 = jnp.float32, jnp.bfloat16


def halves(table):
    table = np.asarray(table, np.float64)
    high = table.astype(np.float32).astype(ml_dtypes.bfloat16)
    low = (table - high.astype(np.float64)).astype(np.float32).astype(ml_dtypes.bfloat16)
    return high, low


def depth_tables():
    freq = np.arange(GRID_Z)[:, None]
    depth = np.arange(GRID_Z)[None, :]
    angle = 2 * np.pi * (freq * depth % M_Z) / M_Z
    forward = np.concatenate([np.cos(angle), -np.sin(angle)], 0)
    twice = np.where(freq == 0, 1.0, 2.0) / M_Z
    inverse = np.concatenate([np.cos(angle) * twice, -np.sin(angle) * twice], 0).T
    return halves(forward) + halves(inverse)


def plane_tables():
    kx = np.arange(BLOCK_X // 2 + 1)
    ky = np.arange(BLOCK_Y)
    source = np.arange(DEVICES)
    px, py = source // N_PY, source % N_PY
    phase = (kx[:, None, None] * px / BLOCK_X + ky[None, :, None] * py / BLOCK_Y) * 2 * np.pi
    phase = phase.reshape(CHUNKS, CHUNK, DEVICES)
    blocks = np.concatenate([np.cos(phase), np.sin(phase)], 1)
    lane = np.arange(CELLS)
    live = lane < SPAN_X * SPAN_Y
    a, e = lane // SPAN_Y - 1, lane % SPAN_Y - 1
    twist = 2 * np.pi * (kx[:, None, None] * a / M_X + ky[None, :, None] * e / M_Y)
    twist = twist.reshape(-1, CELLS)
    out = np.arange(ROWS * COLUMNS)
    high_x, high_y = out // COLUMNS, out % COLUMNS
    inner = 2 * np.pi * (a[:, None] * high_x[None, :] / ROWS + e[:, None] * high_y[None, :] / COLUMNS)
    c, s = np.cos(inner) * live[:, None], np.sin(inner) * live[:, None]
    inner_forward = np.block([[c, -s], [s, c]])
    inner_inverse = np.block([[c.T, s.T], [-s.T, c.T]])
    full_x = BLOCK_X * high_x[None, :]
    full_y = BLOCK_Y * high_y[None, :]
    sine_x = [np.sin(np.pi * (sign * kx[:, None] + full_x) / M_X) ** 2 for sign in (1, -1)]
    sine_y = [np.sin(np.pi * (sign * ky[:, None] + full_y) / M_Y) ** 2 for sign in (1, -1)]
    scale = 1.0 / (M_X * M_Y)
    weight = np.where((kx == 0) | (kx == BLOCK_X // 2), 0.0, scale)[:, None] * np.ones((1, ROWS * COLUMNS))
    return dict(
        blocks=halves(blocks),
        blocks_back=halves(blocks.transpose(0, 2, 1)),
        inner=halves(inner_forward),
        inner_back=halves(inner_inverse),
        twist=(np.cos(twist).astype(np.float32), (-np.sin(twist)).astype(np.float32)),
        sine_x=[t.astype(np.float32) for t in sine_x],
        sine_y=[t.astype(np.float32) for t in sine_y],
        weight=weight.astype(np.float32),
    )


def split(values):
    high = values.astype(bf16)
    return high, (values - high.astype(f32)).astype(bf16)


def dot(a, b):
    return jnp.dot(a, b, preferred_element_type=f32)


def dot_nt(a, b):
    return lax.dot_general(a, b, (((1,), (1,)), ((), ())), preferred_element_type=f32)


def dot3(a, b, mul=dot):
    return mul(a[0], b[0]) + mul(a[0], b[1]) + mul(a[1], b[0])


def cubic_weights(t):
    return (
        ((-0.5 * t + 1.0) * t - 0.5) * t,
        (1.5 * t - 2.5) * t * t + 1.0,
        ((-1.5 * t + 2.0) * t + 0.5) * t,
        (0.5 * t - 0.5) * t * t,
    )


def one_hot(hit):
    return jnp.where(hit, 1.0, 0.0).astype(bf16)


def iota(shape, dim):
    return lax.broadcasted_iota(jnp.int32, shape, dim)


def stencil_cells(base):
    shift = iota((GROUP, CELLS), 1) - base
    return jnp.concatenate([one_hot(shift == a * SPAN_Y + e) for a in range(4) for e in range(4)], 0)


def same_bin(shape):
    return ((iota(shape, 0) ^ iota(shape, 1)) & (GROUP - 1)) == 0


def group_slice(g, size=GROUP):
    return pl.ds(pl.multiple_of(g * size, size), size)


def spread_kernel(direction, offsets, places, depth_row, forward_hi, forward_lo, out, q_hi, q_lo):
    def group(g, _):
        bins = group_slice(g)
        wx = cubic_weights(offsets[0, bins, :])
        wy = cubic_weights(offsets[1, bins, :])
        wz = cubic_weights(offsets[2, bins, :])
        d = direction[bins, :]
        wx = [w * d for w in wx]
        columns = split(jnp.concatenate([x * y for x in wx for y in wy], 0))
        depths = split(jnp.concatenate(wz, 0))
        patches = dot3(depths, columns, dot_nt)
        patches = split(jnp.where(same_bin((4 * GROUP, PAIRS)), patches, 0.0))
        cells = stencil_cells(places[bins, 0:1])
        placed = split(dot(patches[0], cells) + dot(patches[1], cells))
        rows = group_slice(g, 4 * GROUP)
        q_hi[rows, :] = placed[0]
        q_lo[rows, :] = placed[1]
        return 0

    lax.fori_loop(0, GROUPS, group, 0)
    at_depth = one_hot(iota((GRID_Z, 4 * BINS), 0) == depth_row[...])
    gridded = split(dot(at_depth, q_hi[...]) + dot(at_depth, q_lo[...]))
    transformed = dot3((forward_hi[...], forward_lo[...]), gridded)
    for part in range(2):
        for half in range(2):
            out[pl.ds(2 * part + half, GRID_Z, stride=4), :] = transformed[
                part * GRID_Z : (part + 1) * GRID_Z, half * 128 : (half + 1) * 128
            ]


def plane_kernel(
    scalars, received, blocks_hi, blocks_lo, back_hi, back_lo, inner_hi, inner_lo, inback_hi, inback_lo,
    twist_re, twist_im, sx_a, sx_b, sy_a, sy_b, weight_b,
    out, r_hi, r_lo, wide, m_hi, m_lo, narrow, g_hi, g_lo, total,
):
    for j in range(4):
        hi, lo = split(received[pl.ds(j, DEVICES, stride=4), :])
        r_hi[:, 128 * j : 128 * (j + 1)] = hi
        r_lo[:, 128 * j : 128 * (j + 1)] = lo
    total[...] = jnp.zeros_like(total)
    scale_x, scale_y, rest, factor = scalars[0], scalars[1], scalars[2], scalars[3]
    factor_a = factor * (1.0 / (M_X * M_Y))

    def chunk(c, _):
        wide[...] = dot3((blocks_hi[c], blocks_lo[c]), (r_hi[...], r_lo[...]))

        def twisted(j, _):
            top = group_slice(j, BLOCK_Y)
            bottom = pl.ds(pl.multiple_of(CHUNK + j * BLOCK_Y, BLOCK_Y), BLOCK_Y)
            table = pl.ds(pl.multiple_of(c * CHUNK + j * BLOCK_Y, BLOCK_Y), BLOCK_Y)
            tr, ti = twist_re[table, :], twist_im[table, :]
            cre, cim = wide[top, :CELLS], wide[top, CELLS:]
            sre, sim = wide[bottom, :CELLS], wide[bottom, CELLS:]
            ur, ui, vr, vi = cre + sim, cim - sre, cre - sim, cim + sre
            for rows, re, im in (
                (top, ur * tr - ui * ti, ur * ti + ui * tr),
                (bottom, vr * tr + vi * ti, vi * tr - vr * ti),
            ):
                m_hi[rows, :CELLS], m_lo[rows, :CELLS] = split(re)
                m_hi[rows, CELLS:], m_lo[rows, CELLS:] = split(im)
            return 0

        lax.fori_loop(0, PER_CHUNK, twisted, 0, unroll=True)
        narrow[...] = dot3((m_hi[...], m_lo[...]), (inner_hi[...], inner_lo[...]))

        def filtered(j, _):
            top = group_slice(j, BLOCK_Y)
            bottom = pl.ds(pl.multiple_of(CHUNK + j * BLOCK_Y, BLOCK_Y), BLOCK_Y)
            freq = pl.ds(c * PER_CHUNK + j, 1)
            for rows, sx, sy, weight in (
                (top, sx_a, sy_a, factor_a),
                (bottom, sx_b, sy_b, factor * weight_b[freq, :]),
            ):
                denominator = (rest + scale_x * sx[freq, :]) + scale_y * sy[...]
                spectrum = weight / (denominator * denominator)
                for part in range(2):
                    lanes = slice(128 * part, 128 * (part + 1))
                    g_hi[rows, lanes], g_lo[rows, lanes] = split(narrow[rows, lanes] * spectrum)
            return 0

        lax.fori_loop(0, PER_CHUNK, filtered, 0, unroll=True)
        wide[...] = dot3((g_hi[...], g_lo[...]), (inback_hi[...], inback_lo[...]))

        def untwisted(j, _):
            top = group_slice(j, BLOCK_Y)
            bottom = pl.ds(pl.multiple_of(CHUNK + j * BLOCK_Y, BLOCK_Y), BLOCK_Y)
            table = pl.ds(pl.multiple_of(c * CHUNK + j * BLOCK_Y, BLOCK_Y), BLOCK_Y)
            tr, ti = twist_re[table, :], twist_im[table, :]
            zr, zi = wide[top, :CELLS], wide[top, CELLS:]
            yr, yi = wide[bottom, :CELLS], wide[bottom, CELLS:]
            ar, ai = zr * tr + zi * ti, zi * tr - zr * ti
            br, bi = yr * tr - yi * ti, yr * ti + yi * tr
            m_hi[top, :CELLS], m_lo[top, :CELLS] = split(ar + br)
            m_hi[top, CELLS:], m_lo[top, CELLS:] = split(ai + bi)
            m_hi[bottom, :CELLS], m_lo[bottom, :CELLS] = split(bi - ai)
            m_hi[bottom, CELLS:], m_lo[bottom, CELLS:] = split(ar - br)
            return 0

        lax.fori_loop(0, PER_CHUNK, untwisted, 0, unroll=True)
        total[...] += dot3((back_hi[c], back_lo[c]), (m_hi[...], m_lo[...]))
        return 0

    lax.fori_loop(0, CHUNKS, chunk, 0)
    for j in range(4):
        out[pl.ds(j, DEVICES, stride=4), :] = total[:, 128 * j : 128 * (j + 1)]


def gather_kernel(
    received, direction, residual, noise, offsets, places, inverse_hi, inverse_lo,
    image, sums, v_hi, v_lo, e_hi, e_lo,
):
    for part in range(2):
        for half in range(2):
            rows = slice(part * GRID_Z, (part + 1) * GRID_Z)
            lanes = slice(half * 128, (half + 1) * 128)
            v_hi[rows, lanes], v_lo[rows, lanes] = split(received[pl.ds(2 * part + half, GRID_Z, stride=4), :])
    grid_hi, grid_lo = split(dot3((inverse_hi[...], inverse_lo[...]), (v_hi[...], v_lo[...])))
    e_hi[...] = grid_hi
    e_lo[...] = grid_lo

    def group(g, carry):
        bins = group_slice(g)
        shift = iota((GROUP, GRID_Z), 1) - places[bins, 1:2]
        at_depth = jnp.concatenate([one_hot(shift == f - 1) for f in range(4)], 0)
        lines_hi = dot(at_depth, e_hi[...]).astype(bf16)
        lines_lo = dot(at_depth, e_lo[...]).astype(bf16)
        cells = stencil_cells(places[bins, 0:1])
        keep = same_bin((PAIRS, 4 * GROUP))
        read_hi = jnp.where(keep, dot_nt(cells, lines_hi), 0.0).astype(bf16)
        read_lo = jnp.where(keep, dot_nt(cells, lines_lo), 0.0).astype(bf16)
        depths = split(jnp.concatenate(cubic_weights(offsets[2, bins, :]), 0))
        along = dot3((read_hi, read_lo), depths)
        wx = cubic_weights(offsets[0, bins, :])
        wy = cubic_weights(offsets[1, bins, :])
        value = 0.0
        for a in range(4):
            row = 0.0
            for e in range(4):
                start = (4 * a + e) * GROUP
                row = row + wy[e] * along[start : start + GROUP]
            value = value + wx[a] * row
        d, r = direction[bins, :], residual[bins, :]
        value = value + noise[bins, :] * d
        image[bins, :] = value
        return tuple(
            total + (x * y).reshape(GROUP // 8, 8, BIN).sum(0)
            for total, (x, y) in zip(carry, ((r, r), (d, value), (r, value), (value, value)))
        )

    zero = jnp.zeros((8, BIN), f32)
    totals = lax.fori_loop(0, GROUPS, group, (zero,) * 4)
    sums[...] = jnp.concatenate([jnp.broadcast_to(jnp.sum(t, keepdims=True), (1, BIN)) for t in totals], 0)


VMEM = pl.BlockSpec(memory_space=pltpu.VMEM)
SMEM = pl.BlockSpec(memory_space=pltpu.SMEM)


def params():
    return pltpu.CompilerParams(vmem_limit_bytes=40 * 1024 * 1024)


def on_device(solution, residual, direction, offsets, noise, bin_cells, lengths):
    row_index, column_index = lax.axis_index("px"), lax.axis_index("py")
    depth_tabs = depth_tables()
    plane = plane_tables()
    d = direction.reshape(BINS, BIN)
    r = residual.reshape(BINS, BIN)
    offsets = offsets.reshape(3, BINS, BIN)
    base = (bin_cells[0] - row_index * ROWS) * SPAN_Y + (bin_cells[1] - column_index * COLUMNS)
    places = jnp.stack([base, bin_cells[2]], 1)
    depth_row = (
        bin_cells[2].reshape(GROUPS, 1, GROUP) + jnp.arange(-1, 3, dtype=jnp.int32)[None, :, None]
    ).reshape(1, 4 * BINS)

    blocks = pl.pallas_call(
        spread_kernel,
        out_shape=jax.ShapeDtypeStruct((4 * DEVICES, 128), f32),
        in_specs=[VMEM] * 6,
        out_specs=VMEM,
        scratch_shapes=[pltpu.VMEM((4 * BINS, CELLS), bf16)] * 2,
        compiler_params=params(),
        name="spread",
    )(d, offsets, places, depth_row, *depth_tabs[:2])
    received = lax.all_to_all(blocks.reshape(DEVICES, 4, 128), ("px", "py"), 0, 0, tiled=True)

    freq = (row_index * N_PY + column_index).astype(f32)
    depth_part = lengths[2] * jnp.sin(freq * (math.pi / M_Z))
    scalars = jnp.stack(
        [
            lengths[0] * lengths[0],
            lengths[1] * lengths[1],
            1.0 + depth_part * depth_part,
            2.0 * lengths[0] * lengths[1] * lengths[2],
        ]
    )
    tables = (
        *plane["blocks"], *plane["blocks_back"], *plane["inner"], *plane["inner_back"], *plane["twist"],
        *plane["sine_x"], *plane["sine_y"], plane["weight"],
    )
    filtered = pl.pallas_call(
        plane_kernel,
        out_shape=jax.ShapeDtypeStruct((4 * DEVICES, 128), f32),
        in_specs=[SMEM] + [VMEM] * (1 + len(tables)),
        out_specs=VMEM,
        scratch_shapes=[
            pltpu.VMEM((DEVICES, 512), bf16),
            pltpu.VMEM((DEVICES, 512), bf16),
            pltpu.VMEM((2 * CHUNK, 512), f32),
            pltpu.VMEM((2 * CHUNK, 512), bf16),
            pltpu.VMEM((2 * CHUNK, 512), bf16),
            pltpu.VMEM((2 * CHUNK, 256), f32),
            pltpu.VMEM((2 * CHUNK, 256), bf16),
            pltpu.VMEM((2 * CHUNK, 256), bf16),
            pltpu.VMEM((DEVICES, 512), f32),
        ],
        compiler_params=params(),
        name="plane",
    )(scalars, received.reshape(4 * DEVICES, 128), *tables)
    returned = lax.all_to_all(filtered.reshape(DEVICES, 4, 128), ("px", "py"), 0, 0, tiled=True)

    image, sums = pl.pallas_call(
        gather_kernel,
        out_shape=(jax.ShapeDtypeStruct((BINS, BIN), f32), jax.ShapeDtypeStruct((4, 128), f32)),
        in_specs=[VMEM] * 8,
        out_specs=(VMEM, VMEM),
        scratch_shapes=[pltpu.VMEM((2 * GRID_Z, CELLS), bf16)] * 2 + [pltpu.VMEM((GRID_Z, CELLS), bf16)] * 2,
        compiler_params=params(),
        name="interpolate",
    )(returned.reshape(4 * DEVICES, 128), d, r, noise.reshape(BINS, BIN), offsets, places, *depth_tabs[2:])

    everywhere = lax.all_to_all(
        jnp.broadcast_to(sums[:, 0][None, :], (DEVICES, 4)), ("px", "py"), 0, 0, tiled=True
    )
    old_norm, curvature, cross, square = jnp.sum(everywhere, axis=0)
    step = old_norm / curvature
    new_norm = old_norm - 2.0 * step * cross + step * step * square
    image = image.reshape(1, -1)
    new_residual = residual - step * image
    new_solution = solution + step * direction
    new_direction = new_residual + (new_norm / old_norm) * direction
    return new_solution, new_residual, new_direction


def solution(mesh):
    points = P(None, ("px", "py"))
    return jax.shard_map(
        on_device,
        mesh=mesh,
        in_specs=(points, points, points, points, P(("px", "py")), points, P()),
        out_specs=(points, points, points),
        check_vma=False,
    )
```

```python
import jax
import jax.numpy as jnp
import ml_dtypes
import numpy as np
from jax import lax
from jax.experimental import pallas as pl
from jax.experimental.pallas import tpu as pltpu
from jax.sharding import PartitionSpec as P

GRID_X, GRID_Y, GRID_Z = 128, 256, 256
BIN = 128
N_PX, N_PY = 32, 8
DEVICES = N_PX * N_PY
ROWS, COLUMNS = GRID_X // N_PX, GRID_Y // N_PY
SPAN_X, SPAN_Y = ROWS + 3, COLUMNS + 3
CELLS = 256
M_X, M_Y, M_Z = 2 * GRID_X, 2 * GRID_Y, 2 * GRID_Z - 1
BINS = 256
GROUP = 32
GROUPS = BINS // GROUP
PAIRS = GROUP * 16
BLOCK_X, BLOCK_Y = M_X // ROWS, M_Y // COLUMNS
CHUNKS = 3
PER_CHUNK = (BLOCK_X // 2 + 1) // CHUNKS
CHUNK = PER_CHUNK * BLOCK_Y

f32, bf16 = jnp.float32, jnp.bfloat16


def halves(table):
    table = np.asarray(table, np.float64)
    high = table.astype(np.float32).astype(ml_dtypes.bfloat16)
    low = (table - high.astype(np.float64)).astype(np.float32).astype(ml_dtypes.bfloat16)
    return high, low


def depth_tables():
    freq = np.arange(GRID_Z)[:, None]
    depth = np.arange(GRID_Z)[None, :]
    angle = 2 * np.pi * (freq * depth % M_Z) / M_Z
    forward = np.concatenate([np.cos(angle), -np.sin(angle)], 0)
    twice = np.where(freq == 0, 1.0, 2.0) / M_Z
    inverse = np.concatenate([np.cos(angle) * twice, -np.sin(angle) * twice], 0).T
    return halves(forward) + halves(inverse)


def plane_tables():
    kx = np.arange(BLOCK_X // 2 + 1)
    ky = np.arange(BLOCK_Y)
    source = np.arange(DEVICES)
    px, py = source // N_PY, source % N_PY
    phase = (kx[:, None, None] * px / BLOCK_X + ky[None, :, None] * py / BLOCK_Y) * 2 * np.pi
    phase = phase.reshape(CHUNKS, CHUNK, DEVICES)
    blocks = np.concatenate([np.cos(phase), np.sin(phase)], 1)
    lane = np.arange(CELLS)
    live = lane < SPAN_X * SPAN_Y
    a, e = lane // SPAN_Y - 1, lane % SPAN_Y - 1
    twist = 2 * np.pi * (kx[:, None, None] * a / M_X + ky[None, :, None] * e / M_Y)
    twist = twist.reshape(-1, CELLS)
    out = np.arange(ROWS * COLUMNS)
    high_x, high_y = out // COLUMNS, out % COLUMNS
    inner = 2 * np.pi * (a[:, None] * high_x[None, :] / ROWS + e[:, None] * high_y[None, :] / COLUMNS)
    c, s = np.cos(inner) * live[:, None], np.sin(inner) * live[:, None]
    inner_forward = np.block([[c, -s], [s, c]])
    inner_inverse = np.block([[c.T, s.T], [-s.T, c.T]])
    full_x = BLOCK_X * high_x[None, :]
    full_y = BLOCK_Y * high_y[None, :]
    sine_x = [np.sin(np.pi * (sign * kx[:, None] + full_x) / M_X) ** 2 for sign in (1, -1)]
    sine_y = [np.sin(np.pi * (sign * ky[:, None] + full_y) / M_Y) ** 2 for sign in (1, -1)]
    scale = 1.0 / (M_X * M_Y)
    weight = np.where((kx == 0) | (kx == BLOCK_X // 2), 0.0, scale)[:, None] * np.ones((1, ROWS * COLUMNS))
    return dict(
        blocks=halves(blocks),
        blocks_back=halves(blocks.transpose(0, 2, 1)),
        inner=halves(inner_forward),
        inner_back=halves(inner_inverse),
        twist=(np.cos(twist).astype(np.float32), (-np.sin(twist)).astype(np.float32)),
        sine_x=[t.astype(np.float32) for t in sine_x],
        sine_y=[t.astype(np.float32) for t in sine_y],
        weight=weight.astype(np.float32),
        depth_sine=(np.sin(np.pi * np.arange(GRID_Z) / M_Z) ** 2).astype(np.float32),
    )


def split(values):
    high = values.astype(bf16)
    return high, (values - high.astype(f32)).astype(bf16)


def dot(a, b):
    return jnp.dot(a, b, preferred_element_type=f32)


def dot_nt(a, b):
    return lax.dot_general(a, b, (((1,), (1,)), ((), ())), preferred_element_type=f32)


def dot3(a, b, mul=dot):
    return mul(a[0], b[0]) + mul(a[0], b[1]) + mul(a[1], b[0])


def cubic_weights(t):
    return (
        ((-0.5 * t + 1.0) * t - 0.5) * t,
        (1.5 * t - 2.5) * t * t + 1.0,
        ((-1.5 * t + 2.0) * t + 0.5) * t,
        (0.5 * t - 0.5) * t * t,
    )


def one_hot(hit):
    return jnp.where(hit, 1.0, 0.0).astype(bf16)


def iota(shape, dim):
    return lax.broadcasted_iota(jnp.int32, shape, dim)


def stencil_cells(base):
    shift = iota((GROUP, CELLS), 1) - base
    return jnp.concatenate([one_hot(shift == a * SPAN_Y + e) for a in range(4) for e in range(4)], 0)


def same_bin(shape):
    return ((iota(shape, 0) ^ iota(shape, 1)) & (GROUP - 1)) == 0


def group_slice(g, size=GROUP):
    return pl.ds(pl.multiple_of(g * size, size), size)


def block_base(cells):
    first_row, first_column = lax.axis_index("px") * ROWS, lax.axis_index("py") * COLUMNS
    return (cells[:, 0:1] - first_row) * SPAN_Y + (cells[:, 1:2] - first_column)


def spread_kernel(direction, offsets, cells_down, cells_across, forward_hi, forward_lo, out, q_hi, q_lo):
    def group(g, _):
        bins = group_slice(g)
        wx = cubic_weights(offsets[0, bins, :])
        wy = cubic_weights(offsets[1, bins, :])
        wz = cubic_weights(offsets[2, bins, :])
        d = direction[bins, :]
        wx = [w * d for w in wx]
        columns = split(jnp.concatenate([x * y for x in wx for y in wy], 0))
        depths = split(jnp.concatenate(wz, 0))
        patches = dot3(depths, columns, dot_nt)
        patches = split(jnp.where(same_bin((4 * GROUP, PAIRS)), patches, 0.0))
        cells = stencil_cells(block_base(cells_down[bins, :]))
        placed = split(dot(patches[0], cells) + dot(patches[1], cells))
        for f in range(4):
            rows = pl.ds(pl.multiple_of(f * BINS + g * GROUP, GROUP), GROUP)
            q_hi[rows, :] = placed[0][f * GROUP : (f + 1) * GROUP]
            q_lo[rows, :] = placed[1][f * GROUP : (f + 1) * GROUP]
        return 0

    lax.fori_loop(0, GROUPS, group, 0)
    shift = iota((GRID_Z, BINS), 0) - cells_across[2:3, :]
    at_depth = jnp.concatenate([one_hot(shift == f - 1) for f in range(4)], 1)
    gridded = split(dot(at_depth, q_hi[...]) + dot(at_depth, q_lo[...]))
    transformed = dot3((forward_hi[...], forward_lo[...]), gridded)
    for part in range(2):
        for half in range(2):
            out[pl.ds(2 * part + half, GRID_Z, stride=4), :] = transformed[
                part * GRID_Z : (part + 1) * GRID_Z, half * 128 : (half + 1) * 128
            ]


def plane_kernel(
    lengths, depth_sine, received, blocks_hi, blocks_lo, back_hi, back_lo, inner_hi, inner_lo, inback_hi, inback_lo,
    twist_re, twist_im, sx_a, sx_b, sy_a, sy_b, weight_b,
    out, r_hi, r_lo, wide, m_hi, m_lo, narrow, g_hi, g_lo, total,
):
    for j in range(4):
        hi, lo = split(received[pl.ds(j, DEVICES, stride=4), :])
        r_hi[:, 128 * j : 128 * (j + 1)] = hi
        r_lo[:, 128 * j : 128 * (j + 1)] = lo
    total[...] = jnp.zeros_like(total)
    scale_x, scale_y = lengths[0] * lengths[0], lengths[1] * lengths[1]
    rest = 1.0 + lengths[2] * lengths[2] * depth_sine[lax.axis_index("px") * N_PY + lax.axis_index("py")]
    factor = 2.0 * lengths[0] * lengths[1] * lengths[2]
    factor_a = factor * (1.0 / (M_X * M_Y))

    def chunk(c, _):
        wide[...] = dot3((blocks_hi[c], blocks_lo[c]), (r_hi[...], r_lo[...]))

        def twisted(j, _):
            top = group_slice(j, BLOCK_Y)
            bottom = pl.ds(pl.multiple_of(CHUNK + j * BLOCK_Y, BLOCK_Y), BLOCK_Y)
            table = pl.ds(pl.multiple_of(c * CHUNK + j * BLOCK_Y, BLOCK_Y), BLOCK_Y)
            tr, ti = twist_re[table, :], twist_im[table, :]
            cre, cim = wide[top, :CELLS], wide[top, CELLS:]
            sre, sim = wide[bottom, :CELLS], wide[bottom, CELLS:]
            ur, ui, vr, vi = cre + sim, cim - sre, cre - sim, cim + sre
            for rows, re, im in (
                (top, ur * tr - ui * ti, ur * ti + ui * tr),
                (bottom, vr * tr + vi * ti, vi * tr - vr * ti),
            ):
                m_hi[rows, :CELLS], m_lo[rows, :CELLS] = split(re)
                m_hi[rows, CELLS:], m_lo[rows, CELLS:] = split(im)
            return 0

        lax.fori_loop(0, PER_CHUNK, twisted, 0, unroll=True)
        narrow[...] = dot3((m_hi[...], m_lo[...]), (inner_hi[...], inner_lo[...]))

        def filtered(j, _):
            top = group_slice(j, BLOCK_Y)
            bottom = pl.ds(pl.multiple_of(CHUNK + j * BLOCK_Y, BLOCK_Y), BLOCK_Y)
            freq = pl.ds(c * PER_CHUNK + j, 1)
            for rows, sx, sy, weight in (
                (top, sx_a, sy_a, factor_a),
                (bottom, sx_b, sy_b, factor * weight_b[freq, :]),
            ):
                denominator = (rest + scale_x * sx[freq, :]) + scale_y * sy[...]
                spectrum = weight / (denominator * denominator)
                for part in range(2):
                    lanes = slice(128 * part, 128 * (part + 1))
                    g_hi[rows, lanes], g_lo[rows, lanes] = split(narrow[rows, lanes] * spectrum)
            return 0

        lax.fori_loop(0, PER_CHUNK, filtered, 0, unroll=True)
        wide[...] = dot3((g_hi[...], g_lo[...]), (inback_hi[...], inback_lo[...]))

        def untwisted(j, _):
            top = group_slice(j, BLOCK_Y)
            bottom = pl.ds(pl.multiple_of(CHUNK + j * BLOCK_Y, BLOCK_Y), BLOCK_Y)
            table = pl.ds(pl.multiple_of(c * CHUNK + j * BLOCK_Y, BLOCK_Y), BLOCK_Y)
            tr, ti = twist_re[table, :], twist_im[table, :]
            zr, zi = wide[top, :CELLS], wide[top, CELLS:]
            yr, yi = wide[bottom, :CELLS], wide[bottom, CELLS:]
            ar, ai = zr * tr + zi * ti, zi * tr - zr * ti
            br, bi = yr * tr - yi * ti, yr * ti + yi * tr
            m_hi[top, :CELLS], m_lo[top, :CELLS] = split(ar + br)
            m_hi[top, CELLS:], m_lo[top, CELLS:] = split(ai + bi)
            m_hi[bottom, :CELLS], m_lo[bottom, :CELLS] = split(bi - ai)
            m_hi[bottom, CELLS:], m_lo[bottom, CELLS:] = split(ar - br)
            return 0

        lax.fori_loop(0, PER_CHUNK, untwisted, 0, unroll=True)
        total[...] += dot3((back_hi[c], back_lo[c]), (m_hi[...], m_lo[...]))
        return 0

    lax.fori_loop(0, CHUNKS, chunk, 0)
    for j in range(4):
        out[pl.ds(j, DEVICES, stride=4), :] = total[:, 128 * j : 128 * (j + 1)]


def gather_kernel(
    received, direction, residual, noise, offsets, cells_down, inverse_hi, inverse_lo,
    image, sums, v_hi, v_lo, e_hi, e_lo,
):
    for part in range(2):
        for half in range(2):
            rows = slice(part * GRID_Z, (part + 1) * GRID_Z)
            lanes = slice(half * 128, (half + 1) * 128)
            v_hi[rows, lanes], v_lo[rows, lanes] = split(received[pl.ds(2 * part + half, GRID_Z, stride=4), :])
    grid_hi, grid_lo = split(dot3((inverse_hi[...], inverse_lo[...]), (v_hi[...], v_lo[...])))
    e_hi[...] = grid_hi
    e_lo[...] = grid_lo

    def group(g, carry):
        bins = group_slice(g)
        shift = iota((GROUP, GRID_Z), 1) - cells_down[bins, 2:3]
        at_depth = jnp.concatenate([one_hot(shift == f - 1) for f in range(4)], 0)
        lines_hi = dot(at_depth, e_hi[...]).astype(bf16)
        lines_lo = dot(at_depth, e_lo[...]).astype(bf16)
        cells = stencil_cells(block_base(cells_down[bins, :]))
        keep = same_bin((PAIRS, 4 * GROUP))
        read_hi = jnp.where(keep, dot_nt(cells, lines_hi), 0.0).astype(bf16)
        read_lo = jnp.where(keep, dot_nt(cells, lines_lo), 0.0).astype(bf16)
        depths = split(jnp.concatenate(cubic_weights(offsets[2, bins, :]), 0))
        along = dot3((read_hi, read_lo), depths)
        wx = cubic_weights(offsets[0, bins, :])
        wy = cubic_weights(offsets[1, bins, :])
        value = 0.0
        for a in range(4):
            row = 0.0
            for e in range(4):
                start = (4 * a + e) * GROUP
                row = row + wy[e] * along[start : start + GROUP]
            value = value + wx[a] * row
        d, r = direction[bins, :], residual[bins, :]
        value = value + noise[bins, :] * d
        image[bins, :] = value
        return tuple(
            total + (x * y).reshape(GROUP // 8, 8, BIN).sum(0)
            for total, (x, y) in zip(carry, ((r, r), (d, value), (r, value), (value, value)))
        )

    zero = jnp.zeros((8, BIN), f32)
    totals = lax.fori_loop(0, GROUPS, group, (zero,) * 4)
    lane = iota((1, BIN), 1)
    row = jnp.zeros((1, BIN), f32)
    for j, part in enumerate(totals):
        row = jnp.where(lane == j, jnp.sum(part, keepdims=True), row)
    sums[...] = jnp.broadcast_to(row, (DEVICES, BIN))


def step_kernel(sums, iterate, residual, direction, image, new_iterate, new_residual, new_direction):
    row = jnp.sum(sums[...], axis=0, keepdims=True)
    old_norm, curvature, cross, square = (row[:, j : j + 1] for j in range(4))
    step = old_norm / curvature
    new_norm = old_norm - 2.0 * step * cross + step * step * square
    d = direction[...]
    r = residual[...] - step * image[...]
    new_iterate[...] = iterate[...] + step * d
    new_residual[...] = r
    new_direction[...] = r + (new_norm / old_norm) * d


VMEM = pl.BlockSpec(memory_space=pltpu.VMEM)
SMEM = pl.BlockSpec(memory_space=pltpu.SMEM)


def params():
    return pltpu.CompilerParams(vmem_limit_bytes=16 * 1024 * 1024)


def on_device(solution, residual, direction, offsets, noise, bin_cells, lengths):
    depth_tabs = depth_tables()
    plane = plane_tables()
    d, r = direction.reshape(BINS, BIN), residual.reshape(BINS, BIN)
    offsets = offsets.reshape(3, BINS, BIN)
    cells_down = bin_cells.T

    blocks = pl.pallas_call(
        spread_kernel,
        out_shape=jax.ShapeDtypeStruct((4 * DEVICES, 128), f32),
        in_specs=[VMEM] * 6,
        out_specs=VMEM,
        scratch_shapes=[pltpu.VMEM((4 * BINS, CELLS), bf16)] * 2,
        compiler_params=params(),
        name="spread",
    )(d, offsets, cells_down, bin_cells, *depth_tabs[:2])
    received = lax.all_to_all(blocks.reshape(DEVICES, 4, 128), ("px", "py"), 0, 0, tiled=True)

    tables = (
        *plane["blocks"], *plane["blocks_back"], *plane["inner"], *plane["inner_back"], *plane["twist"],
        *plane["sine_x"], *plane["sine_y"], plane["weight"],
    )
    filtered = pl.pallas_call(
        plane_kernel,
        out_shape=jax.ShapeDtypeStruct((4 * DEVICES, 128), f32),
        in_specs=[SMEM] * 2 + [VMEM] * (1 + len(tables)),
        out_specs=VMEM,
        scratch_shapes=[
            pltpu.VMEM((DEVICES, 512), bf16),
            pltpu.VMEM((DEVICES, 512), bf16),
            pltpu.VMEM((2 * CHUNK, 512), f32),
            pltpu.VMEM((2 * CHUNK, 512), bf16),
            pltpu.VMEM((2 * CHUNK, 512), bf16),
            pltpu.VMEM((2 * CHUNK, 256), f32),
            pltpu.VMEM((2 * CHUNK, 256), bf16),
            pltpu.VMEM((2 * CHUNK, 256), bf16),
            pltpu.VMEM((DEVICES, 512), f32),
        ],
        compiler_params=params(),
        name="plane",
    )(lengths, plane["depth_sine"], received.reshape(4 * DEVICES, 128), *tables)
    returned = lax.all_to_all(filtered.reshape(DEVICES, 4, 128), ("px", "py"), 0, 0, tiled=True)

    image, sums = pl.pallas_call(
        gather_kernel,
        out_shape=(jax.ShapeDtypeStruct((BINS, BIN), f32), jax.ShapeDtypeStruct((DEVICES, BIN), f32)),
        in_specs=[VMEM] * 8,
        out_specs=(VMEM, VMEM),
        scratch_shapes=[pltpu.VMEM((2 * GRID_Z, CELLS), bf16)] * 2 + [pltpu.VMEM((GRID_Z, CELLS), bf16)] * 2,
        compiler_params=params(),
        name="interpolate",
    )(returned.reshape(4 * DEVICES, 128), d, r, noise.reshape(BINS, BIN), offsets, cells_down, *depth_tabs[2:])

    everywhere = lax.all_to_all(sums.reshape(DEVICES, 1, BIN), ("px", "py"), 0, 0, tiled=True)
    outs = pl.pallas_call(
        step_kernel,
        out_shape=(jax.ShapeDtypeStruct((BINS, BIN), f32),) * 3,
        in_specs=[VMEM] * 5,
        out_specs=(VMEM,) * 3,
        compiler_params=params(),
        name="step",
    )(everywhere.reshape(DEVICES, BIN), solution.reshape(BINS, BIN), r, d, image)
    return tuple(out.reshape(1, -1) for out in outs)


def solution(mesh):
    points = P(None, ("px", "py"))
    return jax.shard_map(
        on_device,
        mesh=mesh,
        in_specs=(points, points, points, points, P(("px", "py")), points, P()),
        out_specs=(points, points, points),
        check_vma=False,
    )
```

```python
import jax
import jax.numpy as jnp
import ml_dtypes
import numpy as np
from jax import lax
from jax.experimental import pallas as pl
from jax.experimental.pallas import tpu as pltpu
from jax.sharding import PartitionSpec as P

GRID_X, GRID_Y, GRID_Z = 128, 256, 256
BIN = 128
N_PX, N_PY = 32, 8
DEVICES = N_PX * N_PY
ROWS, COLUMNS = GRID_X // N_PX, GRID_Y // N_PY
SPAN_X, SPAN_Y = ROWS + 3, COLUMNS + 3
CELLS = 256
M_X, M_Y, M_Z = 2 * GRID_X, 2 * GRID_Y, 2 * GRID_Z - 1
BINS = 256
SPREAD_GROUP, READ_GROUP = 32, 64
BLOCK_X, BLOCK_Y = M_X // ROWS, M_Y // COLUMNS
CHUNKS = 3
PER_CHUNK = (BLOCK_X // 2 + 1) // CHUNKS
CHUNK = PER_CHUNK * BLOCK_Y
BACK = 384
SMALL_ROWS = 208

f32, bf16 = jnp.float32, jnp.bfloat16


def halves(table):
    table = np.asarray(table, np.float64)
    high = table.astype(np.float32).astype(ml_dtypes.bfloat16)
    low = (table - high.astype(np.float64)).astype(np.float32).astype(ml_dtypes.bfloat16)
    return np.concatenate([high, low], -1)


def depth_tables():
    freq = np.arange(GRID_Z)[:, None]
    depth = np.arange(GRID_Z)[None, :]
    angle = 2 * np.pi * (freq * depth % M_Z) / M_Z
    forward = np.concatenate([np.cos(angle), -np.sin(angle)], 0)
    doubled = np.where(freq == 0, 1.0, 2.0) / M_Z
    inverse = np.concatenate([np.cos(angle) * doubled, -np.sin(angle) * doubled], 0).T
    return halves(forward), halves(inverse)


def plane_tables():
    kx = np.arange(BLOCK_X // 2 + 1)
    ky = np.arange(BLOCK_Y)
    source = np.arange(DEVICES)
    px, py = source // N_PY, source % N_PY
    phase = (kx[:, None, None] * px / BLOCK_X + ky[None, :, None] * py / BLOCK_Y) * 2 * np.pi
    phase = phase.reshape(CHUNKS, CHUNK, DEVICES)
    blocks = np.concatenate([np.cos(phase), np.sin(phase)], 1)
    back = np.pad(blocks.transpose(0, 2, 1), ((0, 0), (0, 0), (0, BACK - 2 * CHUNK)))
    lane = np.arange(CELLS)
    live = lane < SPAN_X * SPAN_Y
    a, e = lane // SPAN_Y - 1, lane % SPAN_Y - 1
    twist_x = 2 * np.pi * kx[:, None] * a / M_X
    twist_y = 2 * np.pi * ky[:, None] * e / M_Y
    out = np.arange(ROWS * COLUMNS)
    high_x, high_y = out // COLUMNS, out % COLUMNS
    inner = 2 * np.pi * (a[:, None] * high_x[None, :] / ROWS + e[:, None] * high_y[None, :] / COLUMNS)
    c, s = np.cos(inner) * live[:, None], np.sin(inner) * live[:, None]
    full_x = BLOCK_X * high_x[None, :]
    full_y = BLOCK_Y * high_y[None, :]
    sine_x = [np.sin(np.pi * (sign * kx[:, None] + full_x) / M_X) ** 2 for sign in (1, -1)]
    sine_y = [np.sin(np.pi * (sign * ky[:, None] + full_y) / M_Y) ** 2 for sign in (1, -1)]
    scale = 1.0 / (M_X * M_Y)
    weight = np.where((kx == 0) | (kx == BLOCK_X // 2), 0.0, scale)[:, None] * np.ones((1, ROWS * COLUMNS))
    depth_sine = np.sin(np.pi * np.arange(GRID_Z) / M_Z) ** 2
    rows = [np.zeros((SMALL_ROWS, CELLS))]
    rows[0][0:16], rows[0][16:32] = np.cos(twist_y), -np.sin(twist_y)
    rows[0][32:48] = np.concatenate(sine_y, 1)
    rows[0][48:81], rows[0][88:121] = np.cos(twist_x), -np.sin(twist_x)
    rows[0][128:161] = np.concatenate(sine_x, 1)
    rows[0][168:201, :128] = weight
    rows[0][201] = depth_sine
    return (
        halves(blocks),
        halves(back),
        halves(np.block([[c, -s], [s, c]])),
        halves(np.block([[c.T, s.T], [-s.T, c.T]])),
        rows[0].astype(np.float32),
    )


def split(values):
    high = values.astype(bf16)
    return high, (values - high.astype(f32)).astype(bf16)


def dot(a, b):
    return jnp.dot(a, b, preferred_element_type=f32)


def dot_nt(a, b):
    return lax.dot_general(a, b, (((1,), (1,)), ((), ())), preferred_element_type=f32)


def dot3(a, b, mul=dot):
    side = 1 if mul is dot_nt else 0
    return mul(jnp.concatenate([a[0], a[0], a[1]], 1), jnp.concatenate([b[0], b[1], b[0]], side))


def cubic_weights(t):
    return (
        ((-0.5 * t + 1.0) * t - 0.5) * t,
        (1.5 * t - 2.5) * t * t + 1.0,
        ((-1.5 * t + 2.0) * t + 0.5) * t,
        (0.5 * t - 0.5) * t * t,
    )


def one_hot(hit):
    return jnp.where(hit, 1.0, 0.0).astype(bf16)


def iota(shape, dim):
    return lax.broadcasted_iota(jnp.int32, shape, dim)


def stencil_cells(base):
    shift = iota(base.shape, 1) - base
    return jnp.concatenate([one_hot(shift == a * SPAN_Y + e) for a in range(4) for e in range(4)], 0)


def same_bin(shape, group):
    return ((iota(shape, 0) ^ iota(shape, 1)) & (group - 1)) == 0


def group_slice(g, size):
    return pl.ds(pl.multiple_of(g * size, size), size)


def twice(lanes):
    return jnp.concatenate([lanes, lanes], 1)


def spread_kernel(
    direction_hbm, offsets_hbm, cells_hbm, forward_hbm,
    out, offsets, base, depth,
    direction, cells, forward, q_hi, q_lo, sems,
):
    group = SPREAD_GROUP
    copies = [
        pltpu.make_async_copy(cells_hbm, cells, sems.at[0]),
        pltpu.make_async_copy(direction_hbm, direction, sems.at[1]),
        *(pltpu.make_async_copy(offsets_hbm.at[:, d, :], offsets.at[d], sems.at[2 + d]) for d in range(3)),
        pltpu.make_async_copy(forward_hbm, forward, sems.at[5]),
    ]
    for copy in copies:
        copy.start()
    copies[0].wait()
    first = (cells[0:1, :] - lax.axis_index("px") * ROWS) * SPAN_Y + cells[1:2, :] - lax.axis_index("py") * COLUMNS
    packed = (first + 256 * cells[2:3, :]).astype(f32)
    own = iota((BINS, BINS), 0) == iota((BINS, BINS), 1)
    packed = jnp.sum(jnp.where(own, packed, 0.0), axis=1, keepdims=True).astype(jnp.int32)
    base[...] = jnp.broadcast_to(packed & 255, (BINS, 128))
    depth[...] = jnp.broadcast_to(packed >> 8, (BINS, 128))
    for copy in copies[1:5]:
        copy.wait()

    def step(g, _):
        bins = group_slice(g, group)
        wx = cubic_weights(offsets[0, bins, :])
        wy = cubic_weights(offsets[1, bins, :])
        wz = cubic_weights(offsets[2, bins, :])
        d = direction[bins, :]
        wx = [w * d for w in wx]
        columns = split(jnp.concatenate([x * y for x in wx for y in wy], 0))
        depths = split(jnp.concatenate(wz, 0))
        patches = dot3(depths, columns, dot_nt)
        patches = split(jnp.where(same_bin(patches.shape, group), patches, 0.0))
        placed = split(dot(jnp.concatenate(patches, 1), jnp.concatenate([stencil_cells(twice(base[bins, :]))] * 2, 0)))
        for f in range(4):
            rows = pl.ds(pl.multiple_of(f * BINS + g * group, group), group)
            q_hi[rows, :] = placed[0][f * group : (f + 1) * group]
            q_lo[rows, :] = placed[1][f * group : (f + 1) * group]
        return 0

    lax.fori_loop(0, BINS // group, step, 0, unroll=4)
    shift = iota((GRID_Z, BINS), 0) - cells[2:3, :]
    at_depth = jnp.concatenate([one_hot(shift == f - 1) for f in range(4)], 1)
    gridded = split(dot(twice(at_depth), jnp.concatenate([q_hi[...], q_lo[...]], 0)))
    copies[5].wait()
    transformed = dot3((forward[:, :GRID_Z], forward[:, GRID_Z:]), gridded)
    for part in range(2):
        for half in range(2):
            out[pl.ds(2 * part + half, GRID_Z, stride=4), :] = transformed[
                part * GRID_Z : (part + 1) * GRID_Z, half * 128 : (half + 1) * 128
            ]


def plane_kernel(
    lengths, received, blocks, back, inner, inner_back, small, out, r_hi, r_lo, wide, m_hi, m_lo, narrow, g_hi, g_lo
):
    for j in range(4):
        lanes = slice(128 * j, 128 * (j + 1))
        r_hi[:, lanes], r_lo[:, lanes] = split(received[pl.ds(j, DEVICES, stride=4), :])
    scale_x, scale_y = lengths[0] * lengths[0], lengths[1] * lengths[1]
    frequency = lax.axis_index("px") * N_PY + lax.axis_index("py")
    sine = jnp.sum(jnp.where(iota((1, GRID_Z), 1) == frequency, small[201:202, :], 0.0), axis=1, keepdims=True)
    rest = 1.0 + lengths[2] * lengths[2] * sine
    factor = 2.0 * lengths[0] * lengths[1] * lengths[2]
    ty_re, ty_im = small[0:16, :], small[16:32, :]
    rest_y = [rest + scale_y * small[32:48, 128 * part : 128 * (part + 1)] for part in range(2)]
    total = 0.0
    for c in range(CHUNKS):
        left = (blocks[c, :, :DEVICES], blocks[c, :, DEVICES:])
        wide[c] = dot3(left, (r_hi[...], r_lo[...]))
        spans = []
        for j in range(PER_CHUNK):
            kx = c * PER_CHUNK + j
            top = slice(j * BLOCK_Y, (j + 1) * BLOCK_Y)
            bottom = slice(CHUNK + j * BLOCK_Y, CHUNK + (j + 1) * BLOCK_Y)
            tx_re, tx_im = small[48 + kx : 49 + kx, :], small[88 + kx : 89 + kx, :]
            spans.append((kx, top, bottom, tx_re * ty_re - tx_im * ty_im, tx_re * ty_im + tx_im * ty_re))
        for kx, top, bottom, tr, ti in spans:
            cre, cim = wide[c, top, :CELLS], wide[c, top, CELLS:]
            sre, sim = wide[c, bottom, :CELLS], wide[c, bottom, CELLS:]
            ur, ui, vr, vi = cre + sim, cim - sre, cre - sim, cim + sre
            for rows, re, im in (
                (top, ur * tr - ui * ti, ur * ti + ui * tr),
                (bottom, vr * tr + vi * ti, vi * tr - vr * ti),
            ):
                m_hi[c, rows, :CELLS], m_lo[c, rows, :CELLS] = split(re)
                m_hi[c, rows, CELLS:], m_lo[c, rows, CELLS:] = split(im)
        narrow[c] = dot3((m_hi[c], m_lo[c]), (inner[:, :CELLS], inner[:, CELLS:]))
        for kx, top, bottom, tr, ti in spans:
            for part, rows in enumerate((top, bottom)):
                lanes = slice(128 * part, 128 * (part + 1))
                denominator = rest_y[part] + scale_x * small[128 + kx : 129 + kx, lanes]
                weight = factor * (1.0 / (M_X * M_Y)) if part == 0 else factor * small[168 + kx : 169 + kx, :128]
                spectrum = twice(weight / (denominator * denominator))
                g_hi[c, rows, :], g_lo[c, rows, :] = split(narrow[c, rows, :] * spectrum)
        wide[c] = dot3((g_hi[c], g_lo[c]), (inner_back[:, : 2 * CELLS], inner_back[:, 2 * CELLS :]))
        for kx, top, bottom, tr, ti in spans:
            zr, zi = wide[c, top, :CELLS], wide[c, top, CELLS:]
            yr, yi = wide[c, bottom, :CELLS], wide[c, bottom, CELLS:]
            ar, ai = zr * tr + zi * ti, zi * tr - zr * ti
            br, bi = yr * tr - yi * ti, yr * ti + yi * tr
            for rows, re, im in ((top, ar + br, ai + bi), (bottom, bi - ai, ar - br)):
                m_hi[c, rows, :CELLS], m_lo[c, rows, :CELLS] = split(re)
                m_hi[c, rows, CELLS:], m_lo[c, rows, CELLS:] = split(im)
        left = (back[c, :, : 2 * CHUNK], back[c, :, BACK : BACK + 2 * CHUNK])
        total = total + dot3(left, (m_hi[c], m_lo[c]))
    for j in range(4):
        out[pl.ds(j, DEVICES, stride=4), :] = total[:, 128 * j : 128 * (j + 1)]


def gather_kernel(received, direction, residual, noise, offsets, base, depth, inverse, image, sums, v_hi, v_lo):
    group = READ_GROUP
    for part in range(2):
        for half in range(2):
            rows = slice(part * GRID_Z, (part + 1) * GRID_Z)
            lanes = slice(half * 128, (half + 1) * 128)
            v_hi[rows, lanes], v_lo[rows, lanes] = split(received[pl.ds(2 * part + half, GRID_Z, stride=4), :])
    grid = split(dot3((inverse[:, : 2 * GRID_Z], inverse[:, 2 * GRID_Z :]), (v_hi[...], v_lo[...])))
    v_hi[:GRID_Z, :], v_lo[:GRID_Z, :] = grid

    def step(g, carry):
        bins = group_slice(g, group)
        shift = iota((group, GRID_Z), 1) - twice(depth[bins, :])
        at_depth = jnp.concatenate([one_hot(shift == f - 1) for f in range(4)], 0)
        lines_hi = dot(at_depth, v_hi[:GRID_Z, :]).astype(bf16)
        lines_lo = dot(at_depth, v_lo[:GRID_Z, :]).astype(bf16)
        cells = stencil_cells(twice(base[bins, :]))
        keep = same_bin((16 * group, 4 * group), group)
        read_hi = jnp.where(keep, dot_nt(cells, lines_hi), 0.0).astype(bf16)
        read_lo = jnp.where(keep, dot_nt(cells, lines_lo), 0.0).astype(bf16)
        depths = split(jnp.concatenate(cubic_weights(offsets[2, bins, :]), 0))
        along = dot3((read_hi, read_lo), depths)
        wx = cubic_weights(offsets[0, bins, :])
        wy = cubic_weights(offsets[1, bins, :])
        value = 0.0
        for a in range(4):
            row = 0.0
            for e in range(4):
                start = (4 * a + e) * group
                row = row + wy[e] * along[start : start + group]
            value = value + wx[a] * row
        d, r = direction[bins, :], residual[bins, :]
        value = value + noise[bins, :] * d
        image[bins, :] = value
        return tuple(
            total + (x * y).reshape(group // 8, 8, BIN).sum(0)
            for total, (x, y) in zip(carry, ((r, r), (d, value), (r, value), (value, value)))
        )

    zero = jnp.zeros((8, BIN), f32)
    totals = lax.fori_loop(0, BINS // group, step, (zero,) * 4, unroll=2)
    lane = iota((1, BIN), 1)
    row = jnp.zeros((1, BIN), f32)
    for j, part in enumerate(totals):
        row = jnp.where(lane == j, jnp.sum(part, keepdims=True), row)
    sums[...] = jnp.broadcast_to(row, (DEVICES, BIN))


def step_kernel(sums, iterate, residual, direction, image, new_iterate, new_residual, new_direction):
    row = jnp.sum(sums[...], axis=0, keepdims=True)
    old_norm, curvature, cross, square = (row[:, j : j + 1] for j in range(4))
    step = old_norm / curvature
    new_norm = old_norm - 2.0 * step * cross + step * step * square
    d = direction[...]
    r = residual[...] - step * image[...]
    new_iterate[...] = iterate[...] + step * d
    new_residual[...] = r
    new_direction[...] = r + (new_norm / old_norm) * d


VMEM = pl.BlockSpec(memory_space=pltpu.VMEM)
HBM = pl.BlockSpec(memory_space=pltpu.HBM)
SMEM = pl.BlockSpec(memory_space=pltpu.SMEM)


def params():
    return pltpu.CompilerParams(vmem_limit_bytes=16 * 1024 * 1024)


def on_device(solution, residual, direction, offsets, noise, bin_cells, lengths):
    forward, inverse = depth_tables()
    d, r = direction.reshape(BINS, BIN), residual.reshape(BINS, BIN)
    point = jax.ShapeDtypeStruct((BINS, BIN), f32)
    index = jax.ShapeDtypeStruct((BINS, BIN), jnp.int32)
    block = jax.ShapeDtypeStruct((4 * DEVICES, 128), f32)

    blocks, by_bin, base, depth = pl.pallas_call(
        spread_kernel,
        out_shape=(block, jax.ShapeDtypeStruct((3, BINS, BIN), f32), index, index),
        in_specs=[HBM] * 4,
        out_specs=(VMEM,) * 4,
        scratch_shapes=[
            pltpu.VMEM((BINS, BIN), f32),
            pltpu.VMEM((3, BINS), jnp.int32),
            pltpu.VMEM(forward.shape, bf16),
            pltpu.VMEM((4 * BINS, CELLS), bf16),
            pltpu.VMEM((4 * BINS, CELLS), bf16),
            pltpu.SemaphoreType.DMA((6,)),
        ],
        compiler_params=params(),
        name="spread",
    )(d, offsets.reshape(3, BINS, BIN).transpose(1, 0, 2), bin_cells, forward)
    received = lax.all_to_all(blocks.reshape(DEVICES, 4, 128), ("px", "py"), 0, 0, tiled=True)

    filtered = pl.pallas_call(
        plane_kernel,
        out_shape=block,
        in_specs=[SMEM] + [VMEM] * 6,
        out_specs=VMEM,
        scratch_shapes=[
            pltpu.VMEM((DEVICES, 512), bf16),
            pltpu.VMEM((DEVICES, 512), bf16),
            pltpu.VMEM((CHUNKS, 2 * CHUNK, 512), f32),
            pltpu.VMEM((CHUNKS, 2 * CHUNK, 512), bf16),
            pltpu.VMEM((CHUNKS, 2 * CHUNK, 512), bf16),
            pltpu.VMEM((CHUNKS, 2 * CHUNK, 256), f32),
            pltpu.VMEM((CHUNKS, 2 * CHUNK, 256), bf16),
            pltpu.VMEM((CHUNKS, 2 * CHUNK, 256), bf16),
        ],
        compiler_params=params(),
        name="plane",
    )(lengths, received.reshape(4 * DEVICES, 128), *plane_tables())
    returned = lax.all_to_all(filtered.reshape(DEVICES, 4, 128), ("px", "py"), 0, 0, tiled=True)

    image, sums = pl.pallas_call(
        gather_kernel,
        out_shape=(point, jax.ShapeDtypeStruct((DEVICES, BIN), f32)),
        in_specs=[VMEM] * 8,
        out_specs=(VMEM, VMEM),
        scratch_shapes=[pltpu.VMEM((2 * GRID_Z, CELLS), bf16)] * 2,
        compiler_params=params(),
        name="interpolate",
    )(returned.reshape(4 * DEVICES, 128), d, r, noise.reshape(BINS, BIN), by_bin, base, depth, inverse)

    everywhere = lax.all_to_all(sums.reshape(DEVICES, 1, BIN), ("px", "py"), 0, 0, tiled=True)
    outs = pl.pallas_call(
        step_kernel,
        out_shape=(point,) * 3,
        in_specs=[VMEM] * 5,
        out_specs=(VMEM,) * 3,
        compiler_params=params(),
        name="step",
    )(everywhere.reshape(DEVICES, BIN), solution.reshape(BINS, BIN), r, d, image)
    return tuple(out.reshape(1, -1) for out in outs)


def solution(mesh):
    points = P(None, ("px", "py"))
    return jax.shard_map(
        on_device,
        mesh=mesh,
        in_specs=(points, points, points, points, P(("px", "py")), points, P()),
        out_specs=(points, points, points),
        check_vma=False,
    )
```

```python
import jax
import jax.numpy as jnp
import ml_dtypes
import numpy as np
from jax import lax
from jax.experimental import pallas as pl
from jax.experimental.pallas import tpu as pltpu
from jax.sharding import PartitionSpec as P

GRID_X, GRID_Y, GRID_Z = 128, 256, 256
BIN = 128
N_PX, N_PY = 32, 8
DEVICES = N_PX * N_PY
ROWS, COLUMNS = GRID_X // N_PX, GRID_Y // N_PY
SPAN_X, SPAN_Y = ROWS + 3, COLUMNS + 3
CELLS = 256
M_X, M_Y, M_Z = 2 * GRID_X, 2 * GRID_Y, 2 * GRID_Z - 1
BINS = 256
SPREAD_GROUP, READ_GROUP = 32, 64
BLOCK_X, BLOCK_Y = M_X // ROWS, M_Y // COLUMNS
CHUNKS = 3
PER_CHUNK = (BLOCK_X // 2 + 1) // CHUNKS
CHUNK = PER_CHUNK * BLOCK_Y
BACK = 384
SMALL_ROWS = 208
TABLES = 5

f32, bf16 = jnp.float32, jnp.bfloat16


def halves(table):
    table = np.asarray(table, np.float64)
    high = table.astype(np.float32).astype(ml_dtypes.bfloat16)
    low = (table - high.astype(np.float64)).astype(np.float32).astype(ml_dtypes.bfloat16)
    return np.concatenate([high, low], -1)


def depth_tables():
    freq = np.arange(GRID_Z)[:, None]
    depth = np.arange(GRID_Z)[None, :]
    angle = 2 * np.pi * (freq * depth % M_Z) / M_Z
    forward = np.concatenate([np.cos(angle), -np.sin(angle)], 0)
    doubled = np.where(freq == 0, 1.0, 2.0) / M_Z
    inverse = np.concatenate([np.cos(angle) * doubled, -np.sin(angle) * doubled], 0).T
    return halves(forward), halves(inverse)


def plane_tables():
    kx = np.arange(BLOCK_X // 2 + 1)
    ky = np.arange(BLOCK_Y)
    source = np.arange(DEVICES)
    px, py = source // N_PY, source % N_PY
    phase = (kx[:, None, None] * px / BLOCK_X + ky[None, :, None] * py / BLOCK_Y) * 2 * np.pi
    phase = phase.reshape(CHUNKS, CHUNK, DEVICES)
    blocks = np.concatenate([np.cos(phase), np.sin(phase)], 1)
    back = np.pad(blocks.transpose(0, 2, 1), ((0, 0), (0, 0), (0, BACK - 2 * CHUNK)))
    lane = np.arange(CELLS)
    live = lane < SPAN_X * SPAN_Y
    a, e = lane // SPAN_Y - 1, lane % SPAN_Y - 1
    twist_x = 2 * np.pi * kx[:, None] * a / M_X
    twist_y = 2 * np.pi * ky[:, None] * e / M_Y
    out = np.arange(ROWS * COLUMNS)
    high_x, high_y = out // COLUMNS, out % COLUMNS
    inner = 2 * np.pi * (a[:, None] * high_x[None, :] / ROWS + e[:, None] * high_y[None, :] / COLUMNS)
    c, s = np.cos(inner) * live[:, None], np.sin(inner) * live[:, None]
    full_x = BLOCK_X * high_x[None, :]
    full_y = BLOCK_Y * high_y[None, :]
    sine_x = [np.sin(np.pi * (sign * kx[:, None] + full_x) / M_X) ** 2 for sign in (1, -1)]
    sine_y = [np.sin(np.pi * (sign * ky[:, None] + full_y) / M_Y) ** 2 for sign in (1, -1)]
    scale = 1.0 / (M_X * M_Y)
    weight = np.where((kx == 0) | (kx == BLOCK_X // 2), 0.0, scale)[:, None] * np.ones((1, ROWS * COLUMNS))
    depth_sine = np.sin(np.pi * np.arange(GRID_Z) / M_Z) ** 2
    rows = [np.zeros((SMALL_ROWS, CELLS))]
    rows[0][0:16], rows[0][16:32] = np.cos(twist_y), -np.sin(twist_y)
    rows[0][32:48] = np.concatenate(sine_y, 1)
    rows[0][48:81], rows[0][88:121] = np.cos(twist_x), -np.sin(twist_x)
    rows[0][128:161] = np.concatenate(sine_x, 1)
    rows[0][168:201, :128] = weight
    rows[0][201] = depth_sine
    return (
        halves(blocks),
        halves(back),
        halves(np.block([[c, -s], [s, c]])),
        halves(np.block([[c.T, s.T], [-s.T, c.T]])),
        rows[0].astype(np.float32),
    )


def split(values):
    high = values.astype(bf16)
    return high, (values - high.astype(f32)).astype(bf16)


def dot(a, b):
    return jnp.dot(a, b, preferred_element_type=f32)


def dot_nt(a, b):
    return lax.dot_general(a, b, (((1,), (1,)), ((), ())), preferred_element_type=f32)


def dot3(a, b, mul=dot):
    side = 1 if mul is dot_nt else 0
    return mul(jnp.concatenate([a[0], a[0], a[1]], 1), jnp.concatenate([b[0], b[1], b[0]], side))


def cubic_weights(t):
    return (
        ((-0.5 * t + 1.0) * t - 0.5) * t,
        (1.5 * t - 2.5) * t * t + 1.0,
        ((-1.5 * t + 2.0) * t + 0.5) * t,
        (0.5 * t - 0.5) * t * t,
    )


def one_hot(hit):
    return jnp.where(hit, 1.0, 0.0).astype(bf16)


def iota(shape, dim):
    return lax.broadcasted_iota(jnp.int32, shape, dim)


def stencil_cells(base):
    shift = iota(base.shape, 1) - base
    return jnp.concatenate([one_hot(shift == a * SPAN_Y + e) for a in range(4) for e in range(4)], 0)


def same_bin(shape, group):
    return ((iota(shape, 0) ^ iota(shape, 1)) & (group - 1)) == 0


def group_slice(g, size):
    return pl.ds(pl.multiple_of(g * size, size), size)


def twice(lanes):
    return jnp.concatenate([lanes, lanes], 1)


def spread_kernel(
    direction_hbm, offsets_hbm, cells_hbm, forward_hbm, *refs
):
    tables_hbm, (out, offsets, base, depth), tables = refs[:TABLES], refs[TABLES : TABLES + 4], refs[TABLES + 4 : 2 * TABLES + 4]
    direction, cells, forward, q_hi, q_lo, sems = refs[2 * TABLES + 4 :]
    group = SPREAD_GROUP
    copies = [
        pltpu.make_async_copy(cells_hbm, cells, sems.at[0]),
        pltpu.make_async_copy(direction_hbm, direction, sems.at[1]),
        *(pltpu.make_async_copy(offsets_hbm.at[:, d, :], offsets.at[d], sems.at[2 + d]) for d in range(3)),
        pltpu.make_async_copy(forward_hbm, forward, sems.at[5]),
        *(pltpu.make_async_copy(tables_hbm[t], tables[t], sems.at[6 + t]) for t in range(TABLES)),
    ]
    for copy in copies:
        copy.start()
    copies[0].wait()
    first = (cells[0:1, :] - lax.axis_index("px") * ROWS) * SPAN_Y + cells[1:2, :] - lax.axis_index("py") * COLUMNS
    packed = (first + 256 * cells[2:3, :]).astype(f32)
    own = iota((BINS, BINS), 0) == iota((BINS, BINS), 1)
    packed = jnp.sum(jnp.where(own, packed, 0.0), axis=1, keepdims=True).astype(jnp.int32)
    base[...] = jnp.broadcast_to(packed & 255, (BINS, 128))
    depth[...] = jnp.broadcast_to(packed >> 8, (BINS, 128))
    for copy in copies[1:5]:
        copy.wait()

    def step(g, _):
        bins = group_slice(g, group)
        wx = cubic_weights(offsets[0, bins, :])
        wy = cubic_weights(offsets[1, bins, :])
        wz = cubic_weights(offsets[2, bins, :])
        d = direction[bins, :]
        wx = [w * d for w in wx]
        columns = split(jnp.concatenate([x * y for x in wx for y in wy], 0))
        depths = split(jnp.concatenate(wz, 0))
        patches = dot3(depths, columns, dot_nt)
        patches = split(jnp.where(same_bin(patches.shape, group), patches, 0.0))
        placed = split(dot(jnp.concatenate(patches, 1), jnp.concatenate([stencil_cells(twice(base[bins, :]))] * 2, 0)))
        for f in range(4):
            rows = pl.ds(pl.multiple_of(f * BINS + g * group, group), group)
            q_hi[rows, :] = placed[0][f * group : (f + 1) * group]
            q_lo[rows, :] = placed[1][f * group : (f + 1) * group]
        return 0

    lax.fori_loop(0, BINS // group, step, 0, unroll=4)
    shift = iota((GRID_Z, BINS), 0) - cells[2:3, :]
    at_depth = jnp.concatenate([one_hot(shift == f - 1) for f in range(4)], 1)
    gridded = split(dot(twice(at_depth), jnp.concatenate([q_hi[...], q_lo[...]], 0)))
    copies[5].wait()
    transformed = dot3((forward[:, :GRID_Z], forward[:, GRID_Z:]), gridded)
    for part in range(2):
        for half in range(2):
            out[pl.ds(2 * part + half, GRID_Z, stride=4), :] = transformed[
                part * GRID_Z : (part + 1) * GRID_Z, half * 128 : (half + 1) * 128
            ]
    for copy in copies[6:]:
        copy.wait()


def plane_kernel(
    lengths, received, blocks, back, inner, inner_back, small, out, r_hi, r_lo, wide, m_hi, m_lo, narrow, g_hi, g_lo
):
    for j in range(4):
        lanes = slice(128 * j, 128 * (j + 1))
        r_hi[:, lanes], r_lo[:, lanes] = split(received[pl.ds(j, DEVICES, stride=4), :])
    scale_x, scale_y = lengths[0] * lengths[0], lengths[1] * lengths[1]
    frequency = lax.axis_index("px") * N_PY + lax.axis_index("py")
    sine = jnp.sum(jnp.where(iota((1, GRID_Z), 1) == frequency, small[201:202, :], 0.0), axis=1, keepdims=True)
    rest = 1.0 + lengths[2] * lengths[2] * sine
    factor = 2.0 * lengths[0] * lengths[1] * lengths[2]
    ty_re, ty_im = small[0:16, :], small[16:32, :]
    rest_y = [rest + scale_y * small[32:48, 128 * part : 128 * (part + 1)] for part in range(2)]
    total = 0.0
    for c in range(CHUNKS):
        left = (blocks[c, :, :DEVICES], blocks[c, :, DEVICES:])
        wide[c] = dot3(left, (r_hi[...], r_lo[...]))
        spans = []
        for j in range(PER_CHUNK):
            kx = c * PER_CHUNK + j
            top = slice(j * BLOCK_Y, (j + 1) * BLOCK_Y)
            bottom = slice(CHUNK + j * BLOCK_Y, CHUNK + (j + 1) * BLOCK_Y)
            tx_re, tx_im = small[48 + kx : 49 + kx, :], small[88 + kx : 89 + kx, :]
            spans.append((kx, top, bottom, tx_re * ty_re - tx_im * ty_im, tx_re * ty_im + tx_im * ty_re))
        for kx, top, bottom, tr, ti in spans:
            cre, cim = wide[c, top, :CELLS], wide[c, top, CELLS:]
            sre, sim = wide[c, bottom, :CELLS], wide[c, bottom, CELLS:]
            ur, ui, vr, vi = cre + sim, cim - sre, cre - sim, cim + sre
            for rows, re, im in (
                (top, ur * tr - ui * ti, ur * ti + ui * tr),
                (bottom, vr * tr + vi * ti, vi * tr - vr * ti),
            ):
                m_hi[c, rows, :CELLS], m_lo[c, rows, :CELLS] = split(re)
                m_hi[c, rows, CELLS:], m_lo[c, rows, CELLS:] = split(im)
        narrow[c] = dot3((m_hi[c], m_lo[c]), (inner[:, :CELLS], inner[:, CELLS:]))
        for kx, top, bottom, tr, ti in spans:
            for part, rows in enumerate((top, bottom)):
                lanes = slice(128 * part, 128 * (part + 1))
                denominator = rest_y[part] + scale_x * small[128 + kx : 129 + kx, lanes]
                weight = factor * (1.0 / (M_X * M_Y)) if part == 0 else factor * small[168 + kx : 169 + kx, :128]
                spectrum = twice(weight / (denominator * denominator))
                g_hi[c, rows, :], g_lo[c, rows, :] = split(narrow[c, rows, :] * spectrum)
        wide[c] = dot3((g_hi[c], g_lo[c]), (inner_back[:, : 2 * CELLS], inner_back[:, 2 * CELLS :]))
        for kx, top, bottom, tr, ti in spans:
            zr, zi = wide[c, top, :CELLS], wide[c, top, CELLS:]
            yr, yi = wide[c, bottom, :CELLS], wide[c, bottom, CELLS:]
            ar, ai = zr * tr + zi * ti, zi * tr - zr * ti
            br, bi = yr * tr - yi * ti, yr * ti + yi * tr
            for rows, re, im in ((top, ar + br, ai + bi), (bottom, bi - ai, ar - br)):
                m_hi[c, rows, :CELLS], m_lo[c, rows, :CELLS] = split(re)
                m_hi[c, rows, CELLS:], m_lo[c, rows, CELLS:] = split(im)
        left = (back[c, :, : 2 * CHUNK], back[c, :, BACK : BACK + 2 * CHUNK])
        total = total + dot3(left, (m_hi[c], m_lo[c]))
    for j in range(4):
        out[pl.ds(j, DEVICES, stride=4), :] = total[:, 128 * j : 128 * (j + 1)]


def gather_kernel(received, direction, residual, noise, offsets, base, depth, inverse, image, sums, v_hi, v_lo):
    group = READ_GROUP
    for part in range(2):
        for half in range(2):
            rows = slice(part * GRID_Z, (part + 1) * GRID_Z)
            lanes = slice(half * 128, (half + 1) * 128)
            v_hi[rows, lanes], v_lo[rows, lanes] = split(received[pl.ds(2 * part + half, GRID_Z, stride=4), :])
    grid = split(dot3((inverse[:, : 2 * GRID_Z], inverse[:, 2 * GRID_Z :]), (v_hi[...], v_lo[...])))
    v_hi[:GRID_Z, :], v_lo[:GRID_Z, :] = grid

    def step(g, carry):
        bins = group_slice(g, group)
        shift = iota((group, GRID_Z), 1) - twice(depth[bins, :])
        at_depth = jnp.concatenate([one_hot(shift == f - 1) for f in range(4)], 0)
        lines_hi = dot(at_depth, v_hi[:GRID_Z, :]).astype(bf16)
        lines_lo = dot(at_depth, v_lo[:GRID_Z, :]).astype(bf16)
        cells = stencil_cells(twice(base[bins, :]))
        keep = same_bin((16 * group, 4 * group), group)
        read_hi = jnp.where(keep, dot_nt(cells, lines_hi), 0.0).astype(bf16)
        read_lo = jnp.where(keep, dot_nt(cells, lines_lo), 0.0).astype(bf16)
        depths = split(jnp.concatenate(cubic_weights(offsets[2, bins, :]), 0))
        along = dot3((read_hi, read_lo), depths)
        wx = cubic_weights(offsets[0, bins, :])
        wy = cubic_weights(offsets[1, bins, :])
        value = 0.0
        for a in range(4):
            row = 0.0
            for e in range(4):
                start = (4 * a + e) * group
                row = row + wy[e] * along[start : start + group]
            value = value + wx[a] * row
        d, r = direction[bins, :], residual[bins, :]
        value = value + noise[bins, :] * d
        image[bins, :] = value
        return tuple(
            total + (x * y).reshape(group // 8, 8, BIN).sum(0)
            for total, (x, y) in zip(carry, ((r, r), (d, value), (r, value), (value, value)))
        )

    zero = jnp.zeros((8, BIN), f32)
    totals = lax.fori_loop(0, BINS // group, step, (zero,) * 4, unroll=2)
    lane = iota((1, BIN), 1)
    row = jnp.zeros((1, BIN), f32)
    for j, part in enumerate(totals):
        row = jnp.where(lane == j, jnp.sum(part, keepdims=True), row)
    sums[...] = jnp.broadcast_to(row, (DEVICES, BIN))


def step_kernel(sums, iterate, residual, direction, image, new_iterate, new_residual, new_direction):
    row = jnp.sum(sums[...], axis=0, keepdims=True)
    old_norm, curvature, cross, square = (row[:, j : j + 1] for j in range(4))
    step = old_norm / curvature
    new_norm = old_norm - 2.0 * step * cross + step * step * square
    d = direction[...]
    r = residual[...] - step * image[...]
    new_iterate[...] = iterate[...] + step * d
    new_residual[...] = r
    new_direction[...] = r + (new_norm / old_norm) * d


VMEM = pl.BlockSpec(memory_space=pltpu.VMEM)
HBM = pl.BlockSpec(memory_space=pltpu.HBM)
SMEM = pl.BlockSpec(memory_space=pltpu.SMEM)


def params():
    return pltpu.CompilerParams(vmem_limit_bytes=16 * 1024 * 1024)


def on_device(solution, residual, direction, offsets, noise, bin_cells, lengths):
    forward, inverse = depth_tables()
    d, r = direction.reshape(BINS, BIN), residual.reshape(BINS, BIN)
    point = jax.ShapeDtypeStruct((BINS, BIN), f32)
    index = jax.ShapeDtypeStruct((BINS, BIN), jnp.int32)
    block = jax.ShapeDtypeStruct((4 * DEVICES, 128), f32)

    tables = plane_tables()
    by_tile = offsets.reshape(3, BINS, BIN).transpose(1, 0, 2)
    operands = [pltpu.with_memory_space_constraint(x, pltpu.HBM) for x in (d, by_tile, bin_cells, forward, *tables)]

    blocks, by_bin, base, depth, *tables = pl.pallas_call(
        spread_kernel,
        out_shape=(
            block, jax.ShapeDtypeStruct((3, BINS, BIN), f32), index, index,
            *(jax.ShapeDtypeStruct(t.shape, t.dtype) for t in tables),
        ),
        in_specs=[HBM] * len(operands),
        out_specs=(VMEM,) * (4 + TABLES),
        scratch_shapes=[
            pltpu.VMEM((BINS, BIN), f32),
            pltpu.VMEM((3, BINS), jnp.int32),
            pltpu.VMEM(forward.shape, bf16),
            pltpu.VMEM((4 * BINS, CELLS), bf16),
            pltpu.VMEM((4 * BINS, CELLS), bf16),
            pltpu.SemaphoreType.DMA((6 + TABLES,)),
        ],
        compiler_params=params(),
        name="spread",
    )(*operands)
    received = lax.all_to_all(blocks.reshape(DEVICES, 4, 128), ("px", "py"), 0, 0, tiled=True)

    filtered = pl.pallas_call(
        plane_kernel,
        out_shape=block,
        in_specs=[SMEM] + [VMEM] * 6,
        out_specs=VMEM,
        scratch_shapes=[
            pltpu.VMEM((DEVICES, 512), bf16),
            pltpu.VMEM((DEVICES, 512), bf16),
            pltpu.VMEM((CHUNKS, 2 * CHUNK, 512), f32),
            pltpu.VMEM((CHUNKS, 2 * CHUNK, 512), bf16),
            pltpu.VMEM((CHUNKS, 2 * CHUNK, 512), bf16),
            pltpu.VMEM((CHUNKS, 2 * CHUNK, 256), f32),
            pltpu.VMEM((CHUNKS, 2 * CHUNK, 256), bf16),
            pltpu.VMEM((CHUNKS, 2 * CHUNK, 256), bf16),
        ],
        compiler_params=params(),
        name="plane",
    )(lengths, received.reshape(4 * DEVICES, 128), *tables)
    returned = lax.all_to_all(filtered.reshape(DEVICES, 4, 128), ("px", "py"), 0, 0, tiled=True)

    image, sums = pl.pallas_call(
        gather_kernel,
        out_shape=(point, jax.ShapeDtypeStruct((DEVICES, BIN), f32)),
        in_specs=[VMEM] * 8,
        out_specs=(VMEM, VMEM),
        scratch_shapes=[pltpu.VMEM((2 * GRID_Z, CELLS), bf16)] * 2,
        compiler_params=params(),
        name="interpolate",
    )(returned.reshape(4 * DEVICES, 128), d, r, noise.reshape(BINS, BIN), by_bin, base, depth, inverse)

    everywhere = lax.all_to_all(sums.reshape(DEVICES, 1, BIN), ("px", "py"), 0, 0, tiled=True)
    outs = pl.pallas_call(
        step_kernel,
        out_shape=(point,) * 3,
        in_specs=[VMEM] * 5,
        out_specs=(VMEM,) * 3,
        compiler_params=params(),
        name="step",
    )(everywhere.reshape(DEVICES, BIN), solution.reshape(BINS, BIN), r, d, image)
    return tuple(out.reshape(1, -1) for out in outs)


def solution(mesh):
    points = P(None, ("px", "py"))
    return jax.shard_map(
        on_device,
        mesh=mesh,
        in_specs=(points, points, points, points, P(("px", "py")), points, P()),
        out_specs=(points, points, points),
        check_vma=False,
    )
```

```python
import jax
import jax.numpy as jnp
import ml_dtypes
import numpy as np
from jax import lax
from jax.experimental import pallas as pl
from jax.experimental.pallas import tpu as pltpu
from jax.sharding import PartitionSpec as P

GRID_X, GRID_Y, GRID_Z = 128, 256, 256
BIN = 128
N_PX, N_PY = 32, 8
DEVICES = N_PX * N_PY
ROWS, COLUMNS = GRID_X // N_PX, GRID_Y // N_PY
SPAN_X, SPAN_Y = ROWS + 3, COLUMNS + 3
CELLS = 256
M_X, M_Y, M_Z = 2 * GRID_X, 2 * GRID_Y, 2 * GRID_Z - 1
BINS = 256
SPREAD_GROUP, READ_GROUP = 32, 32
BLOCK_X, BLOCK_Y = M_X // ROWS, M_Y // COLUMNS
CHUNKS = 3
PER_CHUNK = (BLOCK_X // 2 + 1) // CHUNKS
CHUNK = PER_CHUNK * BLOCK_Y
BACK = 384
SMALL_ROWS = 208
TABLES = 5

f32, bf16 = jnp.float32, jnp.bfloat16


def halves(table):
    table = np.asarray(table, np.float64)
    high = table.astype(np.float32).astype(ml_dtypes.bfloat16)
    low = (table - high.astype(np.float64)).astype(np.float32).astype(ml_dtypes.bfloat16)
    return np.concatenate([high, low], -1)


def depth_tables():
    freq = np.arange(GRID_Z)[:, None]
    depth = np.arange(GRID_Z)[None, :]
    angle = 2 * np.pi * (freq * depth % M_Z) / M_Z
    forward = np.concatenate([np.cos(angle), -np.sin(angle)], 0)
    doubled = np.where(freq == 0, 1.0, 2.0) / M_Z
    inverse = np.concatenate([np.cos(angle) * doubled, -np.sin(angle) * doubled], 0).T
    return halves(forward), halves(inverse)


def plane_tables():
    kx = np.arange(BLOCK_X // 2 + 1)
    ky = np.arange(BLOCK_Y)
    source = np.arange(DEVICES)
    px, py = source // N_PY, source % N_PY
    phase = (kx[:, None, None] * px / BLOCK_X + ky[None, :, None] * py / BLOCK_Y) * 2 * np.pi
    phase = phase.reshape(CHUNKS, CHUNK, DEVICES)
    blocks = np.concatenate([np.cos(phase), np.sin(phase)], 1)
    back = np.pad(blocks.transpose(0, 2, 1), ((0, 0), (0, 0), (0, BACK - 2 * CHUNK)))
    lane = np.arange(CELLS)
    live = lane < SPAN_X * SPAN_Y
    a, e = lane // SPAN_Y - 1, lane % SPAN_Y - 1
    twist_x = 2 * np.pi * kx[:, None] * a / M_X
    twist_y = 2 * np.pi * ky[:, None] * e / M_Y
    out = np.arange(ROWS * COLUMNS)
    high_x, high_y = out // COLUMNS, out % COLUMNS
    inner = 2 * np.pi * (a[:, None] * high_x[None, :] / ROWS + e[:, None] * high_y[None, :] / COLUMNS)
    c, s = np.cos(inner) * live[:, None], np.sin(inner) * live[:, None]
    full_x = BLOCK_X * high_x[None, :]
    full_y = BLOCK_Y * high_y[None, :]
    sine_x = [np.sin(np.pi * (sign * kx[:, None] + full_x) / M_X) ** 2 for sign in (1, -1)]
    sine_y = [np.sin(np.pi * (sign * ky[:, None] + full_y) / M_Y) ** 2 for sign in (1, -1)]
    scale = 1.0 / (M_X * M_Y)
    weight = np.where((kx == 0) | (kx == BLOCK_X // 2), 0.0, scale)[:, None] * np.ones((1, ROWS * COLUMNS))
    depth_sine = np.sin(np.pi * np.arange(GRID_Z) / M_Z) ** 2
    rows = [np.zeros((SMALL_ROWS, CELLS))]
    rows[0][0:16], rows[0][16:32] = np.cos(twist_y), -np.sin(twist_y)
    rows[0][32:48] = np.concatenate(sine_y, 1)
    rows[0][48:81], rows[0][88:121] = np.cos(twist_x), -np.sin(twist_x)
    rows[0][128:161] = np.concatenate(sine_x, 1)
    rows[0][168:201, :128] = weight
    rows[0][201] = depth_sine
    return (
        halves(blocks),
        halves(back),
        halves(np.block([[c, -s], [s, c]])),
        halves(np.block([[c.T, s.T], [-s.T, c.T]])),
        rows[0].astype(np.float32),
    )


def split(values):
    high = values.astype(bf16)
    return high, (values - high.astype(f32)).astype(bf16)


def dot(a, b):
    return jnp.dot(a, b, preferred_element_type=f32)


def dot_nt(a, b):
    return lax.dot_general(a, b, (((1,), (1,)), ((), ())), preferred_element_type=f32)


def dot3(a, b):
    return dot(jnp.concatenate([a[0], a[0], a[1]], 1), jnp.concatenate([b[0], b[1], b[0]], 0))


def interleave(parts):
    while parts:
        parts = [part for part in parts if next(part, 0) is None]


def cubic_weights(t):
    return (
        ((-0.5 * t + 1.0) * t - 0.5) * t,
        (1.5 * t - 2.5) * t * t + 1.0,
        ((-1.5 * t + 2.0) * t + 0.5) * t,
        (0.5 * t - 0.5) * t * t,
    )


def one_hot(hit):
    return jnp.where(hit, 1.0, 0.0).astype(bf16)


def iota(shape, dim):
    return lax.broadcasted_iota(jnp.int32, shape, dim)


def stencil_cells(base):
    shift = iota(base.shape, 1) - base
    return jnp.concatenate([one_hot(shift == a * SPAN_Y + e) for a in range(4) for e in range(4)], 0)


def same_bin(shape, group):
    return ((iota(shape, 0) ^ iota(shape, 1)) & (group - 1)) == 0


def group_slice(g, size):
    return slice(g * size, (g + 1) * size)


def twice(lanes):
    return jnp.concatenate([lanes, lanes], 1)


def spread_kernel(
    direction_hbm, offsets_hbm, cells_hbm, forward_hbm, *refs
):
    tables_hbm, (out, offsets, base, depth), tables = refs[:TABLES], refs[TABLES : TABLES + 4], refs[TABLES + 4 : 2 * TABLES + 4]
    direction, cells, forward, q_hi, q_lo, sems = refs[2 * TABLES + 4 :]
    group = SPREAD_GROUP
    copies = [
        pltpu.make_async_copy(cells_hbm, cells, sems.at[0]),
        pltpu.make_async_copy(direction_hbm, direction, sems.at[1]),
        *(pltpu.make_async_copy(offsets_hbm.at[:, d, :], offsets.at[d], sems.at[2 + d]) for d in range(3)),
        pltpu.make_async_copy(forward_hbm, forward, sems.at[5]),
        *(pltpu.make_async_copy(tables_hbm[t], tables[t], sems.at[6 + t]) for t in range(TABLES)),
    ]
    for copy in copies:
        copy.start()
    copies[0].wait()
    first = (cells[0:1, :] - lax.axis_index("px") * ROWS) * SPAN_Y + cells[1:2, :] - lax.axis_index("py") * COLUMNS
    packed = (first + 256 * cells[2:3, :]).astype(f32)
    own = iota((BINS, BINS), 0) == iota((BINS, BINS), 1)
    packed = jnp.sum(jnp.where(own, packed, 0.0), axis=1, keepdims=True).astype(jnp.int32)
    base[...] = jnp.broadcast_to(packed & 255, (BINS, 128))
    depth[...] = jnp.broadcast_to(packed >> 8, (BINS, 128))
    for copy in copies[1:5]:
        copy.wait()

    def multiplied(g):
        bins = group_slice(g, group)
        wx = cubic_weights(offsets[0, bins, :])
        wy = cubic_weights(offsets[1, bins, :])
        wz = cubic_weights(offsets[2, bins, :])
        d = direction[bins, :]
        wx = [w * d for w in wx]
        columns = jnp.concatenate(split(jnp.concatenate([x * y for x in wx for y in wy], 0)), 1)
        depths = twice(jnp.concatenate(split(jnp.concatenate(wz, 0)), 0))
        yield
        patches = dot_nt(depths, columns)
        yield
        patches = patches[: 4 * group] + patches[4 * group :]
        patches = jnp.concatenate(split(jnp.where(same_bin(patches.shape, group), patches, 0.0)), 0)
        cells = stencil_cells(twice(base[bins, :]))
        yield
        placed = dot(patches, cells)
        yield
        placed = split(placed[: 4 * group] + placed[4 * group :])
        for f in range(4):
            rows = slice((4 * (g // 2) + f) * 2 * group + g % 2 * group, (4 * (g // 2) + f) * 2 * group + (g % 2 + 1) * group)
            q_hi[rows, :] = placed[0][f * group : (f + 1) * group]
            q_lo[rows, :] = placed[1][f * group : (f + 1) * group]

    def pair(p, found):
        parts = [multiplied(2 * p), multiplied(2 * p + 1)]
        while parts:
            parts = [part for part in parts if next(part, 0) is None]
            yield
        own = cells[2:3, 2 * p * group : 2 * (p + 1) * group]
        own = jnp.concatenate([own + f - 1 for f in range(4)], 1)
        at_depth = one_hot(iota((GRID_Z, 8 * group), 0) == own)
        yield
        rows = slice(8 * p * group, 8 * (p + 1) * group)
        found.append(dot(twice(at_depth), jnp.concatenate([q_hi[rows, :], q_lo[rows, :]], 0)))
        yield

    found = []
    interleave([pair(p, found) for p in range(BINS // group // 2)])
    gridded = split(sum(found))
    copies[5].wait()
    transformed = dot3((forward[:, :GRID_Z], forward[:, GRID_Z:]), gridded)
    for part in range(2):
        for half in range(2):
            out[pl.ds(2 * part + half, GRID_Z, stride=4), :] = transformed[
                part * GRID_Z : (part + 1) * GRID_Z, half * 128 : (half + 1) * 128
            ]
    for copy in copies[6:]:
        copy.wait()


def plane_kernel(
    lengths, received, blocks, back, inner, inner_back, small, out, r_hi, r_lo, wide, m_hi, m_lo, narrow, g_hi, g_lo
):
    for j in range(4):
        lanes = slice(128 * j, 128 * (j + 1))
        r_hi[:, lanes], r_lo[:, lanes] = split(received[pl.ds(j, DEVICES, stride=4), :])
    scale_x, scale_y = lengths[0] * lengths[0], lengths[1] * lengths[1]
    frequency = lax.axis_index("px") * N_PY + lax.axis_index("py")
    sine = jnp.sum(jnp.where(iota((1, GRID_Z), 1) == frequency, small[201:202, :], 0.0), axis=1, keepdims=True)
    rest = 1.0 + lengths[2] * lengths[2] * sine
    factor = 2.0 * lengths[0] * lengths[1] * lengths[2]
    ty_re, ty_im = small[0:16, :], small[16:32, :]
    rest_y = [rest + scale_y * small[32:48, 128 * part : 128 * (part + 1)] for part in range(2)]
    def chunk(c):
        left = (blocks[c, :, :DEVICES], blocks[c, :, DEVICES:])
        wide[c] = dot3(left, (r_hi[...], r_lo[...]))
        yield
        spans = []
        for j in range(PER_CHUNK):
            kx = c * PER_CHUNK + j
            top = slice(j * BLOCK_Y, (j + 1) * BLOCK_Y)
            bottom = slice(CHUNK + j * BLOCK_Y, CHUNK + (j + 1) * BLOCK_Y)
            tx_re, tx_im = small[48 + kx : 49 + kx, :], small[88 + kx : 89 + kx, :]
            spans.append((kx, top, bottom, tx_re * ty_re - tx_im * ty_im, tx_re * ty_im + tx_im * ty_re))
        for kx, top, bottom, tr, ti in spans:
            cre, cim = wide[c, top, :CELLS], wide[c, top, CELLS:]
            sre, sim = wide[c, bottom, :CELLS], wide[c, bottom, CELLS:]
            ur, ui, vr, vi = cre + sim, cim - sre, cre - sim, cim + sre
            for rows, re, im in (
                (top, ur * tr - ui * ti, ur * ti + ui * tr),
                (bottom, vr * tr + vi * ti, vi * tr - vr * ti),
            ):
                m_hi[c, rows, :CELLS], m_lo[c, rows, :CELLS] = split(re)
                m_hi[c, rows, CELLS:], m_lo[c, rows, CELLS:] = split(im)
        yield
        narrow[c] = dot3((m_hi[c], m_lo[c]), (inner[:, :CELLS], inner[:, CELLS:]))
        yield
        for kx, top, bottom, tr, ti in spans:
            for part, rows in enumerate((top, bottom)):
                lanes = slice(128 * part, 128 * (part + 1))
                denominator = rest_y[part] + scale_x * small[128 + kx : 129 + kx, lanes]
                weight = factor * (1.0 / (M_X * M_Y)) if part == 0 else factor * small[168 + kx : 169 + kx, :128]
                spectrum = twice(weight / (denominator * denominator))
                g_hi[c, rows, :], g_lo[c, rows, :] = split(narrow[c, rows, :] * spectrum)
        yield
        wide[c] = dot3((g_hi[c], g_lo[c]), (inner_back[:, : 2 * CELLS], inner_back[:, 2 * CELLS :]))
        yield
        for kx, top, bottom, tr, ti in spans:
            zr, zi = wide[c, top, :CELLS], wide[c, top, CELLS:]
            yr, yi = wide[c, bottom, :CELLS], wide[c, bottom, CELLS:]
            ar, ai = zr * tr + zi * ti, zi * tr - zr * ti
            br, bi = yr * tr - yi * ti, yr * ti + yi * tr
            for rows, re, im in ((top, ar + br, ai + bi), (bottom, bi - ai, ar - br)):
                m_hi[c, rows, :CELLS], m_lo[c, rows, :CELLS] = split(re)
                m_hi[c, rows, CELLS:], m_lo[c, rows, CELLS:] = split(im)
        yield
        left = (back[c, :, : 2 * CHUNK], back[c, :, BACK : BACK + 2 * CHUNK])
        totals.append(dot3(left, (m_hi[c], m_lo[c])))
    totals = []
    interleave([chunk(c) for c in range(CHUNKS)])
    total = sum(totals)
    for j in range(4):
        out[pl.ds(j, DEVICES, stride=4), :] = total[:, 128 * j : 128 * (j + 1)]


def gather_kernel(received, direction, residual, noise, offsets, base, depth, inverse, image, sums, v_hi, v_lo):
    group = READ_GROUP
    for part in range(2):
        for half in range(2):
            rows = slice(part * GRID_Z, (part + 1) * GRID_Z)
            lanes = slice(half * 128, (half + 1) * 128)
            v_hi[rows, lanes], v_lo[rows, lanes] = split(received[pl.ds(2 * part + half, GRID_Z, stride=4), :])
    grid = split(dot3((inverse[:, : 2 * GRID_Z], inverse[:, 2 * GRID_Z :]), (v_hi[...], v_lo[...])))
    v_hi[:GRID_Z, :], v_lo[:GRID_Z, :] = grid

    def step(g, found):
        bins = group_slice(g, group)
        shift = iota((group, GRID_Z), 1) - twice(depth[bins, :])
        at_depth = jnp.concatenate([one_hot(shift == f - 1) for f in range(4)], 0)
        yield
        lines = [dot(at_depth, v[:GRID_Z, :]).astype(bf16) for v in (v_hi, v_lo)]
        lines = jnp.concatenate(lines, 0)
        cells = stencil_cells(twice(base[bins, :]))
        yield
        read = dot_nt(cells, lines)
        yield
        read = jnp.where(same_bin(read.shape, group), read, 0.0).astype(bf16)
        depths = jnp.concatenate(split(jnp.concatenate(cubic_weights(offsets[2, bins, :]), 0)), 1)
        depths = jnp.concatenate([depths, depths], 0)
        yield
        along = dot(read, depths)
        yield
        along = along[:, :BIN] + along[:, BIN:]
        wx = cubic_weights(offsets[0, bins, :])
        wy = cubic_weights(offsets[1, bins, :])
        value = 0.0
        for a in range(4):
            row = 0.0
            for e in range(4):
                start = (4 * a + e) * group
                row = row + wy[e] * along[start : start + group]
            value = value + wx[a] * row
        d, r = direction[bins, :], residual[bins, :]
        value = value + noise[bins, :] * d
        image[bins, :] = value
        found.append([(x * y).reshape(group // 8, 8, BIN).sum(0) for x, y in ((r, r), (d, value), (r, value), (value, value))])

    found = []
    interleave([step(g, found) for g in range(BINS // group)])
    totals = [sum(parts) for parts in zip(*found)]
    lane = iota((1, BIN), 1)
    row = jnp.zeros((1, BIN), f32)
    for j, part in enumerate(totals):
        row = jnp.where(lane == j, jnp.sum(part, keepdims=True), row)
    sums[...] = jnp.broadcast_to(row, (DEVICES, BIN))


def step_kernel(sums, iterate, residual, direction, image, new_iterate, new_residual, new_direction):
    row = jnp.sum(sums[...], axis=0, keepdims=True)
    old_norm, curvature, cross, square = (row[:, j : j + 1] for j in range(4))
    step = old_norm / curvature
    new_norm = old_norm - 2.0 * step * cross + step * step * square
    d = direction[...]
    r = residual[...] - step * image[...]
    new_iterate[...] = iterate[...] + step * d
    new_residual[...] = r
    new_direction[...] = r + (new_norm / old_norm) * d


VMEM = pl.BlockSpec(memory_space=pltpu.VMEM)
HBM = pl.BlockSpec(memory_space=pltpu.HBM)
SMEM = pl.BlockSpec(memory_space=pltpu.SMEM)


def params():
    return pltpu.CompilerParams(vmem_limit_bytes=16 * 1024 * 1024)


def on_device(solution, residual, direction, offsets, noise, bin_cells, lengths):
    forward, inverse = depth_tables()
    d, r = direction.reshape(BINS, BIN), residual.reshape(BINS, BIN)
    point = jax.ShapeDtypeStruct((BINS, BIN), f32)
    index = jax.ShapeDtypeStruct((BINS, BIN), jnp.int32)
    block = jax.ShapeDtypeStruct((4 * DEVICES, 128), f32)

    tables = plane_tables()
    by_tile = offsets.reshape(3, BINS, BIN).transpose(1, 0, 2)
    operands = [pltpu.with_memory_space_constraint(x, pltpu.HBM) for x in (d, by_tile, bin_cells, forward, *tables)]

    blocks, by_bin, base, depth, *tables = pl.pallas_call(
        spread_kernel,
        out_shape=(
            block, jax.ShapeDtypeStruct((3, BINS, BIN), f32), index, index,
            *(jax.ShapeDtypeStruct(t.shape, t.dtype) for t in tables),
        ),
        in_specs=[HBM] * len(operands),
        out_specs=(VMEM,) * (4 + TABLES),
        scratch_shapes=[
            pltpu.VMEM((BINS, BIN), f32),
            pltpu.VMEM((3, BINS), jnp.int32),
            pltpu.VMEM(forward.shape, bf16),
            pltpu.VMEM((4 * BINS, CELLS), bf16),
            pltpu.VMEM((4 * BINS, CELLS), bf16),
            pltpu.SemaphoreType.DMA((6 + TABLES,)),
        ],
        compiler_params=params(),
        name="spread",
    )(*operands)
    received = lax.all_to_all(blocks.reshape(DEVICES, 4, 128), ("px", "py"), 0, 0, tiled=True)

    filtered = pl.pallas_call(
        plane_kernel,
        out_shape=block,
        in_specs=[SMEM] + [VMEM] * 6,
        out_specs=VMEM,
        scratch_shapes=[
            pltpu.VMEM((DEVICES, 512), bf16),
            pltpu.VMEM((DEVICES, 512), bf16),
            pltpu.VMEM((CHUNKS, 2 * CHUNK, 512), f32),
            pltpu.VMEM((CHUNKS, 2 * CHUNK, 512), bf16),
            pltpu.VMEM((CHUNKS, 2 * CHUNK, 512), bf16),
            pltpu.VMEM((CHUNKS, 2 * CHUNK, 256), f32),
            pltpu.VMEM((CHUNKS, 2 * CHUNK, 256), bf16),
            pltpu.VMEM((CHUNKS, 2 * CHUNK, 256), bf16),
        ],
        compiler_params=params(),
        name="plane",
    )(lengths, received.reshape(4 * DEVICES, 128), *tables)
    returned = lax.all_to_all(filtered.reshape(DEVICES, 4, 128), ("px", "py"), 0, 0, tiled=True)

    image, sums = pl.pallas_call(
        gather_kernel,
        out_shape=(point, jax.ShapeDtypeStruct((DEVICES, BIN), f32)),
        in_specs=[VMEM] * 8,
        out_specs=(VMEM, VMEM),
        scratch_shapes=[pltpu.VMEM((2 * GRID_Z, CELLS), bf16)] * 2,
        compiler_params=params(),
        name="interpolate",
    )(returned.reshape(4 * DEVICES, 128), d, r, noise.reshape(BINS, BIN), by_bin, base, depth, inverse)

    everywhere = lax.all_to_all(sums.reshape(DEVICES, 1, BIN), ("px", "py"), 0, 0, tiled=True)
    outs = pl.pallas_call(
        step_kernel,
        out_shape=(point,) * 3,
        in_specs=[VMEM] * 5,
        out_specs=(VMEM,) * 3,
        compiler_params=params(),
        name="step",
    )(everywhere.reshape(DEVICES, BIN), solution.reshape(BINS, BIN), r, d, image)
    return tuple(out.reshape(1, -1) for out in outs)


def solution(mesh):
    points = P(None, ("px", "py"))
    return jax.shard_map(
        on_device,
        mesh=mesh,
        in_specs=(points, points, points, points, P(("px", "py")), points, P()),
        out_specs=(points, points, points),
        check_vma=False,
    )
```

```python
import jax
import jax.numpy as jnp
import ml_dtypes
import numpy as np
from jax import lax
from jax.experimental import pallas as pl
from jax.experimental.pallas import tpu as pltpu
from jax.sharding import PartitionSpec as P

GRID_X, GRID_Y, GRID_Z = 128, 256, 256
BIN = 128
N_PX, N_PY = 32, 8
DEVICES = N_PX * N_PY
ROWS, COLUMNS = GRID_X // N_PX, GRID_Y // N_PY
SPAN_X, SPAN_Y = ROWS + 3, COLUMNS + 3
CELLS, OWN, RIM = 256, 128, 64
M_X, M_Y, M_Z = 2 * GRID_X, 2 * GRID_Y, 2 * GRID_Z - 1
BINS = 256
SPREAD_GROUP, READ_GROUP = 32, 32
TABLES = 7
SLOTS = (1, 2, 3, 4, 5, 6, 0)

f32, bf16 = jnp.float32, jnp.bfloat16


def halves(table):
    table = np.asarray(table, np.float64)
    high = table.astype(np.float32).astype(ml_dtypes.bfloat16)
    low = (table - high.astype(np.float64)).astype(np.float32).astype(ml_dtypes.bfloat16)
    return np.concatenate([high, low], -1)


def depth_tables():
    freq = np.arange(GRID_Z)[:, None]
    depth = np.arange(GRID_Z)[None, :]
    angle = 2 * np.pi * (freq * depth % M_Z) / M_Z
    forward = np.concatenate([np.cos(angle), -np.sin(angle)], 0)
    doubled = np.where(freq == 0, 1.0, 2.0) / M_Z
    inverse = np.concatenate([np.cos(angle) * doubled, -np.sin(angle) * doubled], 0).T
    return halves(forward), halves(inverse)


def cas(product, length):
    angle = 2 * np.pi * (product % length) / length
    return np.cos(angle) + np.sin(angle)


def plane_tables():
    kx, ky = np.arange(M_X), np.arange(M_Y)
    px = np.arange(N_PX)
    x = np.concatenate([ROWS * px + slot - 1 for slot in SLOTS])
    along_x = np.zeros((M_X, DEVICES))
    along_x[:, : len(x)] = cas(kx[:, None] * x[None, :], M_X)
    along_y = cas(np.arange(GRID_Y)[:, None] * ky[None, :], M_Y)
    sine_x = np.sin(np.pi * kx / M_X) ** 2
    sines = np.zeros((8, M_Y), np.float32)
    sines[0] = np.sin(np.pi * ky / M_Y) ** 2
    sines[1, :GRID_Z] = np.sin(np.pi * np.arange(GRID_Z) / M_Z) ** 2
    rim = np.zeros((OWN, CELLS), np.float32)
    for row in range(SPAN_X):
        start = {0: OWN + 96, 5: OWN, 6: OWN + 32}.get(row, (row - 1) * COLUMNS)
        for q, column in enumerate((COLUMNS - 1, 0, 1)):
            rim[RIM + 3 * row + q, start + column] = 1.0
    return (
        halves(along_x),
        halves(along_x.T),
        halves(along_y),
        halves(along_y.T),
        np.repeat(sine_x[:, None], 128, 1).astype(np.float32),
        sines,
        rim.astype(ml_dtypes.bfloat16),
    )


def split(values):
    high = values.astype(bf16)
    return high, (values - high.astype(f32)).astype(bf16)


def dot(a, b):
    return jnp.dot(a, b, preferred_element_type=f32)


def dot_nt(a, b):
    return lax.dot_general(a, b, (((1,), (1,)), ((), ())), preferred_element_type=f32)


def dot3(a, b):
    return dot(jnp.concatenate([a[0], a[0], a[1]], 1), jnp.concatenate([b[0], b[1], b[0]], 0))


def interleave(parts):
    while parts:
        parts = [part for part in parts if next(part, 0) is None]


def cubic_weights(t):
    return (
        ((-0.5 * t + 1.0) * t - 0.5) * t,
        (1.5 * t - 2.5) * t * t + 1.0,
        ((-1.5 * t + 2.0) * t + 0.5) * t,
        (0.5 * t - 0.5) * t * t,
    )


def one_hot(hit):
    return jnp.where(hit, 1.0, 0.0).astype(bf16)


def iota(shape, dim):
    return lax.broadcasted_iota(jnp.int32, shape, dim)


def cell_index():
    lane = iota((1, CELLS), 1)
    place, part = lane & 127, (lane & 127) >> 5
    row = jnp.where(lane < OWN, part + 1, jnp.where(part == 3, 0, part + 5))
    rim = place - RIM
    rim_row = (rim * 11) >> 5
    q = rim - 3 * rim_row
    rim_column = jnp.where(q == 0, 0, q + COLUMNS)
    rim_cell = jnp.where(rim < 3 * SPAN_X, rim_row * SPAN_Y + rim_column, -(1 << 20))
    return jnp.where((lane >= OWN) & (part == 2), rim_cell, row * SPAN_Y + (lane & 31) + 1)


def stencil_cells(base):
    shift = cell_index() - base
    return jnp.concatenate([one_hot(shift == a * SPAN_Y + e) for a in range(4) for e in range(4)], 0)


def same_bin(shape, group):
    return ((iota(shape, 0) ^ iota(shape, 1)) & (group - 1)) == 0


def group_slice(g, size):
    return slice(g * size, (g + 1) * size)


def twice(lanes):
    return jnp.concatenate([lanes, lanes], 1)


def spread_kernel(
    direction_hbm, offsets_hbm, cells_hbm, forward_hbm, *refs
):
    tables_hbm, (out, offsets, base, depth), tables = refs[:TABLES], refs[TABLES : TABLES + 4], refs[TABLES + 4 : 2 * TABLES + 4]
    direction, cells, forward, q_hi, q_lo, sems = refs[2 * TABLES + 4 :]
    group = SPREAD_GROUP
    copies = [
        pltpu.make_async_copy(cells_hbm, cells, sems.at[0]),
        pltpu.make_async_copy(direction_hbm, direction, sems.at[1]),
        *(pltpu.make_async_copy(offsets_hbm.at[:, d, :], offsets.at[d], sems.at[2 + d]) for d in range(3)),
        pltpu.make_async_copy(forward_hbm, forward, sems.at[5]),
        *(pltpu.make_async_copy(tables_hbm[t], tables[t], sems.at[6 + t]) for t in range(TABLES)),
    ]
    for copy in copies:
        copy.start()
    copies[0].wait()
    first = (cells[0:1, :] - lax.axis_index("px") * ROWS) * SPAN_Y + cells[1:2, :] - lax.axis_index("py") * COLUMNS
    packed = (first + 256 * cells[2:3, :]).astype(f32)
    own = iota((BINS, BINS), 0) == iota((BINS, BINS), 1)
    packed = jnp.sum(jnp.where(own, packed, 0.0), axis=1, keepdims=True).astype(jnp.int32)
    base[...] = jnp.broadcast_to(packed & 255, (BINS, 128))
    depth[...] = jnp.broadcast_to(packed >> 8, (BINS, 128))
    for copy in copies[1:5]:
        copy.wait()

    def multiplied(g):
        bins = group_slice(g, group)
        wx = cubic_weights(offsets[0, bins, :])
        wy = cubic_weights(offsets[1, bins, :])
        wz = cubic_weights(offsets[2, bins, :])
        d = direction[bins, :]
        wx = [w * d for w in wx]
        columns = jnp.concatenate(split(jnp.concatenate([x * y for x in wx for y in wy], 0)), 1)
        depths = twice(jnp.concatenate(split(jnp.concatenate(wz, 0)), 0))
        yield
        patches = dot_nt(depths, columns)
        yield
        patches = patches[: 4 * group] + patches[4 * group :]
        patches = jnp.concatenate(split(jnp.where(same_bin(patches.shape, group), patches, 0.0)), 0)
        cells = stencil_cells(twice(base[bins, :]))
        yield
        placed = dot(patches, cells)
        yield
        placed = split(placed[: 4 * group] + placed[4 * group :])
        for f in range(4):
            rows = slice((4 * (g // 2) + f) * 2 * group + g % 2 * group, (4 * (g // 2) + f) * 2 * group + (g % 2 + 1) * group)
            q_hi[rows, :] = placed[0][f * group : (f + 1) * group]
            q_lo[rows, :] = placed[1][f * group : (f + 1) * group]

    def pair(p, found):
        parts = [multiplied(2 * p), multiplied(2 * p + 1)]
        while parts:
            parts = [part for part in parts if next(part, 0) is None]
            yield
        own = cells[2:3, 2 * p * group : 2 * (p + 1) * group]
        own = jnp.concatenate([own + f - 1 for f in range(4)], 1)
        at_depth = one_hot(iota((GRID_Z, 8 * group), 0) == own)
        yield
        rows = slice(8 * p * group, 8 * (p + 1) * group)
        found.append(dot(twice(at_depth), jnp.concatenate([q_hi[rows, :], q_lo[rows, :]], 0)))
        yield

    found = []
    interleave([pair(p, found) for p in range(BINS // group // 2)])
    gridded = split(sum(found))
    copies[5].wait()
    transformed = dot3((forward[:, :GRID_Z], forward[:, GRID_Z:]), gridded)
    for part in range(2):
        for half in range(2):
            out[pl.ds(2 * part + half, GRID_Z, stride=4), :] = transformed[
                part * GRID_Z : (part + 1) * GRID_Z, half * 128 : (half + 1) * 128
            ]
    for copy in copies[6:]:
        copy.wait()


def moved(values, rows):
    return pltpu.roll(values, rows % DEVICES, 0)


def turned(values, lanes):
    return pltpu.roll(values, lanes % 128, 1) if lanes % 128 else values


def by_quarter(pieces):
    quarter = iota(pieces[0].shape, 1) >> 5
    result = 0.0
    for q, piece in enumerate(pieces):
        if piece is not None:
            result = jnp.where(quarter == q, piece, result)
    return result


def plane_kernel(
    lengths, received, along_x, back_x, along_y, back_y, sine_x, sines, rim, out, tiles, x_hi, x_lo, spectrum
):
    last_column = (iota((DEVICES, CELLS), 1) & 31) == COLUMNS - 1
    quarter = iota((DEVICES, OWN), 1) >> 5
    place = ((0, 0), (0, 1), (0, 2), (0, 3), (1, 0), (1, 1), (1, 3))

    def filtering():
        yield
        scale_x, scale_y = lengths[0] * lengths[0], lengths[1] * lengths[1]
        frequency = lax.axis_index("px") * N_PY + lax.axis_index("py")
        sine = jnp.where(iota((1, GRID_Z), 1) == frequency, sines[1:2, :GRID_Z], 0.0)
        rest = 1.0 + lengths[2] * lengths[2] * jnp.sum(sine, axis=1, keepdims=True)
        factor = 2.0 / (M_X * M_Y) * lengths[0] * lengths[1] * lengths[2]
        rows = rest + scale_x * sine_x[...]
        for j in range(M_Y // 128):
            lanes = slice(128 * j, 128 * (j + 1))
            denominator = rows + scale_y * sines[0:1, lanes]
            spectrum[:, lanes] = factor / (denominator * denominator)

    def plane(part):
        own, rest = (received[pl.ds(2 * part + half, DEVICES, stride=4), :] for half in range(2))
        rims = dot(jnp.concatenate(split(rest), 0), rim[...])
        yield
        columns = rims[:DEVICES] + rims[DEVICES:]
        columns = jnp.where(last_column, moved(columns, -1), moved(columns, 1))
        tiles[part, 0] = own + columns[:, :OWN]
        tiles[part, 1] = jnp.where(quarter == 2, 0.0, rest) + columns[:, OWN:]
        loaded = [[tiles[part, tile, pl.ds(py, N_PX, stride=N_PY), :] for py in range(N_PY)] for tile in range(2)]
        for slot, (tile, q) in enumerate(place):
            rows = slice(slot * N_PX, (slot + 1) * N_PX)
            for half in range(2):
                lanes = slice(128 * half, 128 * (half + 1))
                values = by_quarter([turned(loaded[tile][4 * half + p], 32 * (p - q)) for p in range(4)])
                x_hi[part, rows, lanes], x_lo[part, rows, lanes] = split(values)
        empty = slice(len(place) * N_PX, DEVICES)
        x_hi[part, empty, :] = jnp.zeros((N_PX, GRID_Y), bf16)
        x_lo[part, empty, :] = jnp.zeros((N_PX, GRID_Y), bf16)
        yield
        values = dot3((along_x[:, :DEVICES], along_x[:, DEVICES:]), (x_hi[part], x_lo[part]))
        yield
        values = split(values)
        yield
        values = dot3(values, (along_y[:, :M_Y], along_y[:, M_Y:]))
        yield
        values = split(values * spectrum[...])
        yield
        values = dot3(values, (back_y[:, :GRID_Y], back_y[:, GRID_Y:]))
        yield
        values = split(values)
        yield
        values = dot3((back_x[:, :M_X], back_x[:, M_X:]), values)
        yield
        for py in range(N_PY):
            lanes = slice(128 * (py // 4), 128 * (py // 4 + 1))
            pieces = [[None] * 4, [None] * 4]
            for slot, (tile, q) in enumerate(place):
                pieces[tile][q] = turned(values[slot * N_PX : (slot + 1) * N_PX, lanes], 32 * (q - py % 4))
            for tile in range(2):
                tiles[part, tile, pl.ds(py, N_PX, stride=N_PY), :] = by_quarter(pieces[tile])
        own, rest = tiles[part, 0], tiles[part, 1]
        out[pl.ds(2 * part, DEVICES, stride=4), :] = own
        region = jnp.concatenate([own, rest], 1)
        region = jnp.concatenate(split(jnp.where(last_column, moved(region, 1), moved(region, -1))), 0)
        yield
        rims = dot_nt(region, rim[...])
        yield
        out[pl.ds(2 * part + 1, DEVICES, stride=4), :] = rest + rims[:DEVICES] + rims[DEVICES:]

    interleave([plane(0), plane(1), filtering()])


def gather_kernel(received, direction, residual, noise, offsets, base, depth, inverse, image, sums, v_hi, v_lo):
    group = READ_GROUP
    for part in range(2):
        for half in range(2):
            rows = slice(part * GRID_Z, (part + 1) * GRID_Z)
            lanes = slice(half * 128, (half + 1) * 128)
            v_hi[rows, lanes], v_lo[rows, lanes] = split(received[pl.ds(2 * part + half, GRID_Z, stride=4), :])
    grid = split(dot3((inverse[:, : 2 * GRID_Z], inverse[:, 2 * GRID_Z :]), (v_hi[...], v_lo[...])))
    v_hi[:GRID_Z, :], v_lo[:GRID_Z, :] = grid

    def step(g, found):
        bins = group_slice(g, group)
        shift = iota((group, GRID_Z), 1) - twice(depth[bins, :])
        at_depth = jnp.concatenate([one_hot(shift == f - 1) for f in range(4)], 0)
        yield
        lines = [dot(at_depth, v[:GRID_Z, :]).astype(bf16) for v in (v_hi, v_lo)]
        lines = jnp.concatenate(lines, 0)
        cells = stencil_cells(twice(base[bins, :]))
        yield
        read = dot_nt(cells, lines)
        yield
        read = jnp.where(same_bin(read.shape, group), read, 0.0).astype(bf16)
        depths = jnp.concatenate(split(jnp.concatenate(cubic_weights(offsets[2, bins, :]), 0)), 1)
        depths = jnp.concatenate([depths, depths], 0)
        yield
        along = dot(read, depths)
        yield
        along = along[:, :BIN] + along[:, BIN:]
        wx = cubic_weights(offsets[0, bins, :])
        wy = cubic_weights(offsets[1, bins, :])
        value = 0.0
        for a in range(4):
            row = 0.0
            for e in range(4):
                start = (4 * a + e) * group
                row = row + wy[e] * along[start : start + group]
            value = value + wx[a] * row
        d, r = direction[bins, :], residual[bins, :]
        value = value + noise[bins, :] * d
        image[bins, :] = value
        found.append([(x * y).reshape(group // 8, 8, BIN).sum(0) for x, y in ((r, r), (d, value), (r, value), (value, value))])

    found = []
    interleave([step(g, found) for g in range(BINS // group)])
    totals = [sum(parts) for parts in zip(*found)]
    lane = iota((1, BIN), 1)
    row = jnp.zeros((1, BIN), f32)
    for j, part in enumerate(totals):
        row = jnp.where(lane == j, jnp.sum(part, keepdims=True), row)
    sums[...] = jnp.broadcast_to(row, (DEVICES, BIN))


def step_kernel(sums, iterate, residual, direction, image, new_iterate, new_residual, new_direction):
    row = jnp.sum(sums[...], axis=0, keepdims=True)
    old_norm, curvature, cross, square = (row[:, j : j + 1] for j in range(4))
    step = old_norm / curvature
    new_norm = old_norm - 2.0 * step * cross + step * step * square
    d = direction[...]
    r = residual[...] - step * image[...]
    new_iterate[...] = iterate[...] + step * d
    new_residual[...] = r
    new_direction[...] = r + (new_norm / old_norm) * d


VMEM = pl.BlockSpec(memory_space=pltpu.VMEM)
HBM = pl.BlockSpec(memory_space=pltpu.HBM)
SMEM = pl.BlockSpec(memory_space=pltpu.SMEM)


def params():
    return pltpu.CompilerParams(vmem_limit_bytes=16 * 1024 * 1024)


def filter_plane(lengths, received, tables):
    return pl.pallas_call(
        plane_kernel,
        out_shape=jax.ShapeDtypeStruct((4 * DEVICES, 128), f32),
        in_specs=[SMEM] + [VMEM] * (1 + TABLES),
        out_specs=VMEM,
        scratch_shapes=[
            pltpu.VMEM((2, 2, DEVICES, OWN), f32),
            pltpu.VMEM((2, DEVICES, GRID_Y), bf16),
            pltpu.VMEM((2, DEVICES, GRID_Y), bf16),
            pltpu.VMEM((M_X, M_Y), f32),
        ],
        compiler_params=params(),
        name="plane",
    )(lengths, received, *tables)


def on_device(solution, residual, direction, offsets, noise, bin_cells, lengths):
    forward, inverse = depth_tables()
    d, r = direction.reshape(BINS, BIN), residual.reshape(BINS, BIN)
    point = jax.ShapeDtypeStruct((BINS, BIN), f32)
    index = jax.ShapeDtypeStruct((BINS, BIN), jnp.int32)
    block = jax.ShapeDtypeStruct((4 * DEVICES, 128), f32)

    tables = plane_tables()
    by_tile = offsets.reshape(3, BINS, BIN).transpose(1, 0, 2)
    operands = [pltpu.with_memory_space_constraint(x, pltpu.HBM) for x in (d, by_tile, bin_cells, forward, *tables)]

    blocks, by_bin, base, depth, *tables = pl.pallas_call(
        spread_kernel,
        out_shape=(
            block, jax.ShapeDtypeStruct((3, BINS, BIN), f32), index, index,
            *(jax.ShapeDtypeStruct(t.shape, t.dtype) for t in tables),
        ),
        in_specs=[HBM] * len(operands),
        out_specs=(VMEM,) * (4 + TABLES),
        scratch_shapes=[
            pltpu.VMEM((BINS, BIN), f32),
            pltpu.VMEM((3, BINS), jnp.int32),
            pltpu.VMEM(forward.shape, bf16),
            pltpu.VMEM((4 * BINS, CELLS), bf16),
            pltpu.VMEM((4 * BINS, CELLS), bf16),
            pltpu.SemaphoreType.DMA((6 + TABLES,)),
        ],
        compiler_params=params(),
        name="spread",
    )(*operands)
    received = lax.all_to_all(blocks.reshape(DEVICES, 4, 128), ("px", "py"), 0, 0, tiled=True)

    filtered = filter_plane(lengths, received.reshape(4 * DEVICES, 128), tables)
    returned = lax.all_to_all(filtered.reshape(DEVICES, 4, 128), ("px", "py"), 0, 0, tiled=True)

    image, sums = pl.pallas_call(
        gather_kernel,
        out_shape=(point, jax.ShapeDtypeStruct((DEVICES, BIN), f32)),
        in_specs=[VMEM] * 8,
        out_specs=(VMEM, VMEM),
        scratch_shapes=[pltpu.VMEM((2 * GRID_Z, CELLS), bf16)] * 2,
        compiler_params=params(),
        name="interpolate",
    )(returned.reshape(4 * DEVICES, 128), d, r, noise.reshape(BINS, BIN), by_bin, base, depth, inverse)

    everywhere = lax.all_to_all(sums.reshape(DEVICES, 1, BIN), ("px", "py"), 0, 0, tiled=True)
    outs = pl.pallas_call(
        step_kernel,
        out_shape=(point,) * 3,
        in_specs=[VMEM] * 5,
        out_specs=(VMEM,) * 3,
        compiler_params=params(),
        name="step",
    )(everywhere.reshape(DEVICES, BIN), solution.reshape(BINS, BIN), r, d, image)
    return tuple(out.reshape(1, -1) for out in outs)


def solution(mesh):
    points = P(None, ("px", "py"))
    return jax.shard_map(
        on_device,
        mesh=mesh,
        in_specs=(points, points, points, points, P(("px", "py")), points, P()),
        out_specs=(points, points, points),
        check_vma=False,
    )
```

```python
import jax
import jax.numpy as jnp
import ml_dtypes
import numpy as np
from jax import lax
from jax.experimental import pallas as pl
from jax.experimental.pallas import tpu as pltpu
from jax.sharding import PartitionSpec as P

GRID_X, GRID_Y, GRID_Z = 128, 256, 256
BIN = 128
N_PX, N_PY = 32, 8
DEVICES = N_PX * N_PY
ROWS, COLUMNS = GRID_X // N_PX, GRID_Y // N_PY
SPAN_X, SPAN_Y = ROWS + 3, COLUMNS + 3
CELLS, OWN, RIM = 256, 128, 64
M_X, M_Y, M_Z = 2 * GRID_X, 2 * GRID_Y, 2 * GRID_Z - 1
BINS = 256
SPREAD_GROUP, READ_GROUP = 32, 32
TABLES = 8
SLOTS = (1, 2, 3, 4, 5, 6, 0)

f32, bf16 = jnp.float32, jnp.bfloat16


def halves(table):
    table = np.asarray(table, np.float64)
    high = table.astype(np.float32).astype(ml_dtypes.bfloat16)
    low = (table - high.astype(np.float64)).astype(np.float32).astype(ml_dtypes.bfloat16)
    return np.concatenate([high, low], -1)


def depth_tables():
    freq = np.arange(GRID_Z)[:, None]
    depth = np.arange(GRID_Z)[None, :]
    angle = 2 * np.pi * (freq * depth % M_Z) / M_Z
    forward = np.concatenate([np.cos(angle), -np.sin(angle)], 0)
    doubled = np.where(freq == 0, 1.0, 2.0) / M_Z
    inverse = np.concatenate([np.cos(angle) * doubled, -np.sin(angle) * doubled], 0).T
    return halves(forward), halves(inverse)


def cas(product, length):
    angle = 2 * np.pi * (product % length) / length
    return np.cos(angle) + np.sin(angle)


def plane_tables():
    kx, ky = np.arange(M_X), np.arange(M_Y)
    px = np.arange(N_PX)
    x = np.concatenate([ROWS * px + slot - 1 for slot in SLOTS])
    along_x = np.zeros((M_X, DEVICES))
    along_x[:, : len(x)] = cas(kx[:, None] * x[None, :], M_X)
    along_y = cas(np.arange(GRID_Y)[:, None] * ky[None, :], M_Y)
    sine_x = np.sin(np.pi * kx / M_X) ** 2
    sines = np.zeros((8, M_Y), np.float32)
    sines[0] = np.sin(np.pi * ky / M_Y) ** 2
    sines[1, :GRID_Z] = np.sin(np.pi * np.arange(GRID_Z) / M_Z) ** 2
    rim = np.zeros((OWN, CELLS), np.float32)
    for row in range(SPAN_X):
        start = {0: OWN + 96, 5: OWN, 6: OWN + 32}.get(row, (row - 1) * COLUMNS)
        for q, column in enumerate((COLUMNS - 1, 0, 1)):
            rim[RIM + 3 * row + q, start + column] = 1.0
    return (
        halves(along_x),
        halves(along_x.T),
        halves(along_y),
        halves(along_y.T),
        np.repeat(sine_x[:, None], 128, 1).astype(np.float32),
        sines,
        rim.astype(ml_dtypes.bfloat16),
    )


def split(values):
    high = values.astype(bf16)
    return high, (values - high.astype(f32)).astype(bf16)


def dot(a, b):
    return jnp.dot(a, b, preferred_element_type=f32)


def dot_nt(a, b):
    return lax.dot_general(a, b, (((1,), (1,)), ((), ())), preferred_element_type=f32)


def dot3(a, b):
    return dot(jnp.concatenate([a[0], a[0], a[1]], 1), jnp.concatenate([b[0], b[1], b[0]], 0))


def interleave(parts):
    while parts:
        parts = [part for part in parts if next(part, 0) is None]


def cubic_weights(t):
    return (
        ((-0.5 * t + 1.0) * t - 0.5) * t,
        (1.5 * t - 2.5) * t * t + 1.0,
        ((-1.5 * t + 2.0) * t + 0.5) * t,
        (0.5 * t - 0.5) * t * t,
    )


def one_hot(hit):
    return jnp.where(hit, 1.0, 0.0).astype(bf16)


def iota(shape, dim):
    return lax.broadcasted_iota(jnp.int32, shape, dim)


def cell_index():
    lane = iota((1, CELLS), 1)
    place, part = lane & 127, (lane & 127) >> 5
    row = jnp.where(lane < OWN, part + 1, jnp.where(part == 3, 0, part + 5))
    rim = place - RIM
    rim_row = (rim * 11) >> 5
    q = rim - 3 * rim_row
    rim_column = jnp.where(q == 0, 0, q + COLUMNS)
    rim_cell = jnp.where(rim < 3 * SPAN_X, rim_row * SPAN_Y + rim_column, -(1 << 20))
    return jnp.where((lane >= OWN) & (part == 2), rim_cell, row * SPAN_Y + (lane & 31) + 1)


def stencil_cells(base):
    shift = cell_index() - base
    return jnp.concatenate([one_hot(shift == a * SPAN_Y + e) for a in range(4) for e in range(4)], 0)


def same_bin(shape, group):
    return ((iota(shape, 0) ^ iota(shape, 1)) & (group - 1)) == 0


def group_slice(g, size):
    return slice(g * size, (g + 1) * size)


def twice(lanes):
    return jnp.concatenate([lanes, lanes], 1)


def spread_kernel(
    direction_hbm, offsets_hbm, cells_hbm, forward_hbm, *refs
):
    tables_hbm, (out, offsets, base, depth), tables = refs[:TABLES], refs[TABLES : TABLES + 4], refs[TABLES + 4 : 2 * TABLES + 4]
    direction, cells, forward, q_hi, q_lo, sems = refs[2 * TABLES + 4 :]
    group = SPREAD_GROUP
    copies = [
        pltpu.make_async_copy(cells_hbm, cells, sems.at[0]),
        pltpu.make_async_copy(direction_hbm, direction, sems.at[1]),
        *(pltpu.make_async_copy(offsets_hbm.at[:, d, :], offsets.at[d], sems.at[2 + d]) for d in range(3)),
        pltpu.make_async_copy(forward_hbm, forward, sems.at[5]),
        *(pltpu.make_async_copy(tables_hbm[t], tables[t], sems.at[6 + t]) for t in range(TABLES)),
    ]
    for copy in copies:
        copy.start()
    copies[0].wait()
    first = (cells[0:1, :] - lax.axis_index("px") * ROWS) * SPAN_Y + cells[1:2, :] - lax.axis_index("py") * COLUMNS
    packed = (first + 256 * cells[2:3, :]).astype(f32)
    own = iota((BINS, BINS), 0) == iota((BINS, BINS), 1)
    packed = jnp.sum(jnp.where(own, packed, 0.0), axis=1, keepdims=True).astype(jnp.int32)
    base[...] = jnp.broadcast_to(packed & 255, (BINS, 128))
    depth[...] = jnp.broadcast_to(packed >> 8, (BINS, 128))
    for copy in copies[1:5]:
        copy.wait()

    def multiplied(g):
        bins = group_slice(g, group)
        wx = cubic_weights(offsets[0, bins, :])
        wy = cubic_weights(offsets[1, bins, :])
        wz = cubic_weights(offsets[2, bins, :])
        d = direction[bins, :]
        wx = [w * d for w in wx]
        columns = jnp.concatenate(split(jnp.concatenate([x * y for x in wx for y in wy], 0)), 1)
        depths = twice(jnp.concatenate(split(jnp.concatenate(wz, 0)), 0))
        yield
        patches = dot_nt(depths, columns)
        yield
        patches = patches[: 4 * group] + patches[4 * group :]
        patches = jnp.concatenate(split(jnp.where(same_bin(patches.shape, group), patches, 0.0)), 0)
        cells = stencil_cells(twice(base[bins, :]))
        yield
        placed = dot(patches, cells)
        yield
        placed = split(placed[: 4 * group] + placed[4 * group :])
        for f in range(4):
            rows = slice((4 * (g // 2) + f) * 2 * group + g % 2 * group, (4 * (g // 2) + f) * 2 * group + (g % 2 + 1) * group)
            q_hi[rows, :] = placed[0][f * group : (f + 1) * group]
            q_lo[rows, :] = placed[1][f * group : (f + 1) * group]

    def pair(p, found):
        parts = [multiplied(2 * p), multiplied(2 * p + 1)]
        while parts:
            parts = [part for part in parts if next(part, 0) is None]
            yield
        own = cells[2:3, 2 * p * group : 2 * (p + 1) * group]
        own = jnp.concatenate([own + f - 1 for f in range(4)], 1)
        at_depth = one_hot(iota((GRID_Z, 8 * group), 0) == own)
        yield
        rows = slice(8 * p * group, 8 * (p + 1) * group)
        found.append(dot(twice(at_depth), jnp.concatenate([q_hi[rows, :], q_lo[rows, :]], 0)))
        yield

    found = []
    interleave([pair(p, found) for p in range(BINS // group // 2)])
    gridded = split(sum(found))
    copies[5].wait()
    transformed = dot3((forward[:, :GRID_Z], forward[:, GRID_Z:]), gridded)
    for part in range(2):
        for half in range(2):
            out[pl.ds(2 * part + half, GRID_Z, stride=4), :] = transformed[
                part * GRID_Z : (part + 1) * GRID_Z, half * 128 : (half + 1) * 128
            ]
    for copy in copies[6:]:
        copy.wait()


def moved(values, rows):
    return pltpu.roll(values, rows % DEVICES, 0)


def turned(values, lanes):
    return pltpu.roll(values, lanes % 128, 1) if lanes % 128 else values


def by_quarter(pieces):
    quarter = iota(pieces[0].shape, 1) >> 5
    result = 0.0
    for q, piece in enumerate(pieces):
        if piece is not None:
            result = jnp.where(quarter == q, piece, result)
    return result


def plane_kernel(
    received, along_x, back_x, along_y, back_y, sine_x, sines, rim, lengths, out, tiles, x_hi, x_lo, spectrum
):
    last_column = (iota((DEVICES, CELLS), 1) & 31) == COLUMNS - 1
    quarter = iota((DEVICES, OWN), 1) >> 5
    place = ((0, 0), (0, 1), (0, 2), (0, 3), (1, 0), (1, 1), (1, 3))

    def filtering():
        yield
        length_x, length_y, length_z = (lengths[0:1, j : j + 1] for j in range(3))
        scale_x, scale_y = length_x * length_x, length_y * length_y
        frequency = lax.axis_index("px") * N_PY + lax.axis_index("py")
        sine = jnp.where(iota((1, GRID_Z), 1) == frequency, sines[1:2, :GRID_Z], 0.0)
        rest = 1.0 + length_z * length_z * jnp.sum(sine, axis=1, keepdims=True)
        factor = 2.0 / (M_X * M_Y) * length_x * length_y * length_z
        rows = rest + scale_x * sine_x[...]
        for j in range(M_Y // 128):
            lanes = slice(128 * j, 128 * (j + 1))
            denominator = rows + scale_y * sines[0:1, lanes]
            spectrum[:, lanes] = factor / (denominator * denominator)

    def plane(part):
        own, rest = (received[pl.ds(2 * part + half, DEVICES, stride=4), :] for half in range(2))
        rims = dot(jnp.concatenate(split(rest), 0), rim[...])
        yield
        columns = rims[:DEVICES] + rims[DEVICES:]
        columns = jnp.where(last_column, moved(columns, -1), moved(columns, 1))
        tiles[part, 0] = own + columns[:, :OWN]
        tiles[part, 1] = jnp.where(quarter == 2, 0.0, rest) + columns[:, OWN:]
        loaded = [[tiles[part, tile, pl.ds(py, N_PX, stride=N_PY), :] for py in range(N_PY)] for tile in range(2)]
        for slot, (tile, q) in enumerate(place):
            rows = slice(slot * N_PX, (slot + 1) * N_PX)
            for half in range(2):
                lanes = slice(128 * half, 128 * (half + 1))
                values = by_quarter([turned(loaded[tile][4 * half + p], 32 * (p - q)) for p in range(4)])
                x_hi[part, rows, lanes], x_lo[part, rows, lanes] = split(values)
        empty = slice(len(place) * N_PX, DEVICES)
        x_hi[part, empty, :] = jnp.zeros((N_PX, GRID_Y), bf16)
        x_lo[part, empty, :] = jnp.zeros((N_PX, GRID_Y), bf16)
        yield
        values = dot3((along_x[:, :DEVICES], along_x[:, DEVICES:]), (x_hi[part], x_lo[part]))
        yield
        values = split(values)
        yield
        values = dot3(values, (along_y[:, :M_Y], along_y[:, M_Y:]))
        yield
        values = split(values * spectrum[...])
        yield
        values = dot3(values, (back_y[:, :GRID_Y], back_y[:, GRID_Y:]))
        yield
        values = split(values)
        yield
        values = dot3((back_x[:, :M_X], back_x[:, M_X:]), values)
        yield
        for py in range(N_PY):
            lanes = slice(128 * (py // 4), 128 * (py // 4 + 1))
            pieces = [[None] * 4, [None] * 4]
            for slot, (tile, q) in enumerate(place):
                pieces[tile][q] = turned(values[slot * N_PX : (slot + 1) * N_PX, lanes], 32 * (q - py % 4))
            for tile in range(2):
                tiles[part, tile, pl.ds(py, N_PX, stride=N_PY), :] = by_quarter(pieces[tile])
        own, rest = tiles[part, 0], tiles[part, 1]
        out[pl.ds(2 * part, DEVICES, stride=4), :] = own
        region = jnp.concatenate([own, rest], 1)
        region = jnp.concatenate(split(jnp.where(last_column, moved(region, 1), moved(region, -1))), 0)
        yield
        rims = dot_nt(region, rim[...])
        yield
        out[pl.ds(2 * part + 1, DEVICES, stride=4), :] = rest + rims[:DEVICES] + rims[DEVICES:]

    interleave([plane(0), plane(1), filtering()])


def gather_kernel(received, direction, residual, noise, offsets, base, depth, inverse, image, sums, v_hi, v_lo):
    group = READ_GROUP
    for part in range(2):
        for half in range(2):
            rows = slice(part * GRID_Z, (part + 1) * GRID_Z)
            lanes = slice(half * 128, (half + 1) * 128)
            v_hi[rows, lanes], v_lo[rows, lanes] = split(received[pl.ds(2 * part + half, GRID_Z, stride=4), :])
    grid = split(dot3((inverse[:, : 2 * GRID_Z], inverse[:, 2 * GRID_Z :]), (v_hi[...], v_lo[...])))
    v_hi[:GRID_Z, :], v_lo[:GRID_Z, :] = grid

    def step(g, found):
        bins = group_slice(g, group)
        shift = iota((group, GRID_Z), 1) - twice(depth[bins, :])
        at_depth = jnp.concatenate([one_hot(shift == f - 1) for f in range(4)], 0)
        yield
        lines = [dot(at_depth, v[:GRID_Z, :]).astype(bf16) for v in (v_hi, v_lo)]
        lines = jnp.concatenate(lines, 0)
        cells = stencil_cells(twice(base[bins, :]))
        yield
        read = dot_nt(cells, lines)
        yield
        read = jnp.where(same_bin(read.shape, group), read, 0.0).astype(bf16)
        depths = jnp.concatenate(split(jnp.concatenate(cubic_weights(offsets[2, bins, :]), 0)), 1)
        depths = jnp.concatenate([depths, depths], 0)
        yield
        along = dot(read, depths)
        yield
        along = along[:, :BIN] + along[:, BIN:]
        wx = cubic_weights(offsets[0, bins, :])
        wy = cubic_weights(offsets[1, bins, :])
        value = 0.0
        for a in range(4):
            row = 0.0
            for e in range(4):
                start = (4 * a + e) * group
                row = row + wy[e] * along[start : start + group]
            value = value + wx[a] * row
        d, r = direction[bins, :], residual[bins, :]
        value = value + noise[bins, :] * d
        image[bins, :] = value
        found.append([(x * y).reshape(group // 8, 8, BIN).sum(0) for x, y in ((r, r), (d, value), (r, value), (value, value))])

    found = []
    interleave([step(g, found) for g in range(BINS // group)])
    totals = [sum(parts) for parts in zip(*found)]
    lane = iota((1, BIN), 1)
    row = jnp.zeros((1, BIN), f32)
    for j, part in enumerate(totals):
        row = jnp.where(lane == j, jnp.sum(part, keepdims=True), row)
    sums[...] = jnp.broadcast_to(row, (DEVICES, BIN))


def step_kernel(sums, iterate, residual, direction, image, new_iterate, new_residual, new_direction):
    row = jnp.sum(sums[...], axis=0, keepdims=True)
    old_norm, curvature, cross, square = (row[:, j : j + 1] for j in range(4))
    step = old_norm / curvature
    new_norm = old_norm - 2.0 * step * cross + step * step * square
    d = direction[...]
    r = residual[...] - step * image[...]
    new_iterate[...] = iterate[...] + step * d
    new_residual[...] = r
    new_direction[...] = r + (new_norm / old_norm) * d


VMEM = pl.BlockSpec(memory_space=pltpu.VMEM)
HBM = pl.BlockSpec(memory_space=pltpu.HBM)


def params():
    return pltpu.CompilerParams(vmem_limit_bytes=16 * 1024 * 1024)


def filter_plane(received, tables):
    return pl.pallas_call(
        plane_kernel,
        out_shape=jax.ShapeDtypeStruct((4 * DEVICES, 128), f32),
        in_specs=[VMEM] * (1 + TABLES),
        out_specs=VMEM,
        scratch_shapes=[
            pltpu.VMEM((2, 2, DEVICES, OWN), f32),
            pltpu.VMEM((2, DEVICES, GRID_Y), bf16),
            pltpu.VMEM((2, DEVICES, GRID_Y), bf16),
            pltpu.VMEM((M_X, M_Y), f32),
        ],
        compiler_params=params(),
        name="plane",
    )(received, *tables)


def on_device(solution, residual, direction, offsets, noise, bin_cells, lengths):
    forward, inverse = depth_tables()
    d, r = direction.reshape(BINS, BIN), residual.reshape(BINS, BIN)
    point = jax.ShapeDtypeStruct((BINS, BIN), f32)
    index = jax.ShapeDtypeStruct((BINS, BIN), jnp.int32)
    block = jax.ShapeDtypeStruct((4 * DEVICES, 128), f32)

    tables = (*plane_tables(), lengths.reshape(1, 3))
    by_tile = offsets.reshape(3, BINS, BIN).transpose(1, 0, 2)
    operands = [pltpu.with_memory_space_constraint(x, pltpu.HBM) for x in (d, by_tile, bin_cells, forward, *tables)]

    blocks, by_bin, base, depth, *tables = pl.pallas_call(
        spread_kernel,
        out_shape=(
            block, jax.ShapeDtypeStruct((3, BINS, BIN), f32), index, index,
            *(jax.ShapeDtypeStruct(t.shape, t.dtype) for t in tables),
        ),
        in_specs=[HBM] * len(operands),
        out_specs=(VMEM,) * (4 + TABLES),
        scratch_shapes=[
            pltpu.VMEM((BINS, BIN), f32),
            pltpu.VMEM((3, BINS), jnp.int32),
            pltpu.VMEM(forward.shape, bf16),
            pltpu.VMEM((4 * BINS, CELLS), bf16),
            pltpu.VMEM((4 * BINS, CELLS), bf16),
            pltpu.SemaphoreType.DMA((6 + TABLES,)),
        ],
        compiler_params=params(),
        name="spread",
    )(*operands)
    received = lax.all_to_all(blocks.reshape(DEVICES, 4, 128), ("px", "py"), 0, 0, tiled=True)

    filtered = filter_plane(received.reshape(4 * DEVICES, 128), tables)
    returned = lax.all_to_all(filtered.reshape(DEVICES, 4, 128), ("px", "py"), 0, 0, tiled=True)

    image, sums = pl.pallas_call(
        gather_kernel,
        out_shape=(point, jax.ShapeDtypeStruct((DEVICES, BIN), f32)),
        in_specs=[VMEM] * 8,
        out_specs=(VMEM, VMEM),
        scratch_shapes=[pltpu.VMEM((2 * GRID_Z, CELLS), bf16)] * 2,
        compiler_params=params(),
        name="interpolate",
    )(returned.reshape(4 * DEVICES, 128), d, r, noise.reshape(BINS, BIN), by_bin, base, depth, inverse)

    everywhere = lax.all_to_all(sums.reshape(DEVICES, 1, BIN), ("px", "py"), 0, 0, tiled=True)
    outs = pl.pallas_call(
        step_kernel,
        out_shape=(point,) * 3,
        in_specs=[VMEM] * 5,
        out_specs=(VMEM,) * 3,
        compiler_params=params(),
        name="step",
    )(everywhere.reshape(DEVICES, BIN), solution.reshape(BINS, BIN), r, d, image)
    return tuple(out.reshape(1, -1) for out in outs)


def solution(mesh):
    points = P(None, ("px", "py"))
    return jax.shard_map(
        on_device,
        mesh=mesh,
        in_specs=(points, points, points, points, P(("px", "py")), points, P()),
        out_specs=(points, points, points),
        check_vma=False,
    )
```

```python
import jax
import jax.numpy as jnp
import ml_dtypes
import numpy as np
from jax import lax
from jax.experimental import pallas as pl
from jax.experimental.pallas import tpu as pltpu
from jax.sharding import PartitionSpec as P

GRID_X, GRID_Y, GRID_Z = 128, 256, 256
BIN = 128
N_PX, N_PY = 32, 8
DEVICES = N_PX * N_PY
ROWS, COLUMNS = GRID_X // N_PX, GRID_Y // N_PY
SPAN_X, SPAN_Y = ROWS + 3, COLUMNS + 3
CELLS, OWN, RIM = 256, 128, 64
M_X, M_Y, M_Z = 2 * GRID_X, 2 * GRID_Y, 2 * GRID_Z - 1
BINS = 256
SPREAD_GROUP, READ_GROUP = 16, 32
TABLES = 8
SLOTS = (1, 2, 3, 4, 5, 6, 0)

f32, bf16 = jnp.float32, jnp.bfloat16


def halves(table):
    table = np.asarray(table, np.float64)
    high = table.astype(np.float32).astype(ml_dtypes.bfloat16)
    low = (table - high.astype(np.float64)).astype(np.float32).astype(ml_dtypes.bfloat16)
    return np.concatenate([high, low], -1)


def depth_tables():
    freq = np.arange(GRID_Z)[:, None]
    depth = np.arange(GRID_Z)[None, :]
    angle = 2 * np.pi * (freq * depth % M_Z) / M_Z
    forward = np.concatenate([np.cos(angle), -np.sin(angle)], 0)
    doubled = np.where(freq == 0, 1.0, 2.0) / M_Z
    inverse = np.concatenate([np.cos(angle) * doubled, -np.sin(angle) * doubled], 0).T
    return halves(forward), halves(inverse)


def cas(product, length):
    angle = 2 * np.pi * (product % length) / length
    return np.cos(angle) + np.sin(angle)


def plane_tables():
    kx, ky = np.arange(M_X), np.arange(M_Y)
    px = np.arange(N_PX)
    x = np.concatenate([ROWS * px + slot - 1 for slot in SLOTS])
    along_x = np.zeros((M_X, DEVICES))
    along_x[:, : len(x)] = cas(kx[:, None] * x[None, :], M_X)
    along_y = cas(np.arange(GRID_Y)[:, None] * ky[None, :], M_Y)
    sine_x = np.sin(np.pi * kx / M_X) ** 2
    sines = np.zeros((8, M_Y), np.float32)
    sines[0] = np.sin(np.pi * ky / M_Y) ** 2
    sines[1, :GRID_Z] = np.sin(np.pi * np.arange(GRID_Z) / M_Z) ** 2
    rim = np.zeros((OWN, CELLS), np.float32)
    for row in range(SPAN_X):
        start = {0: OWN + 96, 5: OWN, 6: OWN + 32}.get(row, (row - 1) * COLUMNS)
        for q, column in enumerate((COLUMNS - 1, 0, 1)):
            rim[RIM + 3 * row + q, start + column] = 1.0
    return (
        halves(along_x),
        halves(along_x.T),
        halves(along_y),
        halves(along_y.T),
        np.repeat(sine_x[:, None], 128, 1).astype(np.float32),
        sines,
        rim.astype(ml_dtypes.bfloat16),
    )


def split(values):
    high = values.astype(bf16)
    return high, (values - high.astype(f32)).astype(bf16)


def dot(a, b):
    return jnp.dot(a, b, preferred_element_type=f32)


def dot_nt(a, b):
    return lax.dot_general(a, b, (((1,), (1,)), ((), ())), preferred_element_type=f32)


def dot3(a, b):
    return dot(jnp.concatenate([a[0], a[0], a[1]], 1), jnp.concatenate([b[0], b[1], b[0]], 0))


def interleave(parts):
    while parts:
        parts = [part for part in parts if next(part, 0) is None]


def cubic_weights(t):
    return (
        ((-0.5 * t + 1.0) * t - 0.5) * t,
        (1.5 * t - 2.5) * t * t + 1.0,
        ((-1.5 * t + 2.0) * t + 0.5) * t,
        (0.5 * t - 0.5) * t * t,
    )


def one_hot(hit):
    return jnp.where(hit, 1.0, 0.0).astype(bf16)


def iota(shape, dim):
    return lax.broadcasted_iota(jnp.int32, shape, dim)


def cell_index():
    lane = iota((1, CELLS), 1)
    place, part = lane & 127, (lane & 127) >> 5
    row = jnp.where(lane < OWN, part + 1, jnp.where(part == 3, 0, part + 5))
    rim = place - RIM
    rim_row = (rim * 11) >> 5
    q = rim - 3 * rim_row
    rim_column = jnp.where(q == 0, 0, q + COLUMNS)
    rim_cell = jnp.where(rim < 3 * SPAN_X, rim_row * SPAN_Y + rim_column, -(1 << 20))
    return jnp.where((lane >= OWN) & (part == 2), rim_cell, row * SPAN_Y + (lane & 31) + 1)


def stencil_cells(base):
    shift = cell_index() - base
    return jnp.concatenate([one_hot(shift == a * SPAN_Y + e) for a in range(4) for e in range(4)], 0)


def same_bin(shape, group):
    return ((iota(shape, 0) ^ iota(shape, 1)) & (group - 1)) == 0


def group_slice(g, size):
    return slice(g * size, (g + 1) * size)


def twice(lanes):
    return jnp.concatenate([lanes, lanes], 1)


def spread_kernel(
    direction_hbm, offsets_hbm, cells_hbm, forward_hbm, *refs
):
    tables_hbm, (out, offsets, base, depth), tables = refs[:TABLES], refs[TABLES : TABLES + 4], refs[TABLES + 4 : 2 * TABLES + 4]
    direction, cells, forward, q_hi, q_lo, sems = refs[2 * TABLES + 4 :]
    group, beside = SPREAD_GROUP, 64 // SPREAD_GROUP
    copies = [
        pltpu.make_async_copy(cells_hbm, cells, sems.at[0]),
        pltpu.make_async_copy(direction_hbm, direction, sems.at[1]),
        *(pltpu.make_async_copy(offsets_hbm.at[:, d, :], offsets.at[d], sems.at[2 + d]) for d in range(3)),
        pltpu.make_async_copy(forward_hbm, forward, sems.at[5]),
        *(pltpu.make_async_copy(tables_hbm[t], tables[t], sems.at[6 + t]) for t in range(TABLES)),
    ]
    for copy in copies:
        copy.start()
    copies[0].wait()
    first = (cells[0:1, :] - lax.axis_index("px") * ROWS) * SPAN_Y + cells[1:2, :] - lax.axis_index("py") * COLUMNS
    packed = (first + 256 * cells[2:3, :]).astype(f32)
    own = iota((BINS, BINS), 0) == iota((BINS, BINS), 1)
    packed = jnp.sum(jnp.where(own, packed, 0.0), axis=1, keepdims=True).astype(jnp.int32)
    base[...] = jnp.broadcast_to(packed & 255, (BINS, 128))
    depth[...] = jnp.broadcast_to(packed >> 8, (BINS, 128))
    for copy in copies[1:5]:
        copy.wait()

    def multiplied(g):
        bins = group_slice(g, group)
        wx = cubic_weights(offsets[0, bins, :])
        wy = cubic_weights(offsets[1, bins, :])
        wz = cubic_weights(offsets[2, bins, :])
        d = direction[bins, :]
        wx = [w * d for w in wx]
        columns = jnp.concatenate(split(jnp.concatenate([x * y for x in wx for y in wy], 0)), 1)
        depths = twice(jnp.concatenate(split(jnp.concatenate(wz, 0)), 0))
        yield
        patches = dot_nt(depths, columns)
        yield
        patches = patches[: 4 * group] + patches[4 * group :]
        patches = jnp.concatenate(split(jnp.where(same_bin(patches.shape, group), patches, 0.0)), 0)
        cells = stencil_cells(twice(base[bins, :]))
        yield
        placed = dot(patches, cells)
        yield
        placed = split(placed[: 4 * group] + placed[4 * group :])
        for f in range(4):
            start = (4 * (g // beside) + f) * beside * group + g % beside * group
            q_hi[start : start + group, :] = placed[0][f * group : (f + 1) * group]
            q_lo[start : start + group, :] = placed[1][f * group : (f + 1) * group]

    def several(p, found):
        parts = [multiplied(beside * p + j) for j in range(beside)]
        while parts:
            parts = [part for part in parts if next(part, 0) is None]
            yield
        own = cells[2:3, beside * p * group : beside * (p + 1) * group]
        own = jnp.concatenate([own + f - 1 for f in range(4)], 1)
        at_depth = one_hot(iota((GRID_Z, 4 * beside * group), 0) == own)
        yield
        rows = slice(4 * beside * p * group, 4 * beside * (p + 1) * group)
        found.append(dot(twice(at_depth), jnp.concatenate([q_hi[rows, :], q_lo[rows, :]], 0)))
        yield

    found = []
    running = [several(p, found) for p in range(BINS // group // beside)]
    for turn in range(16):
        for p, part in enumerate(running):
            if turn >= p:
                next(part, 0)

    gridded = split(sum(found))
    copies[5].wait()
    transformed = dot3((forward[:, :GRID_Z], forward[:, GRID_Z:]), gridded)
    for part in range(2):
        for half in range(2):
            out[pl.ds(2 * part + half, GRID_Z, stride=4), :] = transformed[
                part * GRID_Z : (part + 1) * GRID_Z, half * 128 : (half + 1) * 128
            ]
    for copy in copies[6:]:
        copy.wait()


def moved(values, rows):
    return pltpu.roll(values, rows % DEVICES, 0)


def turned(values, lanes):
    return pltpu.roll(values, lanes % 128, 1) if lanes % 128 else values


def by_quarter(pieces):
    quarter = iota(pieces[0].shape, 1) >> 5
    result = 0.0
    for q, piece in enumerate(pieces):
        if piece is not None:
            result = jnp.where(quarter == q, piece, result)
    return result


def plane_kernel(
    received, along_x, back_x, along_y, back_y, sine_x, sines, rim, lengths, out, tiles, x_hi, x_lo, spectrum
):
    last_column = (iota((DEVICES, CELLS), 1) & 31) == COLUMNS - 1
    quarter = iota((DEVICES, OWN), 1) >> 5
    place = ((0, 0), (0, 1), (0, 2), (0, 3), (1, 0), (1, 1), (1, 3))

    def filtering():
        yield
        length_x, length_y, length_z = (lengths[0:1, j : j + 1] for j in range(3))
        scale_x, scale_y = length_x * length_x, length_y * length_y
        frequency = lax.axis_index("px") * N_PY + lax.axis_index("py")
        sine = jnp.where(iota((1, GRID_Z), 1) == frequency, sines[1:2, :GRID_Z], 0.0)
        rest = 1.0 + length_z * length_z * jnp.sum(sine, axis=1, keepdims=True)
        factor = 2.0 / (M_X * M_Y) * length_x * length_y * length_z
        rows = rest + scale_x * sine_x[...]
        for j in range(M_Y // 128):
            lanes = slice(128 * j, 128 * (j + 1))
            denominator = rows + scale_y * sines[0:1, lanes]
            spectrum[:, lanes] = factor / (denominator * denominator)

    def plane(part):
        own, rest = (received[pl.ds(2 * part + half, DEVICES, stride=4), :] for half in range(2))
        rims = dot(jnp.concatenate(split(rest), 0), rim[...])
        yield
        columns = rims[:DEVICES] + rims[DEVICES:]
        columns = jnp.where(last_column, moved(columns, -1), moved(columns, 1))
        tiles[part, 0] = own + columns[:, :OWN]
        tiles[part, 1] = jnp.where(quarter == 2, 0.0, rest) + columns[:, OWN:]
        loaded = [[tiles[part, tile, pl.ds(py, N_PX, stride=N_PY), :] for py in range(N_PY)] for tile in range(2)]
        for slot, (tile, q) in enumerate(place):
            rows = slice(slot * N_PX, (slot + 1) * N_PX)
            for half in range(2):
                lanes = slice(128 * half, 128 * (half + 1))
                values = by_quarter([turned(loaded[tile][4 * half + p], 32 * (p - q)) for p in range(4)])
                x_hi[part, rows, lanes], x_lo[part, rows, lanes] = split(values)
        empty = slice(len(place) * N_PX, DEVICES)
        x_hi[part, empty, :] = jnp.zeros((N_PX, GRID_Y), bf16)
        x_lo[part, empty, :] = jnp.zeros((N_PX, GRID_Y), bf16)
        yield
        found = []

        def half(h):
            rows = slice(h * M_X // 2, (h + 1) * M_X // 2)
            values = dot3((along_x[rows, :DEVICES], along_x[rows, DEVICES:]), (x_hi[part], x_lo[part]))
            yield
            values = split(values)
            yield
            values = dot3(values, (along_y[:, :M_Y], along_y[:, M_Y:]))
            yield
            values = split(values * spectrum[rows, :])
            yield
            values = dot3(values, (back_y[:, :GRID_Y], back_y[:, GRID_Y:]))
            yield
            values = split(values)
            yield
            left = slice(rows.start + M_X, rows.stop + M_X)
            found.append(dot3((back_x[:, rows], back_x[:, left]), values))
            yield

        parts = [half(0), half(1)]
        while parts:
            parts = [p for p in parts if next(p, 0) is None]
            yield
        values = sum(found)
        for py in range(N_PY):
            lanes = slice(128 * (py // 4), 128 * (py // 4 + 1))
            pieces = [[None] * 4, [None] * 4]
            for slot, (tile, q) in enumerate(place):
                pieces[tile][q] = turned(values[slot * N_PX : (slot + 1) * N_PX, lanes], 32 * (q - py % 4))
            for tile in range(2):
                tiles[part, tile, pl.ds(py, N_PX, stride=N_PY), :] = by_quarter(pieces[tile])
        own, rest = tiles[part, 0], tiles[part, 1]
        out[pl.ds(2 * part, DEVICES, stride=4), :] = own
        region = jnp.concatenate([own, rest], 1)
        region = jnp.concatenate(split(jnp.where(last_column, moved(region, 1), moved(region, -1))), 0)
        yield
        rims = dot_nt(region, rim[...])
        yield
        out[pl.ds(2 * part + 1, DEVICES, stride=4), :] = rest + rims[:DEVICES] + rims[DEVICES:]

    interleave([plane(0), plane(1), filtering()])


def gather_kernel(received, direction, residual, noise, offsets, base, depth, inverse, image, sums, v_hi, v_lo):
    group = READ_GROUP
    for part in range(2):
        for half in range(2):
            rows = slice(part * GRID_Z, (part + 1) * GRID_Z)
            lanes = slice(half * 128, (half + 1) * 128)
            v_hi[rows, lanes], v_lo[rows, lanes] = split(received[pl.ds(2 * part + half, GRID_Z, stride=4), :])
    grid = split(dot3((inverse[:, : 2 * GRID_Z], inverse[:, 2 * GRID_Z :]), (v_hi[...], v_lo[...])))
    v_hi[:GRID_Z, :], v_lo[:GRID_Z, :] = grid

    def step(g, found):
        bins = group_slice(g, group)
        shift = iota((group, GRID_Z), 1) - twice(depth[bins, :])
        at_depth = jnp.concatenate([one_hot(shift == f - 1) for f in range(4)], 0)
        yield
        lines = [dot(at_depth, v[:GRID_Z, :]).astype(bf16) for v in (v_hi, v_lo)]
        lines = jnp.concatenate(lines, 0)
        cells = stencil_cells(twice(base[bins, :]))
        yield
        read = dot_nt(cells, lines)
        yield
        read = jnp.where(same_bin(read.shape, group), read, 0.0).astype(bf16)
        depths = jnp.concatenate(split(jnp.concatenate(cubic_weights(offsets[2, bins, :]), 0)), 1)
        depths = jnp.concatenate([depths, depths], 0)
        yield
        along = dot(read, depths)
        yield
        along = along[:, :BIN] + along[:, BIN:]
        wx = cubic_weights(offsets[0, bins, :])
        wy = cubic_weights(offsets[1, bins, :])
        value = 0.0
        for a in range(4):
            row = 0.0
            for e in range(4):
                start = (4 * a + e) * group
                row = row + wy[e] * along[start : start + group]
            value = value + wx[a] * row
        d, r = direction[bins, :], residual[bins, :]
        value = value + noise[bins, :] * d
        image[bins, :] = value
        found.append([(x * y).reshape(group // 8, 8, BIN).sum(0) for x, y in ((r, r), (d, value), (r, value), (value, value))])

    found = []
    interleave([step(g, found) for g in range(BINS // group)])
    totals = [sum(parts) for parts in zip(*found)]
    lane = iota((1, BIN), 1)
    row = jnp.zeros((1, BIN), f32)
    for j, part in enumerate(totals):
        row = jnp.where(lane == j, jnp.sum(part, keepdims=True), row)
    sums[...] = jnp.broadcast_to(row, (DEVICES, BIN))


def step_kernel(sums, iterate, residual, direction, image, new_iterate, new_residual, new_direction):
    row = jnp.sum(sums[...], axis=0, keepdims=True)
    old_norm, curvature, cross, square = (row[:, j : j + 1] for j in range(4))
    step = old_norm / curvature
    new_norm = old_norm - 2.0 * step * cross + step * step * square
    d = direction[...]
    r = residual[...] - step * image[...]
    new_iterate[...] = iterate[...] + step * d
    new_residual[...] = r
    new_direction[...] = r + (new_norm / old_norm) * d


VMEM = pl.BlockSpec(memory_space=pltpu.VMEM)
HBM = pl.BlockSpec(memory_space=pltpu.HBM)


def params():
    return pltpu.CompilerParams(vmem_limit_bytes=16 * 1024 * 1024)


def filter_plane(received, tables):
    return pl.pallas_call(
        plane_kernel,
        out_shape=jax.ShapeDtypeStruct((4 * DEVICES, 128), f32),
        in_specs=[VMEM] * (1 + TABLES),
        out_specs=VMEM,
        scratch_shapes=[
            pltpu.VMEM((2, 2, DEVICES, OWN), f32),
            pltpu.VMEM((2, DEVICES, GRID_Y), bf16),
            pltpu.VMEM((2, DEVICES, GRID_Y), bf16),
            pltpu.VMEM((M_X, M_Y), f32),
        ],
        compiler_params=params(),
        name="plane",
    )(received, *tables)


def on_device(solution, residual, direction, offsets, noise, bin_cells, lengths):
    forward, inverse = depth_tables()
    d, r = direction.reshape(BINS, BIN), residual.reshape(BINS, BIN)
    point = jax.ShapeDtypeStruct((BINS, BIN), f32)
    index = jax.ShapeDtypeStruct((BINS, BIN), jnp.int32)
    block = jax.ShapeDtypeStruct((4 * DEVICES, 128), f32)

    tables = (*plane_tables(), lengths.reshape(1, 3))
    by_tile = offsets.reshape(3, BINS, BIN).transpose(1, 0, 2)
    operands = [pltpu.with_memory_space_constraint(x, pltpu.HBM) for x in (d, by_tile, bin_cells, forward, *tables)]

    blocks, by_bin, base, depth, *tables = pl.pallas_call(
        spread_kernel,
        out_shape=(
            block, jax.ShapeDtypeStruct((3, BINS, BIN), f32), index, index,
            *(jax.ShapeDtypeStruct(t.shape, t.dtype) for t in tables),
        ),
        in_specs=[HBM] * len(operands),
        out_specs=(VMEM,) * (4 + TABLES),
        scratch_shapes=[
            pltpu.VMEM((BINS, BIN), f32),
            pltpu.VMEM((3, BINS), jnp.int32),
            pltpu.VMEM(forward.shape, bf16),
            pltpu.VMEM((4 * BINS, CELLS), bf16),
            pltpu.VMEM((4 * BINS, CELLS), bf16),
            pltpu.SemaphoreType.DMA((6 + TABLES,)),
        ],
        compiler_params=params(),
        name="spread",
    )(*operands)
    received = lax.all_to_all(blocks.reshape(DEVICES, 4, 128), ("px", "py"), 0, 0, tiled=True)

    filtered = filter_plane(received.reshape(4 * DEVICES, 128), tables)
    returned = lax.all_to_all(filtered.reshape(DEVICES, 4, 128), ("px", "py"), 0, 0, tiled=True)

    image, sums = pl.pallas_call(
        gather_kernel,
        out_shape=(point, jax.ShapeDtypeStruct((DEVICES, BIN), f32)),
        in_specs=[VMEM] * 8,
        out_specs=(VMEM, VMEM),
        scratch_shapes=[pltpu.VMEM((2 * GRID_Z, CELLS), bf16)] * 2,
        compiler_params=params(),
        name="interpolate",
    )(returned.reshape(4 * DEVICES, 128), d, r, noise.reshape(BINS, BIN), by_bin, base, depth, inverse)

    everywhere = lax.all_to_all(sums.reshape(DEVICES, 1, BIN), ("px", "py"), 0, 0, tiled=True)
    outs = pl.pallas_call(
        step_kernel,
        out_shape=(point,) * 3,
        in_specs=[VMEM] * 5,
        out_specs=(VMEM,) * 3,
        compiler_params=params(),
        name="step",
    )(everywhere.reshape(DEVICES, BIN), solution.reshape(BINS, BIN), r, d, image)
    return tuple(out.reshape(1, -1) for out in outs)


def solution(mesh):
    points = P(None, ("px", "py"))
    return jax.shard_map(
        on_device,
        mesh=mesh,
        in_specs=(points, points, points, points, P(("px", "py")), points, P()),
        out_specs=(points, points, points),
        check_vma=False,
    )
```

```python
import jax
import jax.numpy as jnp
import ml_dtypes
import numpy as np
from jax import lax
from jax.experimental import pallas as pl
from jax.experimental.pallas import tpu as pltpu
from jax.sharding import PartitionSpec as P

GRID_X, GRID_Y, GRID_Z = 128, 256, 256
BIN = 128
N_PX, N_PY = 32, 8
DEVICES = N_PX * N_PY
ROWS, COLUMNS = GRID_X // N_PX, GRID_Y // N_PY
SPAN_X, SPAN_Y = ROWS + 3, COLUMNS + 3
CELLS, OWN, RIM = 256, 128, 64
M_X, M_Y, M_Z = 2 * GRID_X, 2 * GRID_Y, 2 * GRID_Z - 1
BINS = 256
SPREAD_GROUP, READ_GROUP = 16, 32
TABLES = 8
SLOTS = (1, 2, 3, 4, 5, 6, 0)

f32, bf16 = jnp.float32, jnp.bfloat16


def halves(table):
    table = np.asarray(table, np.float64)
    high = table.astype(np.float32).astype(ml_dtypes.bfloat16)
    low = (table - high.astype(np.float64)).astype(np.float32).astype(ml_dtypes.bfloat16)
    return np.concatenate([high, low], -1)


def depth_tables():
    freq = np.arange(GRID_Z)[:, None]
    depth = np.arange(GRID_Z)[None, :]
    angle = 2 * np.pi * (freq * depth % M_Z) / M_Z
    forward = np.concatenate([np.cos(angle), -np.sin(angle)], 0)
    doubled = np.where(freq == 0, 1.0, 2.0) / M_Z
    inverse = np.concatenate([np.cos(angle) * doubled, -np.sin(angle) * doubled], 0).T
    return halves(forward), halves(inverse)


def cas(product, length):
    angle = 2 * np.pi * (product % length) / length
    return np.cos(angle) + np.sin(angle)


def plane_tables():
    kx, ky = np.arange(M_X), np.arange(M_Y)
    px = np.arange(N_PX)
    x = np.concatenate([ROWS * px + slot - 1 for slot in SLOTS])
    along_x = np.zeros((M_X, DEVICES))
    along_x[:, : len(x)] = cas(kx[:, None] * x[None, :], M_X)
    along_y = cas(np.arange(GRID_Y)[:, None] * ky[None, :], M_Y)
    sine_x = np.sin(np.pi * kx / M_X) ** 2
    sines = np.zeros((8, M_Y), np.float32)
    sines[0] = np.sin(np.pi * ky / M_Y) ** 2
    sines[1, :GRID_Z] = np.sin(np.pi * np.arange(GRID_Z) / M_Z) ** 2
    rim = np.zeros((OWN, CELLS), np.float32)
    for row in range(SPAN_X):
        start = {0: OWN + 96, 5: OWN, 6: OWN + 32}.get(row, (row - 1) * COLUMNS)
        for q, column in enumerate((COLUMNS - 1, 0, 1)):
            rim[RIM + 3 * row + q, start + column] = 1.0
    return (
        halves(along_x),
        halves(along_x.T),
        halves(along_y),
        halves(along_y.T),
        np.repeat(sine_x[:, None], 128, 1).astype(np.float32),
        sines,
        rim.astype(ml_dtypes.bfloat16),
    )


def split(values):
    high = values.astype(bf16)
    return high, (values - high.astype(f32)).astype(bf16)


def dot(a, b):
    return jnp.dot(a, b, preferred_element_type=f32)


def dot_nt(a, b):
    return lax.dot_general(a, b, (((1,), (1,)), ((), ())), preferred_element_type=f32)


def dot3(a, b):
    return dot(jnp.concatenate([a[0], a[0], a[1]], 1), jnp.concatenate([b[0], b[1], b[0]], 0))


def interleave(parts):
    while parts:
        parts = [part for part in parts if next(part, 0) is None]


def cubic_weights(t):
    return (
        ((-0.5 * t + 1.0) * t - 0.5) * t,
        (1.5 * t - 2.5) * t * t + 1.0,
        ((-1.5 * t + 2.0) * t + 0.5) * t,
        (0.5 * t - 0.5) * t * t,
    )


def one_hot(hit):
    return jnp.where(hit, 1.0, 0.0).astype(bf16)


def iota(shape, dim):
    return lax.broadcasted_iota(jnp.int32, shape, dim)


def cell_index():
    lane = iota((1, CELLS), 1)
    place, part = lane & 127, (lane & 127) >> 5
    row = jnp.where(lane < OWN, part + 1, jnp.where(part == 3, 0, part + 5))
    rim = place - RIM
    rim_row = (rim * 11) >> 5
    q = rim - 3 * rim_row
    rim_column = jnp.where(q == 0, 0, q + COLUMNS)
    rim_cell = jnp.where(rim < 3 * SPAN_X, rim_row * SPAN_Y + rim_column, -(1 << 20))
    return jnp.where((lane >= OWN) & (part == 2), rim_cell, row * SPAN_Y + (lane & 31) + 1)


def stencil_cells(base):
    shift = cell_index() - base
    return jnp.concatenate([one_hot(shift == a * SPAN_Y + e) for a in range(4) for e in range(4)], 0)


def same_bin(shape, group):
    return ((iota(shape, 0) ^ iota(shape, 1)) & (group - 1)) == 0


def group_slice(g, size):
    return slice(g * size, (g + 1) * size)


def twice(lanes):
    return jnp.concatenate([lanes, lanes], 1)


def spread_kernel(
    direction_hbm, offsets_hbm, cells_hbm, forward_hbm, *refs
):
    tables_hbm, (out, offsets, base, depth), tables = refs[:TABLES], refs[TABLES : TABLES + 4], refs[TABLES + 4 : 2 * TABLES + 4]
    direction, cells, forward, q_hi, q_lo, sems = refs[2 * TABLES + 4 :]
    group, beside = SPREAD_GROUP, 64 // SPREAD_GROUP
    copies = [
        pltpu.make_async_copy(cells_hbm, cells, sems.at[0]),
        pltpu.make_async_copy(direction_hbm, direction, sems.at[1]),
        *(pltpu.make_async_copy(offsets_hbm.at[:, d, :], offsets.at[d], sems.at[2 + d]) for d in range(3)),
        pltpu.make_async_copy(forward_hbm, forward, sems.at[5]),
        *(pltpu.make_async_copy(tables_hbm[t], tables[t], sems.at[6 + t]) for t in range(TABLES)),
    ]
    for copy in copies:
        copy.start()
    copies[0].wait()
    first = (cells[0:1, :] - lax.axis_index("px") * ROWS) * SPAN_Y + cells[1:2, :] - lax.axis_index("py") * COLUMNS
    packed = (first + 256 * cells[2:3, :]).astype(f32)
    own = iota((BINS, BINS), 0) == iota((BINS, BINS), 1)
    packed = jnp.sum(jnp.where(own, packed, 0.0), axis=1, keepdims=True).astype(jnp.int32)
    base[...] = jnp.broadcast_to(packed & 255, (BINS, 128))
    depth[...] = jnp.broadcast_to(packed >> 8, (BINS, 128))
    for copy in copies[1:5]:
        copy.wait()

    def multiplied(g):
        bins = group_slice(g, group)
        wx = cubic_weights(offsets[0, bins, :])
        wy = cubic_weights(offsets[1, bins, :])
        wz = cubic_weights(offsets[2, bins, :])
        d = direction[bins, :]
        wx = [w * d for w in wx]
        columns = jnp.concatenate(split(jnp.concatenate([x * y for x in wx for y in wy], 0)), 1)
        depths = twice(jnp.concatenate(split(jnp.concatenate(wz, 0)), 0))
        yield
        patches = dot_nt(depths, columns)
        yield
        patches = patches[: 4 * group] + patches[4 * group :]
        patches = jnp.concatenate(split(jnp.where(same_bin(patches.shape, group), patches, 0.0)), 0)
        cells = stencil_cells(twice(base[bins, :]))
        yield
        placed = dot(patches, cells)
        yield
        placed = placed.astype(bf16)
        placed = placed[: 4 * group], placed[4 * group :]
        for f in range(4):
            start = (4 * (g // beside) + f) * beside * group + g % beside * group
            q_hi[start : start + group, :] = placed[0][f * group : (f + 1) * group]
            q_lo[start : start + group, :] = placed[1][f * group : (f + 1) * group]

    def several(p, found):
        parts = [multiplied(beside * p + j) for j in range(beside)]
        while parts:
            parts = [part for part in parts if next(part, 0) is None]
            yield
        own = cells[2:3, beside * p * group : beside * (p + 1) * group]
        own = jnp.concatenate([own + f - 1 for f in range(4)], 1)
        at_depth = one_hot(iota((GRID_Z, 4 * beside * group), 0) == own)
        yield
        rows = slice(4 * beside * p * group, 4 * beside * (p + 1) * group)
        found.append(dot(twice(at_depth), jnp.concatenate([q_hi[rows, :], q_lo[rows, :]], 0)))
        yield

    found = []
    running = [several(p, found) for p in range(BINS // group // beside)]
    for turn in range(16):
        for p, part in enumerate(running):
            if turn >= p:
                next(part, 0)

    gridded = split(sum(found))
    copies[5].wait()
    for part in range(2):
        rows = slice(part * GRID_Z, (part + 1) * GRID_Z)
        transformed = dot3((forward[rows, :GRID_Z], forward[rows, GRID_Z:]), gridded)
        for half in range(2):
            out[pl.ds(2 * part + half, GRID_Z, stride=4), :] = transformed[:, half * 128 : (half + 1) * 128]
    for copy in copies[6:]:
        copy.wait()


def moved(values, rows):
    return pltpu.roll(values, rows % DEVICES, 0)


def turned(values, lanes):
    return pltpu.roll(values, lanes % 128, 1) if lanes % 128 else values


def by_quarter(pieces):
    quarter = iota(pieces[0].shape, 1) >> 5
    result = 0.0
    for q, piece in enumerate(pieces):
        if piece is not None:
            result = jnp.where(quarter == q, piece, result)
    return result


def plane_kernel(
    received, along_x, back_x, along_y, back_y, sine_x, sines, rim, lengths, out, tiles, x_hi, x_lo, spectrum
):
    rim_lane = iota((DEVICES, OWN), 1) & 31
    before = rim_lane == 3 * ((rim_lane * 11) >> 5)
    place = ((0, 0), (0, 1), (0, 2), (0, 3), (1, 0), (1, 1), (1, 3))

    def filtering():
        yield
        length_x, length_y, length_z = (lengths[0:1, j : j + 1] for j in range(3))
        scale_x, scale_y = length_x * length_x, length_y * length_y
        frequency = lax.axis_index("px") * N_PY + lax.axis_index("py")
        sine = jnp.where(iota((1, GRID_Z), 1) == frequency, sines[1:2, :GRID_Z], 0.0)
        rest = 1.0 + length_z * length_z * jnp.sum(sine, axis=1, keepdims=True)
        factor = 2.0 / (M_X * M_Y) * length_x * length_y * length_z
        rows = rest + scale_x * sine_x[...]
        for j in range(M_Y // 128):
            lanes = slice(128 * j, 128 * (j + 1))
            denominator = rows + scale_y * sines[0:1, lanes]
            spectrum[:, lanes] = factor / (denominator * denominator)

    def plane(part):
        own, rest = (received[pl.ds(2 * part + half, DEVICES, stride=4), :] for half in range(2))
        to_owner = jnp.where(before, moved(rest, -1), moved(rest, 1))
        rims = dot(jnp.concatenate(split(to_owner), 0), rim[...])
        yield
        columns = rims[:DEVICES] + rims[DEVICES:]
        tiles[part, 0] = own + columns[:, :OWN]
        tiles[part, 1] = rest + columns[:, OWN:]
        loaded = [[tiles[part, tile, pl.ds(py, N_PX, stride=N_PY), :] for py in range(N_PY)] for tile in range(2)]
        for slot, (tile, q) in enumerate(place):
            rows = slice(slot * N_PX, (slot + 1) * N_PX)
            for half in range(2):
                lanes = slice(128 * half, 128 * (half + 1))
                values = by_quarter([turned(loaded[tile][4 * half + p], 32 * (p - q)) for p in range(4)])
                x_hi[part, rows, lanes], x_lo[part, rows, lanes] = split(values)
        empty = slice(len(place) * N_PX, DEVICES)
        x_hi[part, empty, :] = jnp.zeros((N_PX, GRID_Y), bf16)
        x_lo[part, empty, :] = jnp.zeros((N_PX, GRID_Y), bf16)
        yield
        found = []

        def half(h):
            rows = slice(h * M_X // 2, (h + 1) * M_X // 2)
            values = dot3((along_x[rows, :DEVICES], along_x[rows, DEVICES:]), (x_hi[part], x_lo[part]))
            yield
            values = split(values)
            yield
            values = dot3(values, (along_y[:, :M_Y], along_y[:, M_Y:]))
            yield
            values = split(values * spectrum[rows, :])
            yield
            values = dot3(values, (back_y[:, :GRID_Y], back_y[:, GRID_Y:]))
            yield
            values = split(values)
            left = slice(rows.start + M_X, rows.stop + M_X)
            found.append(dot3((back_x[:, rows], back_x[:, left]), values))
            yield

        parts = [half(0), half(1)]
        while parts:
            parts = [p for p in parts if next(p, 0) is None]
            yield
        values = sum(found)
        for py in range(N_PY):
            lanes = slice(128 * (py // 4), 128 * (py // 4 + 1))
            pieces = [[None] * 4, [None] * 4]
            for slot, (tile, q) in enumerate(place):
                pieces[tile][q] = turned(values[slot * N_PX : (slot + 1) * N_PX, lanes], 32 * (q - py % 4))
            for tile in range(2):
                tiles[part, tile, pl.ds(py, N_PX, stride=N_PY), :] = by_quarter(pieces[tile])
        own, rest = tiles[part, 0], tiles[part, 1]
        out[pl.ds(2 * part, DEVICES, stride=4), :] = own
        region = jnp.concatenate(split(jnp.concatenate([own, rest], 1)), 0)
        yield
        rims = dot_nt(region, rim[...])
        yield
        rims = rims[:DEVICES] + rims[DEVICES:]
        rims = jnp.where(before, moved(rims, 1), moved(rims, -1))
        out[pl.ds(2 * part + 1, DEVICES, stride=4), :] = rest + rims

    interleave([plane(0), plane(1), filtering()])


def gather_kernel(received, direction, residual, noise, offsets, base, depth, inverse, image, sums, v_hi, v_lo):
    group = READ_GROUP
    for part in range(2):
        for half in range(2):
            rows = slice(part * GRID_Z, (part + 1) * GRID_Z)
            lanes = slice(half * 128, (half + 1) * 128)
            v_hi[rows, lanes], v_lo[rows, lanes] = split(received[pl.ds(2 * part + half, GRID_Z, stride=4), :])
    grid = split(dot3((inverse[:, : 2 * GRID_Z], inverse[:, 2 * GRID_Z :]), (v_hi[...], v_lo[...])))
    v_hi[:GRID_Z, :], v_lo[:GRID_Z, :] = grid

    def step(g, found):
        bins = group_slice(g, group)
        shift = iota((group, GRID_Z), 1) - twice(depth[bins, :])
        at_depth = jnp.concatenate([one_hot(shift == f - 1) for f in range(4)], 0)
        yield
        lines = [dot(at_depth, v[:GRID_Z, :]).astype(bf16) for v in (v_hi, v_lo)]
        lines = jnp.concatenate(lines, 0)
        cells = stencil_cells(twice(base[bins, :]))
        yield
        read = dot_nt(cells, lines)
        yield
        read = jnp.where(same_bin(read.shape, group), read, 0.0).astype(bf16)
        depths = jnp.concatenate(split(jnp.concatenate(cubic_weights(offsets[2, bins, :]), 0)), 1)
        depths = jnp.concatenate([depths, depths], 0)
        yield
        along = dot(read, depths)
        yield
        along = along[:, :BIN] + along[:, BIN:]
        wx = cubic_weights(offsets[0, bins, :])
        wy = cubic_weights(offsets[1, bins, :])
        value = 0.0
        for a in range(4):
            row = 0.0
            for e in range(4):
                start = (4 * a + e) * group
                row = row + wy[e] * along[start : start + group]
            value = value + wx[a] * row
        d, r = direction[bins, :], residual[bins, :]
        value = value + noise[bins, :] * d
        image[bins, :] = value
        found.append([(x * y).reshape(group // 8, 8, BIN).sum(0) for x, y in ((r, r), (d, value), (r, value), (value, value))])

    found = []
    interleave([step(g, found) for g in range(BINS // group)])
    totals = [sum(parts) for parts in zip(*found)]
    lane = iota((1, BIN), 1)
    row = jnp.zeros((1, BIN), f32)
    for j, part in enumerate(totals):
        row = jnp.where(lane == j, jnp.sum(part, keepdims=True), row)
    sums[...] = jnp.broadcast_to(row, (DEVICES, BIN))


def step_kernel(sums, iterate, residual, direction, image, new_iterate, new_residual, new_direction):
    row = jnp.sum(sums[...], axis=0, keepdims=True)
    old_norm, curvature, cross, square = (row[:, j : j + 1] for j in range(4))
    step = old_norm / curvature
    new_norm = old_norm - 2.0 * step * cross + step * step * square
    d = direction[...]
    r = residual[...] - step * image[...]
    new_iterate[...] = iterate[...] + step * d
    new_residual[...] = r
    new_direction[...] = r + (new_norm / old_norm) * d


VMEM = pl.BlockSpec(memory_space=pltpu.VMEM)
HBM = pl.BlockSpec(memory_space=pltpu.HBM)


def params():
    return pltpu.CompilerParams(vmem_limit_bytes=16 * 1024 * 1024)


def filter_plane(received, tables):
    return pl.pallas_call(
        plane_kernel,
        out_shape=jax.ShapeDtypeStruct((4 * DEVICES, 128), f32),
        in_specs=[VMEM] * (1 + TABLES),
        out_specs=VMEM,
        scratch_shapes=[
            pltpu.VMEM((2, 2, DEVICES, OWN), f32),
            pltpu.VMEM((2, DEVICES, GRID_Y), bf16),
            pltpu.VMEM((2, DEVICES, GRID_Y), bf16),
            pltpu.VMEM((M_X, M_Y), f32),
        ],
        compiler_params=params(),
        name="plane",
    )(received, *tables)


def on_device(solution, residual, direction, offsets, noise, bin_cells, lengths):
    forward, inverse = depth_tables()
    d, r = direction.reshape(BINS, BIN), residual.reshape(BINS, BIN)
    point = jax.ShapeDtypeStruct((BINS, BIN), f32)
    index = jax.ShapeDtypeStruct((BINS, BIN), jnp.int32)
    block = jax.ShapeDtypeStruct((4 * DEVICES, 128), f32)

    tables = (*plane_tables(), lengths.reshape(1, 3))
    by_tile = offsets.reshape(3, BINS, BIN).transpose(1, 0, 2)
    operands = [pltpu.with_memory_space_constraint(x, pltpu.HBM) for x in (d, by_tile, bin_cells, forward, *tables)]

    blocks, by_bin, base, depth, *tables = pl.pallas_call(
        spread_kernel,
        out_shape=(
            block, jax.ShapeDtypeStruct((3, BINS, BIN), f32), index, index,
            *(jax.ShapeDtypeStruct(t.shape, t.dtype) for t in tables),
        ),
        in_specs=[HBM] * len(operands),
        out_specs=(VMEM,) * (4 + TABLES),
        scratch_shapes=[
            pltpu.VMEM((BINS, BIN), f32),
            pltpu.VMEM((3, BINS), jnp.int32),
            pltpu.VMEM(forward.shape, bf16),
            pltpu.VMEM((4 * BINS, CELLS), bf16),
            pltpu.VMEM((4 * BINS, CELLS), bf16),
            pltpu.SemaphoreType.DMA((6 + TABLES,)),
        ],
        compiler_params=params(),
        name="spread",
    )(*operands)
    received = lax.all_to_all(blocks.reshape(DEVICES, 4, 128), ("px", "py"), 0, 0, tiled=True)

    filtered = filter_plane(received.reshape(4 * DEVICES, 128), tables)
    returned = lax.all_to_all(filtered.reshape(DEVICES, 4, 128), ("px", "py"), 0, 0, tiled=True)

    image, sums = pl.pallas_call(
        gather_kernel,
        out_shape=(point, jax.ShapeDtypeStruct((DEVICES, BIN), f32)),
        in_specs=[VMEM] * 8,
        out_specs=(VMEM, VMEM),
        scratch_shapes=[pltpu.VMEM((2 * GRID_Z, CELLS), bf16)] * 2,
        compiler_params=params(),
        name="interpolate",
    )(returned.reshape(4 * DEVICES, 128), d, r, noise.reshape(BINS, BIN), by_bin, base, depth, inverse)

    everywhere = lax.all_to_all(sums.reshape(DEVICES, 1, BIN), ("px", "py"), 0, 0, tiled=True)
    outs = pl.pallas_call(
        step_kernel,
        out_shape=(point,) * 3,
        in_specs=[VMEM] * 5,
        out_specs=(VMEM,) * 3,
        compiler_params=params(),
        name="step",
    )(everywhere.reshape(DEVICES, BIN), solution.reshape(BINS, BIN), r, d, image)
    return tuple(out.reshape(1, -1) for out in outs)


def solution(mesh):
    points = P(None, ("px", "py"))
    return jax.shard_map(
        on_device,
        mesh=mesh,
        in_specs=(points, points, points, points, P(("px", "py")), points, P()),
        out_specs=(points, points, points),
        check_vma=False,
    )
```

```python
import jax
import jax.numpy as jnp
import ml_dtypes
import numpy as np
from jax import lax
from jax.experimental import pallas as pl
from jax.experimental.pallas import tpu as pltpu
from jax.sharding import PartitionSpec as P

GRID_X, GRID_Y, GRID_Z = 128, 256, 256
BIN = 128
N_PX, N_PY = 32, 8
DEVICES = N_PX * N_PY
ROWS, COLUMNS = GRID_X // N_PX, GRID_Y // N_PY
SPAN_X, SPAN_Y = ROWS + 3, COLUMNS + 3
CELLS, OWN, RIM = 256, 128, 64
M_X, M_Y, M_Z = 2 * GRID_X, 2 * GRID_Y, 2 * GRID_Z - 1
BINS = 256
SPREAD_GROUP, READ_GROUP = 16, 32
TABLES = 8
SLOTS = (1, 2, 3, 4, 5, 6, 0)

f32, bf16 = jnp.float32, jnp.bfloat16


def halves(table):
    table = np.asarray(table, np.float64)
    high = table.astype(np.float32).astype(ml_dtypes.bfloat16)
    low = (table - high.astype(np.float64)).astype(np.float32).astype(ml_dtypes.bfloat16)
    return np.concatenate([high, low], -1)


def depth_tables():
    freq = np.arange(GRID_Z)[:, None]
    depth = np.arange(GRID_Z)[None, :]
    angle = 2 * np.pi * (freq * depth % M_Z) / M_Z
    forward = np.concatenate([np.cos(angle), -np.sin(angle)], 0)
    doubled = np.where(freq == 0, 1.0, 2.0) / M_Z
    inverse = np.concatenate([np.cos(angle) * doubled, -np.sin(angle) * doubled], 0).T
    return halves(forward), halves(inverse)


def cas(product, length):
    angle = 2 * np.pi * (product % length) / length
    return np.cos(angle) + np.sin(angle)


def plane_tables():
    kx, ky = np.arange(M_X), np.arange(M_Y)
    px = np.arange(N_PX)
    x = np.concatenate([ROWS * px + slot - 1 for slot in SLOTS])
    along_x = np.zeros((M_X, DEVICES))
    along_x[:, : len(x)] = cas(kx[:, None] * x[None, :], M_X)
    along_y = cas(np.arange(GRID_Y)[:, None] * ky[None, :], M_Y)
    sine_x = np.sin(np.pi * kx / M_X) ** 2
    sines = np.zeros((8, M_Y), np.float32)
    sines[0] = np.sin(np.pi * ky / M_Y) ** 2
    sines[1, :GRID_Z] = np.sin(np.pi * np.arange(GRID_Z) / M_Z) ** 2
    rim = np.zeros((OWN, CELLS), np.float32)
    for row in range(SPAN_X):
        start = {0: OWN + 96, 5: OWN, 6: OWN + 32}.get(row, (row - 1) * COLUMNS)
        for q, column in enumerate((COLUMNS - 1, 0, 1)):
            rim[RIM + 3 * row + q, start + column] = 1.0
    return (
        halves(along_x),
        halves(along_x.T),
        halves(along_y),
        halves(along_y.T),
        np.repeat(sine_x[:, None], 128, 1).astype(np.float32),
        sines,
        rim.astype(ml_dtypes.bfloat16),
    )


def split(values):
    high = values.astype(bf16)
    return high, (values - high.astype(f32)).astype(bf16)


def dot(a, b):
    return jnp.dot(a, b, preferred_element_type=f32)


def dot_nt(a, b):
    return lax.dot_general(a, b, (((1,), (1,)), ((), ())), preferred_element_type=f32)


def dot3(a, b):
    return dot(jnp.concatenate([a[0], a[0], a[1]], 1), jnp.concatenate([b[0], b[1], b[0]], 0))


def interleave(parts):
    while parts:
        parts = [part for part in parts if next(part, 0) is None]


def cubic_weights(t):
    return (
        ((-0.5 * t + 1.0) * t - 0.5) * t,
        (1.5 * t - 2.5) * t * t + 1.0,
        ((-1.5 * t + 2.0) * t + 0.5) * t,
        (0.5 * t - 0.5) * t * t,
    )


def one_hot(hit):
    return jnp.where(hit, 1.0, 0.0).astype(bf16)


def iota(shape, dim):
    return lax.broadcasted_iota(jnp.int32, shape, dim)


def cell_index():
    lane = iota((1, CELLS), 1)
    place, part = lane & 127, (lane & 127) >> 5
    row = jnp.where(lane < OWN, part + 1, jnp.where(part == 3, 0, part + 5))
    rim = place - RIM
    rim_row = (rim * 11) >> 5
    q = rim - 3 * rim_row
    rim_column = jnp.where(q == 0, 0, q + COLUMNS)
    rim_cell = jnp.where(rim < 3 * SPAN_X, rim_row * SPAN_Y + rim_column, -(1 << 20))
    return jnp.where((lane >= OWN) & (part == 2), rim_cell, row * SPAN_Y + (lane & 31) + 1)


def stencil_cells(base):
    shift = cell_index() - base
    return jnp.concatenate([one_hot(shift == a * SPAN_Y + e) for a in range(4) for e in range(4)], 0)


def same_bin(shape, group):
    return ((iota(shape, 0) ^ iota(shape, 1)) & (group - 1)) == 0


def group_slice(g, size):
    return slice(g * size, (g + 1) * size)


def twice(lanes):
    return jnp.concatenate([lanes, lanes], 1)


def spread_kernel(
    direction_hbm, offsets_hbm, cells_hbm, forward_hbm, *refs
):
    tables_hbm, (out, offsets, base, depth), tables = refs[:TABLES], refs[TABLES : TABLES + 4], refs[TABLES + 4 : 2 * TABLES + 4]
    direction, cells, forward, q_hi, q_lo, sems = refs[2 * TABLES + 4 :]
    group, beside = SPREAD_GROUP, 64 // SPREAD_GROUP
    copies = [
        pltpu.make_async_copy(cells_hbm, cells, sems.at[0]),
        pltpu.make_async_copy(direction_hbm, direction, sems.at[1]),
        *(pltpu.make_async_copy(offsets_hbm.at[:, d, :], offsets.at[d], sems.at[2 + d]) for d in range(3)),
        pltpu.make_async_copy(forward_hbm, forward, sems.at[5]),
        *(pltpu.make_async_copy(tables_hbm[t], tables[t], sems.at[6 + t]) for t in range(TABLES)),
    ]
    for copy in copies:
        copy.start()
    copies[0].wait()
    first = (cells[0:1, :] - lax.axis_index("px") * ROWS) * SPAN_Y + cells[1:2, :] - lax.axis_index("py") * COLUMNS
    packed = (first + 256 * cells[2:3, :]).astype(f32)
    own = iota((BINS, BINS), 0) == iota((BINS, BINS), 1)
    packed = jnp.sum(jnp.where(own, packed, 0.0), axis=1, keepdims=True).astype(jnp.int32)
    base[...] = jnp.broadcast_to(packed & 255, (BINS, 128))
    depth[...] = jnp.broadcast_to(packed >> 8, (BINS, 128))
    for copy in copies[1:5]:
        copy.wait()

    def multiplied(g):
        bins = group_slice(g, group)
        wx = cubic_weights(offsets[0, bins, :])
        wy = cubic_weights(offsets[1, bins, :])
        wz = cubic_weights(offsets[2, bins, :])
        d = direction[bins, :]
        wx = [w * d for w in wx]
        columns = jnp.concatenate(split(jnp.concatenate([x * y for x in wx for y in wy], 0)), 1)
        depths = twice(jnp.concatenate(split(jnp.concatenate(wz, 0)), 0))
        yield
        patches = dot_nt(depths, columns)
        yield
        patches = patches[: 4 * group] + patches[4 * group :]
        patches = jnp.concatenate(split(jnp.where(same_bin(patches.shape, group), patches, 0.0)), 0)
        cells = stencil_cells(twice(base[bins, :]))
        yield
        placed = dot(patches, cells)
        yield
        placed = placed.astype(bf16)
        placed = placed[: 4 * group], placed[4 * group :]
        for f in range(4):
            start = (4 * (g // beside) + f) * beside * group + g % beside * group
            q_hi[start : start + group, :] = placed[0][f * group : (f + 1) * group]
            q_lo[start : start + group, :] = placed[1][f * group : (f + 1) * group]

    def several(p, found):
        parts = [multiplied(beside * p + j) for j in range(beside)]
        while parts:
            parts = [part for part in parts if next(part, 0) is None]
            yield
        own = cells[2:3, beside * p * group : beside * (p + 1) * group]
        own = jnp.concatenate([own + f - 1 for f in range(4)], 1)
        at_depth = one_hot(iota((GRID_Z, 4 * beside * group), 0) == own)
        yield
        rows = slice(4 * beside * p * group, 4 * beside * (p + 1) * group)
        found.append(dot(twice(at_depth), jnp.concatenate([q_hi[rows, :], q_lo[rows, :]], 0)))
        yield

    found = []
    running = [several(p, found) for p in range(BINS // group // beside)]
    for turn in range(16):
        for p, part in enumerate(running):
            if turn >= p:
                next(part, 0)

    gridded = split(sum(found))
    copies[5].wait()
    for part in range(2):
        rows = slice(part * GRID_Z, (part + 1) * GRID_Z)
        transformed = dot3((forward[rows, :GRID_Z], forward[rows, GRID_Z:]), gridded)
        for half in range(2):
            out[pl.ds(2 * part + half, GRID_Z, stride=4), :] = transformed[:, half * 128 : (half + 1) * 128]
    for copy in copies[6:]:
        copy.wait()


def moved(values, rows):
    return pltpu.roll(values, rows % DEVICES, 0)


def turned(values, lanes):
    return pltpu.roll(values, lanes % 128, 1) if lanes % 128 else values


def by_quarter(pieces):
    quarter = iota(pieces[0].shape, 1) >> 5
    result = 0.0
    for q, piece in enumerate(pieces):
        if piece is not None:
            result = jnp.where(quarter == q, piece, result)
    return result


def plane_kernel(
    received, along_x, back_x, along_y, back_y, sine_x, sines, rim, lengths, out, tiles, x_hi, x_lo, spectrum
):
    rim_lane = iota((DEVICES, OWN), 1) & 31
    before = rim_lane == 3 * ((rim_lane * 11) >> 5)
    place = ((0, 0), (0, 1), (0, 2), (0, 3), (1, 0), (1, 1), (1, 3))

    def filtering():
        length_x, length_y, length_z = (lengths[0:1, j : j + 1] for j in range(3))
        scale_x, scale_y = length_x * length_x, length_y * length_y
        frequency = lax.axis_index("px") * N_PY + lax.axis_index("py")
        sine = jnp.where(iota((1, GRID_Z), 1) == frequency, sines[1:2, :GRID_Z], 0.0)
        rest = 1.0 + length_z * length_z * jnp.sum(sine, axis=1, keepdims=True)
        factor = 2.0 / (M_X * M_Y) * length_x * length_y * length_z
        rows = rest + scale_x * sine_x[...]
        for j in range(M_Y // 128):
            lanes = slice(128 * j, 128 * (j + 1))
            denominator = rows + scale_y * sines[0:1, lanes]
            spectrum[:, lanes] = factor / (denominator * denominator)
        yield

    def plane(part):
        own, rest = (received[pl.ds(2 * part + half, DEVICES, stride=4), :] for half in range(2))
        to_owner = jnp.where(before, moved(rest, -1), moved(rest, 1))
        rims = dot(jnp.concatenate(split(to_owner), 0), rim[...])
        yield
        columns = rims[:DEVICES] + rims[DEVICES:]
        tiles[part, 0] = own + columns[:, :OWN]
        tiles[part, 1] = rest + columns[:, OWN:]
        loaded = [[tiles[part, tile, pl.ds(py, N_PX, stride=N_PY), :] for py in range(N_PY)] for tile in range(2)]
        for slot, (tile, q) in enumerate(place):
            rows = slice(slot * N_PX, (slot + 1) * N_PX)
            for half in range(2):
                lanes = slice(128 * half, 128 * (half + 1))
                values = by_quarter([turned(loaded[tile][4 * half + p], 32 * (p - q)) for p in range(4)])
                x_hi[part, rows, lanes], x_lo[part, rows, lanes] = split(values)
        empty = slice(len(place) * N_PX, DEVICES)
        x_hi[part, empty, :] = jnp.zeros((N_PX, GRID_Y), bf16)
        x_lo[part, empty, :] = jnp.zeros((N_PX, GRID_Y), bf16)
        yield
        found = []

        def half(h):
            rows = slice(h * M_X // 2, (h + 1) * M_X // 2)
            values = dot3((along_x[rows, :DEVICES], along_x[rows, DEVICES:]), (x_hi[part], x_lo[part]))
            yield
            values = split(values)
            yield
            values = dot3(values, (along_y[:, :M_Y], along_y[:, M_Y:]))
            yield
            values = split(values * spectrum[rows, :])
            yield
            values = dot3(values, (back_y[:, :GRID_Y], back_y[:, GRID_Y:]))
            yield
            values = split(values)
            left = slice(rows.start + M_X, rows.stop + M_X)
            found.append(dot3((back_x[:, rows], back_x[:, left]), values))
            yield

        parts = [half(0), half(1)]
        while parts:
            parts = [p for p in parts if next(p, 0) is None]
            yield
        values = sum(found)
        for py in range(N_PY):
            lanes = slice(128 * (py // 4), 128 * (py // 4 + 1))
            pieces = [[None] * 4, [None] * 4]
            for slot, (tile, q) in enumerate(place):
                pieces[tile][q] = turned(values[slot * N_PX : (slot + 1) * N_PX, lanes], 32 * (q - py % 4))
            for tile in range(2):
                tiles[part, tile, pl.ds(py, N_PX, stride=N_PY), :] = by_quarter(pieces[tile])
        own, rest = tiles[part, 0], tiles[part, 1]
        out[pl.ds(2 * part, DEVICES, stride=4), :] = own
        region = jnp.concatenate(split(jnp.concatenate([own, rest], 1)), 0)
        yield
        rims = dot_nt(region, rim[...])
        yield
        rims = rims[:DEVICES] + rims[DEVICES:]
        rims = jnp.where(before, moved(rims, 1), moved(rims, -1))
        out[pl.ds(2 * part + 1, DEVICES, stride=4), :] = rest + rims

    interleave([filtering(), plane(0), plane(1)])


def gather_kernel(received, direction, residual, noise, offsets, base, depth, inverse, image, sums, v_hi, v_lo):
    group = READ_GROUP
    for part in range(2):
        for half in range(2):
            rows = slice(part * GRID_Z, (part + 1) * GRID_Z)
            lanes = slice(half * 128, (half + 1) * 128)
            v_hi[rows, lanes], v_lo[rows, lanes] = split(received[pl.ds(2 * part + half, GRID_Z, stride=4), :])
    grid = split(dot3((inverse[:, : 2 * GRID_Z], inverse[:, 2 * GRID_Z :]), (v_hi[...], v_lo[...])))
    v_hi[:GRID_Z, :], v_lo[:GRID_Z, :] = grid

    def step(g, found):
        bins = group_slice(g, group)
        shift = iota((group, GRID_Z), 1) - twice(depth[bins, :])
        at_depth = jnp.concatenate([one_hot(shift == f - 1) for f in range(4)], 0)
        yield
        lines = [dot(at_depth, v[:GRID_Z, :]).astype(bf16) for v in (v_hi, v_lo)]
        lines = jnp.concatenate(lines, 0)
        cells = stencil_cells(twice(base[bins, :]))
        yield
        read = dot_nt(cells, lines)
        yield
        read = jnp.where(same_bin(read.shape, group), read, 0.0).astype(bf16)
        depths = jnp.concatenate(split(jnp.concatenate(cubic_weights(offsets[2, bins, :]), 0)), 1)
        depths = jnp.concatenate([depths, depths], 0)
        yield
        along = dot(read, depths)
        yield
        along = along[:, :BIN] + along[:, BIN:]
        wx = cubic_weights(offsets[0, bins, :])
        wy = cubic_weights(offsets[1, bins, :])
        value = 0.0
        for a in range(4):
            row = 0.0
            for e in range(4):
                start = (4 * a + e) * group
                row = row + wy[e] * along[start : start + group]
            value = value + wx[a] * row
        d, r = direction[bins, :], residual[bins, :]
        value = value + noise[bins, :] * d
        image[bins, :] = value
        found.append([(x * y).reshape(group // 8, 8, BIN).sum(0) for x, y in ((r, r), (d, value), (r, value), (value, value))])

    found = []
    interleave([step(g, found) for g in range(BINS // group)])
    totals = [sum(parts) for parts in zip(*found)]
    lane = iota((1, BIN), 1)
    row = jnp.zeros((1, BIN), f32)
    for j, part in enumerate(totals):
        row = jnp.where(lane == j, jnp.sum(part, keepdims=True), row)
    sums[...] = jnp.broadcast_to(row, (DEVICES, BIN))


def step_kernel(sums, iterate, residual, direction, image, new_iterate, new_residual, new_direction):
    row = jnp.sum(sums[...], axis=0, keepdims=True)
    old_norm, curvature, cross, square = (row[:, j : j + 1] for j in range(4))
    step = old_norm / curvature
    new_norm = old_norm - 2.0 * step * cross + step * step * square
    d = direction[...]
    r = residual[...] - step * image[...]
    new_iterate[...] = iterate[...] + step * d
    new_residual[...] = r
    new_direction[...] = r + (new_norm / old_norm) * d


VMEM = pl.BlockSpec(memory_space=pltpu.VMEM)
HBM = pl.BlockSpec(memory_space=pltpu.HBM)


def params():
    return pltpu.CompilerParams(vmem_limit_bytes=16 * 1024 * 1024)


def filter_plane(received, tables):
    return pl.pallas_call(
        plane_kernel,
        out_shape=jax.ShapeDtypeStruct((4 * DEVICES, 128), f32),
        in_specs=[VMEM] * (1 + TABLES),
        out_specs=VMEM,
        scratch_shapes=[
            pltpu.VMEM((2, 2, DEVICES, OWN), f32),
            pltpu.VMEM((2, DEVICES, GRID_Y), bf16),
            pltpu.VMEM((2, DEVICES, GRID_Y), bf16),
            pltpu.VMEM((M_X, M_Y), f32),
        ],
        compiler_params=params(),
        name="plane",
    )(received, *tables)


def on_device(solution, residual, direction, offsets, noise, bin_cells, lengths):
    forward, inverse = depth_tables()
    d, r = direction.reshape(BINS, BIN), residual.reshape(BINS, BIN)
    point = jax.ShapeDtypeStruct((BINS, BIN), f32)
    index = jax.ShapeDtypeStruct((BINS, BIN), jnp.int32)
    block = jax.ShapeDtypeStruct((4 * DEVICES, 128), f32)

    tables = (*plane_tables(), lengths.reshape(1, 3))
    by_tile = offsets.reshape(3, BINS, BIN).transpose(1, 0, 2)
    operands = [pltpu.with_memory_space_constraint(x, pltpu.HBM) for x in (d, by_tile, bin_cells, forward, *tables)]

    blocks, by_bin, base, depth, *tables = pl.pallas_call(
        spread_kernel,
        out_shape=(
            block, jax.ShapeDtypeStruct((3, BINS, BIN), f32), index, index,
            *(jax.ShapeDtypeStruct(t.shape, t.dtype) for t in tables),
        ),
        in_specs=[HBM] * len(operands),
        out_specs=(VMEM,) * (4 + TABLES),
        scratch_shapes=[
            pltpu.VMEM((BINS, BIN), f32),
            pltpu.VMEM((3, BINS), jnp.int32),
            pltpu.VMEM(forward.shape, bf16),
            pltpu.VMEM((4 * BINS, CELLS), bf16),
            pltpu.VMEM((4 * BINS, CELLS), bf16),
            pltpu.SemaphoreType.DMA((6 + TABLES,)),
        ],
        compiler_params=params(),
        name="spread",
    )(*operands)
    received = lax.all_to_all(blocks.reshape(DEVICES, 4, 128), ("px", "py"), 0, 0, tiled=True)

    filtered = filter_plane(received.reshape(4 * DEVICES, 128), tables)
    returned = lax.all_to_all(filtered.reshape(DEVICES, 4, 128), ("px", "py"), 0, 0, tiled=True)

    image, sums = pl.pallas_call(
        gather_kernel,
        out_shape=(point, jax.ShapeDtypeStruct((DEVICES, BIN), f32)),
        in_specs=[VMEM] * 8,
        out_specs=(VMEM, VMEM),
        scratch_shapes=[pltpu.VMEM((2 * GRID_Z, CELLS), bf16)] * 2,
        compiler_params=params(),
        name="interpolate",
    )(returned.reshape(4 * DEVICES, 128), d, r, noise.reshape(BINS, BIN), by_bin, base, depth, inverse)

    everywhere = lax.all_to_all(sums.reshape(DEVICES, 1, BIN), ("px", "py"), 0, 0, tiled=True)
    outs = pl.pallas_call(
        step_kernel,
        out_shape=(point,) * 3,
        in_specs=[VMEM] * 5,
        out_specs=(VMEM,) * 3,
        compiler_params=params(),
        name="step",
    )(everywhere.reshape(DEVICES, BIN), solution.reshape(BINS, BIN), r, d, image)
    return tuple(out.reshape(1, -1) for out in outs)


def solution(mesh):
    points = P(None, ("px", "py"))
    return jax.shard_map(
        on_device,
        mesh=mesh,
        in_specs=(points, points, points, points, P(("px", "py")), points, P()),
        out_specs=(points, points, points),
        check_vma=False,
    )
```
